128 devices in a mesh: qblk: 16 (over x_lo, y, core), kblk: 8 (over z, x_hi).
Axes of the slice: x: 4 (x_hi: 2, x_lo: 2; x = x_hi * 2 + x_lo), y: 4, z: 4, core: 2. Of those that a mesh axis runs over, the one named last changes fastest.
Arguments:
- queries: bfloat16 [32768, 128], P(('qblk', 'kblk')), may hold values from -8 to 8
- keys: bfloat16 [32768, 128], P(('qblk', 'kblk')), may hold values from -8 to 8
- values: bfloat16 [32768, 128], P(('qblk', 'kblk')), may hold values from -6 to 6
- grad_out: bfloat16 [32768, 128], P(('qblk', 'kblk')), may hold values from -6 to 6
- key_blocks: int32 [256, 16], replicated, may hold values from 0 to 255, as said below
Outputs:
- attended: bfloat16 [32768, 128], P(('qblk', 'kblk'))
- query_grads: bfloat16 [32768, 128], P(('qblk', 'kblk'))
- key_grads: bfloat16 [32768, 128], P(('qblk', 'kblk'))
- value_grads: bfloat16 [32768, 128], P(('qblk', 'kblk'))
The draws below stay inside these ranges and needn't reach their ends.
Inputs may be any that keep to these rules, and one draw needn't show every extreme that they name: `key_blocks`: row b lists 16 key block numbers, each at most b; its first entry is b itself; numbers may repeat within a row.
All inputs are finite; a program needn't handle non-finite values.
Results may differ from the reference program's by a relative error of at most 0.034.
Values may be sent and summed in bfloat16 or wider, within the bound.
A program may use at most 64 MiB of HBM per device.

```python
import math
import jax
import jax.numpy as jnp
from jax import lax

HEAD = 128
BLOCK = 128
NNZ = 16
TOKENS = 32768


def draw_queries(key, part):
    key = jax.random.fold_in(key, 11)
    first = jax.random.fold_in(key, 0)
    drawn = jnp.clip(jax.random.normal(first, (TOKENS, HEAD), jnp.float32), -6.0, 6.0)
    return drawn.astype(jnp.bfloat16)


def draw_keys(key, part):
    key = jax.random.fold_in(key, 23)
    first = jax.random.fold_in(key, 0)
    drawn = jnp.clip(jax.random.normal(first, (TOKENS, HEAD), jnp.float32), -6.0, 6.0)
    return drawn.astype(jnp.bfloat16)


def draw_key_blocks(key, part):
    key = jax.random.fold_in(key, 37)
    block_ids = jnp.arange(TOKENS // BLOCK, dtype=jnp.int32)
    raw = jax.random.randint(key, (TOKENS // BLOCK, NNZ), 0, 1 << 30, dtype=jnp.int32)
    picks = raw % (block_ids[:, None] + 1)
    return picks.at[:, 0].set(block_ids)


def steps_of(rng, extent, cuts, least, top_value):
    gain, own = 1.0, jax.random.fold_in(rng, 6)
    for dim, shards_of in cuts:
        heights = jnp.exp(jax.random.uniform(jax.random.fold_in(own, dim), (shards_of,), jnp.float32, least / len(cuts), top_value / len(cuts)))
        gain = gain * jnp.repeat(heights, extent[dim] // shards_of).reshape([-1 if axis == dim else 1 for axis in range(len(extent))])
    return gain


def scatter_about(rng, shape, spread, most, shards=(), held_as=jnp.bfloat16):
    gain = steps_of(rng, shape, shards, -0.22, 0.18) if shards else 1.0
    entries = jax.random.normal(rng, shape, jnp.float32) * spread * gain
    return jnp.minimum(jnp.maximum(entries, -most), most).astype(held_as)


def setup_inputs(seed: int = 0) -> dict:
    arg_keys = jax.random.split(jax.random.key(seed), 6)
    return {
        "queries": draw_queries(jax.random.fold_in(arg_keys[5], 71), 0),
        "keys": draw_keys(jax.random.fold_in(arg_keys[5], 71), 0),
        "values": scatter_about(arg_keys[2], (TOKENS, HEAD), 1.0, 6.0, ((0, 128),)),
        "grad_out": scatter_about(arg_keys[3], (TOKENS, HEAD), 1.0, 6.0, ((0, 128),)),
        "key_blocks": draw_key_blocks(jax.random.fold_in(arg_keys[5], 71), 0),
    }


masked_score = -1e+30

def against(left, right):
    return lax.dot_general(left, right, (((1,), (1,)), ((), ())), preferred_element_type=jnp.float32)

def across(left, right):
    return lax.dot_general(left, right, (((0,), (0,)), ((), ())), preferred_element_type=jnp.float32)

def reference(queries, keys, values, grad_out, key_blocks):
    head_dim = queries.shape[1]
    score_scale = 1.0 / math.sqrt(head_dim)
    block_count = TOKENS // BLOCK
    query_tiles = queries.reshape(block_count, BLOCK, head_dim)
    grad_tiles = grad_out.reshape(block_count, BLOCK, head_dim)
    key_tiles = keys.reshape(block_count, BLOCK, head_dim)
    value_tiles = values.reshape(block_count, BLOCK, head_dim)
    earlier = jnp.tril(jnp.ones((NNZ, NNZ), dtype=bool), -1)
    repeated = jnp.any((key_blocks[:, :, None] == key_blocks[:, None, :]) & earlier[None], axis=2)
    inside = jnp.arange(BLOCK, dtype=jnp.int32)

    def step(running, block_index):
        chosen = key_blocks[block_index].astype(jnp.int32)
        unique_entry = jnp.logical_not(repeated[block_index])
        key_sel = key_tiles[chosen].reshape(NNZ * BLOCK, head_dim)
        value_sel = value_tiles[chosen].reshape(NNZ * BLOCK, head_dim)
        key_pos = (chosen[:, None] * BLOCK + inside[None, :]).reshape(NNZ * BLOCK)
        query_pos = block_index * BLOCK + inside
        allowed = jnp.repeat(unique_entry, BLOCK)[None, :] & (query_pos[:, None] >= key_pos[None, :])
        rows_q = query_tiles[block_index]
        rows_grad = grad_tiles[block_index]
        scores = against(rows_q, key_sel) * score_scale
        row_top = lax.optimization_barrier(jnp.max(jnp.where(allowed, scores, masked_score), axis=1))
        row_total = lax.optimization_barrier(jnp.sum(jnp.where(allowed, jnp.exp(scores - row_top[:, None]), 0.0), axis=1))
        log_total = row_top + jnp.log(row_total)
        exact = jnp.where(allowed, jnp.exp(scores - log_total[:, None]), 0.0)
        weights = exact.astype(jnp.bfloat16)
        output_rows = jnp.dot(weights, value_sel, preferred_element_type=jnp.float32).astype(jnp.bfloat16)
        delta = lax.optimization_barrier(jnp.sum(rows_grad.astype(jnp.float32) * output_rows.astype(jnp.float32), axis=1))
        prob_grad = against(rows_grad, value_sel)
        score_grad = (exact * (prob_grad - delta[:, None])).astype(jnp.bfloat16)
        query_grad = (jnp.dot(score_grad, key_sel, preferred_element_type=jnp.float32) * score_scale).astype(jnp.bfloat16)
        pair = jnp.concatenate([across(score_grad, rows_q), across(weights, rows_grad)], axis=1)
        running = running.at[key_pos].add(pair)
        return (running, (output_rows, query_grad))
    start_sums = jnp.zeros((TOKENS, 2 * head_dim), jnp.float32)
    key_sums, (output_stack, query_stack) = lax.scan(step, start_sums, jnp.arange(block_count, dtype=jnp.int32))
    attended = output_stack.reshape(TOKENS, head_dim)
    query_grads = query_stack.reshape(TOKENS, head_dim)
    key_grads = (key_sums[:, :head_dim] * score_scale).astype(jnp.bfloat16)
    value_grads = key_sums[:, head_dim:].astype(jnp.bfloat16)
    return (attended, query_grads, key_grads, value_grads)
```

```python
import functools
import math

import jax
import jax.numpy as jnp
from jax import lax
from jax.experimental import pallas as pl
from jax.experimental.pallas import tpu as pltpu
from jax.sharding import PartitionSpec as P

BLOCK = 128
SLOTS = 64
UNROLL = 4
MESH = pl.DeviceIdType.MESH

masked_score = -1e30
LOG2E = 1.4426950408889634


def against(left, right):
    return lax.dot_general(
        left, right, (((1,), (1,)), ((), ())), preferred_element_type=jnp.float32
    )


def across(left, right):
    return lax.dot_general(
        left, right, (((0,), (0,)), ((), ())), preferred_element_type=jnp.float32
    )


def dot(left, right):
    return jnp.dot(left, right, preferred_element_type=jnp.float32)


KEY, QUERY, SAME_KEY, DIAGONAL, PERM, PERM_KEY, SAME_QUERY, KEY_END, QUERY_END = range(9)


def iota(shape, dim):
    return lax.broadcasted_iota(jnp.int32, shape, dim)


def fiota(shape, dim):
    return iota(shape, dim).astype(jnp.float32)


def ones_where(cond):
    return jnp.where(cond, 1.0, 0.0).astype(jnp.float32)


def list_pairs(i, j, blocks_ref, table, slot_query):
    own = blocks_ref[pl.ds(pl.multiple_of(i * 16, 16), 16), :]
    key_of = iota((16, 32), 1)
    key_ids = (key_of // 2) * 16 + 2 * j + key_of % 2
    listed = jnp.zeros((16, 32), jnp.float32)
    for n in range(16):
        listed = jnp.maximum(listed, ones_where(own[:, n : n + 1] == key_ids))
    unit = ones_where(iota((32, 32), 0) == iota((32, 32), 1))
    pairs = against(unit, listed)
    earlier_query = ones_where(iota((16, 16), 0) < iota((16, 16), 1))
    earlier_key = ones_where(iota((32, 32), 1) < iota((32, 32), 0))
    in_key = dot(pairs, earlier_query)
    in_query = dot(earlier_key, pairs)
    key_count = jnp.sum(pairs, axis=1, keepdims=True)
    query_count = jnp.sum(pairs, axis=0, keepdims=True)
    key_first = jnp.sum(in_query, axis=1, keepdims=True)
    query_first = jnp.sum(in_key, axis=0, keepdims=True)
    by_key = jnp.where(pairs > 0, key_first + in_key, -1.0)
    by_query = jnp.where(pairs > 0, query_first + in_query, -1.0)
    total = jnp.sum(jnp.sum(pairs, axis=1, keepdims=True), axis=0, keepdims=True)

    lane = fiota((32, 128), 1)
    keys = fiota((32, 128), 0)
    id_col = (iota((32, 128), 0) // 2) * 16 + 2 * j + iota((32, 128), 0) % 2
    zero = jnp.zeros((32, 128), jnp.float32)
    rows = {n: zero for n in range(7)}
    for q in range(16):
        at_key = by_key[:, q : q + 1] == lane
        at_query = by_query[:, q : q + 1] == lane
        rows[KEY] += jnp.where(at_key, keys, 0.0)
        rows[QUERY] += jnp.where(at_key, float(q), 0.0)
        rows[SAME_KEY] += jnp.where(at_key, ones_where(in_key[:, q : q + 1] > 0), 0.0)
        rows[DIAGONAL] += jnp.where(at_key & (id_col == 16 * i + q), 1.0, 0.0)
        rows[PERM] += jnp.where(at_query, by_key[:, q : q + 1], 0.0)
        rows[PERM_KEY] += jnp.where(at_query, keys, 0.0)
        rows[SAME_QUERY] += jnp.where(at_query, ones_where(in_query[:, q : q + 1] > 0), 0.0)
    most = {KEY: 31, QUERY: 15, SAME_KEY: 1, DIAGONAL: 1, PERM: SLOTS - 1, PERM_KEY: 31, SAME_QUERY: 1}
    for n in range(7):
        rows[n] = jnp.sum(rows[n], axis=0, keepdims=True)
        table[n : n + 1, :] = jnp.clip(rows[n].astype(jnp.int32), 0, most[n])
    key_end = jnp.where(key_count > 0, key_first + key_count, 0.0)
    key_end = jnp.sum(jnp.where(keys == lane, key_end, 0.0), axis=0, keepdims=True)
    table[KEY_END : KEY_END + 1, :] = jnp.clip(key_end.astype(jnp.int32), 0, SLOTS)
    query_end = jnp.where(query_count > 0, query_first + query_count, 0.0)
    table[QUERY_END : QUERY_END + 1, 0:16] = jnp.clip(query_end.astype(jnp.int32), 0, SLOTS)

    query_row = jnp.where(fiota((1, 128), 1) < total, rows[QUERY], -1.0)
    slot_query[...] = jnp.sum(
        jnp.where(iota((SLOTS, 128), 0) == iota((SLOTS, 128), 1), query_row, 0.0),
        axis=1,
        keepdims=True,
    )


def most_pairs(blocks_ref):
    lists = jnp.transpose(blocks_ref[...].astype(jnp.float32)).astype(jnp.int32)
    groups = (lists // 2) % 8
    counts = jnp.zeros((8, 256), jnp.float32)
    group_of = iota((8, 256), 0)
    for n in range(16):
        fresh = jnp.ones((1, 256), jnp.float32)
        for m in range(n):
            fresh = jnp.where(lists[m : m + 1] == lists[n : n + 1], 0.0, fresh)
        counts += jnp.where(groups[n : n + 1] == group_of, fresh, 0.0)
    member = ones_where(iota((256, 16), 0) // 16 == iota((256, 16), 1))
    return jnp.max(dot(counts, member))


def kernel(
    q_ref, k_ref, v_ref, g_ref, blocks_ref,
    attended_ref, query_grads_ref, key_grads_ref, value_grads_ref, flag_ref,
    kv, qg, table_v, table, slot_query, bias, probs, prob_grads, tops, totals, moments,
    stats_out, stats, offsets, deltas, rounded, key_acc, query_acc,
    sib_out, sib_in, y_out, y_in, x_out, x_in, z_out, z_in, h_out, h_in,
    local_sem, kv_send, kv_recv, qg_send, qg_recv, st_send, st_recv, red_send, red_recv,
):
    i, j = lax.axis_index("qblk"), lax.axis_index("kblk")
    core, y, x = i % 2, (i // 2) % 4, i // 8
    h, z = j % 2, j // 2
    scale = 1.0 / math.sqrt(BLOCK)

    def sibling():
        return (i + 1 - 2 * core, j)

    def x_partner():
        return ((i + 8) % 16, j)

    def y_peer(d):
        return (x * 8 + ((y + d) % 4) * 2 + core, j)

    def h_partner():
        return (i, j + 1 - 2 * h)

    def z_peer(d):
        return (i, ((z + d) % 4) * 2 + h)

    def zh_peer(d):
        return (i, ((z + d) % 4) * 2 + 1 - h)

    loads = []
    for n, (src, dst) in enumerate(
        ((k_ref, kv.at[i, 0]), (v_ref, kv.at[i, 1]), (q_ref, qg.at[j, 0]), (g_ref, qg.at[j, 1]))
    ):
        loads.append(pltpu.make_async_copy(src, dst, local_sem.at[n]))
        loads[-1].start()

    peers = [sibling(), x_partner(), h_partner()]
    peers += [y_peer(d) for d in (1, 2, 3)] + [z_peer(d) for d in (1, 2, 3)]
    peers += [zh_peer(d) for d in (1, 2, 3)]
    barrier = pltpu.get_barrier_semaphore()
    for peer in peers:
        pl.semaphore_signal(barrier, inc=1, device_id=peer, device_id_type=MESH)
    pl.semaphore_wait(barrier, len(peers))
    for load in loads:
        load.wait()

    def send(src, dst, sems, n, peer):
        copy = pltpu.make_async_remote_copy(
            src_ref=src, dst_ref=dst, send_sem=sems[0].at[n], recv_sem=sems[1].at[n],
            device_id=peer, device_id_type=MESH,
        )
        copy.start()
        return copy

    kv_sems, qg_sems = (kv_send, kv_recv), (qg_send, qg_recv)
    kv_x = send(kv.at[i], kv.at[i], kv_sems, 0, x_partner())
    qg_h = send(qg.at[j], qg.at[j], qg_sems, 0, h_partner())
    kv_y = [send(kv.at[i], kv.at[i], kv_sems, d, y_peer(d)) for d in (1, 3, 2)]
    qg_z = [send(qg.at[j], qg.at[j], qg_sems, d, z_peer(d)) for d in (1, 3, 2)]
    kv_sib = [send(kv.at[i], kv.at[i], kv_sems, 7, sibling())]

    list_pairs(i, j, blocks_ref, table_v, slot_query)
    to_smem = pltpu.make_async_copy(table_v, table, local_sem.at[4])
    to_smem.start()
    bias[0] = jnp.zeros((BLOCK, BLOCK), jnp.float32)
    bias[1] = jnp.where(
        iota((BLOCK, BLOCK), 0) <= iota((BLOCK, BLOCK), 1), 0.0, masked_score
    ).astype(jnp.float32)
    key_acc[0] = jnp.zeros((2, BLOCK, BLOCK), jnp.float32)
    query_acc[0] = jnp.zeros((2, BLOCK, BLOCK), jnp.float32)

    kv_x.wait_recv()
    far = (i + 8) % 16
    kv_far = [send(kv.at[far], kv.at[far], kv_sems, 3 + d, y_peer(d)) for d in (1, 3, 2)]
    kv_sib.append(send(kv.at[far], kv.at[far], kv_sems, 8, sibling()))
    qg_h.wait_recv()
    other = j + 1 - 2 * h
    qg_far = [send(qg.at[other], qg.at[other], qg_sems, 3 + d, z_peer(d)) for d in (1, 3, 2)]

    flag_ref[...] = jnp.full((8, 128), most_pairs(blocks_ref), jnp.float32).astype(jnp.int32)

    for n, d in enumerate((1, 3, 2)):
        kv_y[n].wait_recv()
        src = x * 8 + ((y - d + 4) % 4) * 2 + core
        kv_sib.append(send(kv.at[src], kv.at[src], kv_sems, 8 + d, sibling()))
    for n, d in enumerate((1, 3, 2)):
        kv_far[n].wait_recv()
        src = (1 - x) * 8 + ((y - d + 4) % 4) * 2 + core
        kv_sib.append(send(kv.at[src], kv.at[src], kv_sems, 11 + d, sibling()))
    for copy in qg_z + qg_far:
        copy.wait_recv()
    for copy in kv_sib:
        copy.wait_recv()
    to_smem.wait()

    def score_step(step, carry):
        for u in range(UNROLL):
            s = step * UNROLL + u
            k, q = table[KEY, s], table[QUERY, s]
            scores = against(kv[k // 2, 0, k % 2], qg[q // 2, 0, q % 2]) * (scale * LOG2E)
            scores += bias[table[DIAGONAL, s]]
            prob_grad = against(kv[k // 2, 1, k % 2], qg[q // 2, 1, q % 2])
            top = jnp.max(scores, axis=0, keepdims=True)
            prob = jnp.exp2(scores - top)
            probs[s] = prob
            prob_grads[s] = prob_grad
            tops[pl.ds(s, 1), :] = top
            totals[pl.ds(s, 1), :] = jnp.sum(prob, axis=0, keepdims=True)
            moments[pl.ds(s, 1), :] = jnp.sum(prob * prob_grad, axis=0, keepdims=True)
        return carry

    lax.fori_loop(0, SLOTS // UNROLL, score_step, 0)

    top, total, moment, owner = tops[...], totals[...], moments[...], slot_query[...]
    for q in range(16):
        mine = owner == float(q)
        top_q = jnp.max(jnp.where(mine, top, masked_score), axis=0, keepdims=True)
        part = jnp.where(mine, jnp.exp2(top - top_q), 0.0)
        total_q = jnp.sum(part * total, axis=0, keepdims=True)
        moment_q = jnp.sum(part * moment, axis=0, keepdims=True)
        some = total_q > 0
        safe = jnp.where(some, total_q, 1.0)
        stats_out[0, q : q + 1, :] = jnp.where(some, top_q + jnp.log2(safe), masked_score)
        stats_out[1, q : q + 1, :] = moment_q / safe

    st_sems = (st_send, st_recv)
    st_copies = []
    stats[j] = stats_out[...]
    for n, peer in enumerate(
        [z_peer(1), z_peer(3), h_partner(), z_peer(2), zh_peer(1), zh_peer(3), zh_peer(2)]
    ):
        st_copies.append(send(stats_out, stats.at[j], st_sems, n, peer))
    for copy in st_copies:
        copy.wait_recv()
    logs = stats[:, 0]
    best = jnp.max(logs, axis=0)
    offset = best + jnp.log2(jnp.sum(jnp.exp2(logs - best[None]), axis=0))
    delta = jnp.sum(jnp.exp2(logs - offset[None]) * stats[:, 1], axis=0)
    for q in range(16):
        offsets[q] = offset[q : q + 1, :]
        deltas[q] = delta[q : q + 1, :]

    def key_step(step, carry):
        for u in range(UNROLL):
            s = step * UNROLL + u
            q = table[QUERY, s]
            keep = table[SAME_KEY, s].astype(jnp.float32)
            prob = probs[s] * jnp.exp2(tops[pl.ds(s, 1), :] - offsets[q])
            weights = prob.astype(jnp.bfloat16)
            score_grad = (prob * (prob_grads[s] - deltas[q])).astype(jnp.bfloat16)
            rounded[s, 0] = score_grad
            rounded[s, 1] = weights
            key_acc[s + 1, 0] = key_acc[s, 0] * keep + dot(score_grad, qg[q // 2, 0, q % 2])
            key_acc[s + 1, 1] = key_acc[s, 1] * keep + dot(weights, qg[q // 2, 1, q % 2])
        return carry

    lax.fori_loop(0, SLOTS // UNROLL, key_step, 0)

    red = (red_send, red_recv)

    def sib_step(n, carry):
        owner = (n % 2) * 8 + (n // 2) * 2 + 1 - core
        for b in range(2):
            sib_out[n, :, b] = key_acc[table[KEY_END, owner * 2 + b]].astype(jnp.bfloat16)
        return carry

    lax.fori_loop(0, 8, sib_step, 0)
    sib_copy = send(sib_out, sib_in, red, 0, sibling())

    def query_step(step, carry):
        for u in range(UNROLL):
            s = step * UNROLL + u
            k, at = table[PERM_KEY, s], table[PERM, s]
            keep = table[SAME_QUERY, s].astype(jnp.float32)
            query_acc[s + 1, 0] = query_acc[s, 0] * keep + across(rounded[at, 0], kv[k // 2, 0, k % 2])
            query_acc[s + 1, 1] = query_acc[s, 1] * keep + across(rounded[at, 1], kv[k // 2, 1, k % 2])
        return carry

    lax.fori_loop(0, SLOTS // UNROLL, query_step, 0)

    def z_step(n, carry):
        for b in range(2):
            z_out[n // 2, n % 2, :, b] = query_acc[table[QUERY_END, n * 2 + b]].astype(jnp.bfloat16)
        return carry

    lax.fori_loop(0, 8, z_step, 0)
    z_copies = []
    for d in (1, 3, 2):
        z_copies.append(send(z_out.at[(z + d) % 4], z_in.at[d - 1], red, d, z_peer(d)))

    sib_copy.wait_recv()

    def y_step(n, carry):
        owner = (n % 2) * 8 + (n // 2) * 2 + core
        for b in range(2):
            both = key_acc[table[KEY_END, owner * 2 + b]] + sib_in[n, :, b].astype(jnp.float32)
            y_out[n // 2, n % 2, :, b] = both.astype(jnp.bfloat16)
        return carry

    lax.fori_loop(0, 8, y_step, 0)
    y_copies = []
    for d in (1, 3, 2):
        y_copies.append(send(y_out.at[(y + d) % 4], y_in.at[d - 1], red, 3 + d, y_peer(d)))

    def total_of(own, arrived, at):
        total = own[at].astype(jnp.float32)
        for d in range(3):
            total += arrived[(d,) + at[1:]].astype(jnp.float32)
        return total

    def sum_of(own, arrived, row, col):
        total = own[row, col].astype(jnp.float32)
        for d in range(3):
            total += arrived[d, col].astype(jnp.float32)
        return total

    for copy in z_copies:
        copy.wait_recv()
    h_out[...] = sum_of(z_out, z_in, z, 1 - h).astype(jnp.bfloat16)
    h_copy = send(h_out, h_in, red, 7, h_partner())
    for copy in y_copies:
        copy.wait_recv()
    x_out[...] = sum_of(y_out, y_in, y, 1 - x).astype(jnp.bfloat16)
    x_copy = send(x_out, x_in, red, 8, x_partner())
    query_sum = sum_of(z_out, z_in, z, h)
    key_sum = sum_of(y_out, y_in, y, x)
    h_copy.wait_recv()
    query_sum += h_in[...].astype(jnp.float32)
    for b in range(2):
        rows = pl.ds(b * BLOCK, BLOCK)
        query_grads_ref[rows, :] = (query_sum[0, b] * scale).astype(jnp.bfloat16)
        attended_ref[rows, :] = query_sum[1, b].astype(jnp.bfloat16)
    x_copy.wait_recv()
    key_sum += x_in[...].astype(jnp.float32)
    for b in range(2):
        rows = pl.ds(b * BLOCK, BLOCK)
        key_grads_ref[rows, :] = (key_sum[0, b] * scale).astype(jnp.bfloat16)
        value_grads_ref[rows, :] = key_sum[1, b].astype(jnp.bfloat16)

    for copy in [kv_x, qg_h, sib_copy, h_copy, x_copy]:
        copy.wait_send()
    for copy in kv_y + kv_far + kv_sib + qg_z + qg_far + st_copies + z_copies + y_copies:
        copy.wait_send()


def fast(queries, keys, values, grad_out, key_blocks):
    rows, head = queries.shape
    out = jax.ShapeDtypeStruct((rows, head), jnp.bfloat16)
    f32, bf16 = jnp.float32, jnp.bfloat16
    tile = (BLOCK, BLOCK)
    dma = pltpu.SemaphoreType.DMA
    any_spec = pl.BlockSpec(memory_space=pl.ANY)
    vmem_spec = pl.BlockSpec(memory_space=pltpu.VMEM)
    return pl.pallas_call(
        kernel,
        out_shape=[out] * 4 + [jax.ShapeDtypeStruct((8, 128), jnp.int32)],
        in_specs=[any_spec] * 4 + [vmem_spec],
        out_specs=[vmem_spec] * 5,
        scratch_shapes=[
            pltpu.VMEM((16, 2, 2) + tile, bf16),
            pltpu.VMEM((8, 2, 2) + tile, bf16),
            pltpu.VMEM((16, 128), jnp.int32),
            pltpu.SMEM((16, 128), jnp.int32),
            pltpu.VMEM((SLOTS, 1), f32),
            pltpu.VMEM((2,) + tile, f32),
            pltpu.VMEM((SLOTS,) + tile, f32),
            pltpu.VMEM((SLOTS,) + tile, f32),
            pltpu.VMEM((SLOTS, 128), f32),
            pltpu.VMEM((SLOTS, 128), f32),
            pltpu.VMEM((SLOTS, 128), f32),
            pltpu.VMEM((2, 16, 128), f32),
            pltpu.VMEM((8, 2, 16, 128), f32),
            pltpu.VMEM((16, 1, 128), f32),
            pltpu.VMEM((16, 1, 128), f32),
            pltpu.VMEM((SLOTS, 2) + tile, bf16),
            pltpu.VMEM((SLOTS + 1, 2) + tile, f32),
            pltpu.VMEM((SLOTS + 1, 2) + tile, f32),
            pltpu.VMEM((8, 2, 2) + tile, bf16),
            pltpu.VMEM((8, 2, 2) + tile, bf16),
            pltpu.VMEM((4, 2, 2, 2) + tile, bf16),
            pltpu.VMEM((3, 2, 2, 2) + tile, bf16),
            pltpu.VMEM((2, 2) + tile, bf16),
            pltpu.VMEM((2, 2) + tile, bf16),
            pltpu.VMEM((4, 2, 2, 2) + tile, bf16),
            pltpu.VMEM((3, 2, 2, 2) + tile, bf16),
            pltpu.VMEM((2, 2) + tile, bf16),
            pltpu.VMEM((2, 2) + tile, bf16),
            dma((5,)), dma((15,)), dma((15,)), dma((7,)), dma((7,)),
            dma((7,)), dma((7,)), dma((9,)), dma((9,)),
        ],
        compiler_params=pltpu.CompilerParams(
            collective_id=0, has_side_effects=True, vmem_limit_bytes=56 << 20
        ),
        name="block_sparse_attention",
    )(*(x.reshape(2, BLOCK, BLOCK) for x in (queries, keys, values, grad_out)), key_blocks)


def in_blocks(block_fn, row_count):
    block_rows = 512
    firsts = jnp.arange(row_count // block_rows, dtype=jnp.int32) * block_rows
    stacked = lax.map(lambda anchor: block_fn(anchor, block_rows), firsts)
    return jax.tree.map(lambda layer: layer.reshape((row_count,) + layer.shape[2:]), stacked)


def general(queries, keys, values, grad_out, key_blocks):
    own_rows, head_dim = queries.shape
    block_len = BLOCK
    key_groups = lax.axis_size("kblk")
    query_index = lax.axis_index("qblk")
    key_index = lax.axis_index("kblk")
    score_scale = 1.0 / math.sqrt(head_dim)
    query_all, grad_all = (
        lax.all_gather(queries, "qblk", axis=0, tiled=True),
        lax.all_gather(grad_out, "qblk", axis=0, tiled=True),
    )
    key_all, value_all = (
        lax.all_gather(keys, "kblk", axis=0, tiled=True),
        lax.all_gather(values, "kblk", axis=0, tiled=True),
    )
    query_count = query_all.shape[0]
    key_count = key_all.shape[0]
    query_line = jnp.arange(query_count, dtype=jnp.int32)
    query_pos = (query_line // own_rows * key_groups + key_index) * own_rows + query_line % own_rows
    key_pos = query_index * key_count + jnp.arange(key_count, dtype=jnp.int32)
    query_block_ids = query_pos[::block_len] // block_len
    key_block_ids = key_pos[::block_len] // block_len
    listed = jnp.take(key_blocks, query_block_ids, axis=0)
    block_allowed = jnp.any(listed[:, :, None] == key_block_ids[None, None, :], axis=1)

    def tile(first_row, row_count):
        rows_q = lax.dynamic_slice_in_dim(query_all, first_row, row_count, 0)
        positions = lax.dynamic_slice_in_dim(query_pos, first_row, row_count, 0)
        coarse = lax.dynamic_slice_in_dim(
            block_allowed, first_row // block_len, row_count // block_len, 0
        )
        fine_allowed = jnp.broadcast_to(
            coarse[:, None, :, None],
            (row_count // block_len, block_len, key_count // block_len, block_len),
        ).reshape(row_count, key_count)
        allowed = fine_allowed & (positions[:, None] >= key_pos[None, :])
        scores = against(rows_q, key_all) * score_scale
        return (scores, allowed)

    def local_stats(first_row, row_count):
        scores, allowed = tile(first_row, row_count)
        row_top = jnp.max(jnp.where(allowed, scores, masked_score), axis=1)
        row_total = jnp.sum(jnp.where(allowed, jnp.exp(scores - row_top[:, None]), 0.0), axis=1)
        return (row_top, row_total)

    row_top, row_total = in_blocks(local_stats, query_count)
    top_all = lax.pmax(row_top, "qblk")
    total_all = lax.psum(row_total * jnp.exp(row_top - top_all), "qblk")
    log_total = top_all + jnp.log(total_all)

    def block_fn(anchor, block_rows):
        scores, allowed = tile(anchor, block_rows)
        offsets = lax.dynamic_slice_in_dim(log_total, anchor, block_rows, 0)
        weights = jnp.where(allowed, jnp.exp(scores - offsets[:, None]), 0.0).astype(jnp.bfloat16)
        return jnp.dot(weights, value_all, preferred_element_type=jnp.float32)

    attended = lax.psum_scatter(
        in_blocks(block_fn, lax.axis_size("qblk") * own_rows),
        "qblk",
        scatter_dimension=0,
        tiled=True,
    ).astype(jnp.bfloat16)
    own_delta = jnp.sum(grad_out.astype(jnp.float32) * attended.astype(jnp.float32), axis=1)
    delta_all = lax.all_gather(own_delta, "qblk", axis=0, tiled=True)
    back_rows = 512

    def back_step(running, anchor):
        scores, allowed = tile(anchor, back_rows)
        offsets = lax.dynamic_slice_in_dim(log_total, anchor, back_rows, 0)
        deltas = lax.dynamic_slice_in_dim(delta_all, anchor, back_rows, 0)
        rows_q = lax.dynamic_slice_in_dim(query_all, anchor, back_rows, 0)
        rows_grad = lax.dynamic_slice_in_dim(grad_all, anchor, back_rows, 0)
        exact = jnp.where(allowed, jnp.exp(scores - offsets[:, None]), 0.0)
        weights = exact.astype(jnp.bfloat16)
        prob_grad = against(rows_grad, value_all)
        score_grad = (exact * (prob_grad - deltas[:, None])).astype(jnp.bfloat16)
        query_grad = jnp.dot(score_grad, key_all, preferred_element_type=jnp.float32)
        pair = jnp.concatenate([across(score_grad, rows_q), across(weights, rows_grad)], axis=1)
        return (running + pair, query_grad)

    firsts = jnp.arange(query_count // back_rows, dtype=jnp.int32) * back_rows
    start_sums = jnp.zeros((key_count, 2 * head_dim), jnp.float32)
    key_terms, query_terms = lax.scan(back_step, start_sums, firsts)
    query_terms = query_terms.reshape(query_count, head_dim)
    query_grads = (
        lax.psum_scatter(
            query_terms.astype(jnp.bfloat16), "qblk", scatter_dimension=0, tiled=True
        ).astype(jnp.float32)
        * score_scale
    ).astype(jnp.bfloat16)
    key_sums = lax.psum_scatter(
        key_terms.astype(jnp.bfloat16), "kblk", scatter_dimension=0, tiled=True
    ).astype(jnp.float32)
    key_grads = (key_sums[:, :head_dim] * score_scale).astype(jnp.bfloat16)
    value_grads = key_sums[:, head_dim:].astype(jnp.bfloat16)
    return (attended, query_grads, key_grads, value_grads)


def per_device(queries, keys, values, grad_out, key_blocks):
    *outs, most = fast(queries, keys, values, grad_out, key_blocks)
    return lax.cond(
        most[0, 0] > SLOTS,
        lambda: general(queries, keys, values, grad_out, key_blocks),
        lambda: tuple(outs),
    )


def solution(mesh):
    split = P(("qblk", "kblk"), None)
    return jax.shard_map(
        per_device,
        mesh=mesh,
        in_specs=(split, split, split, split, P()),
        out_specs=(split, split, split, split),
        check_vma=False,
    )
```

```python
import functools
import math

import jax
import jax.numpy as jnp
from jax import lax
from jax.experimental import pallas as pl
from jax.experimental.pallas import tpu as pltpu
from jax.sharding import PartitionSpec as P

BLOCK = 128
SLOTS = 64
UNROLL = 4
MESH = pl.DeviceIdType.MESH

masked_score = -1e30
LOG2E = 1.4426950408889634


def against(left, right):
    return lax.dot_general(
        left, right, (((1,), (1,)), ((), ())), preferred_element_type=jnp.float32
    )


def across(left, right):
    return lax.dot_general(
        left, right, (((0,), (0,)), ((), ())), preferred_element_type=jnp.float32
    )


def dot(left, right):
    return jnp.dot(left, right, preferred_element_type=jnp.float32)


KEY, QUERY, SAME_KEY, DIAGONAL, PERM, PERM_KEY, SAME_QUERY, KEY_END, QUERY_END = range(9)
LISTED = 16


def iota(shape, dim):
    return lax.broadcasted_iota(jnp.int32, shape, dim)


def fiota(shape, dim):
    return iota(shape, dim).astype(jnp.float32)


def ones_where(cond):
    return jnp.where(cond, 1.0, 0.0).astype(jnp.float32)


def list_pairs(i, j, lists_ref, table, slot_query):
    lists = lists_ref[...].astype(jnp.float32)
    chosen = ones_where(iota((256, 16), 0) == 16 * i + iota((256, 16), 1))
    own = dot(lists, chosen)
    key_ids = ((iota((32, 16), 0) // 2) * 16 + 2 * j + iota((32, 16), 0) % 2).astype(jnp.float32)
    pairs = jnp.zeros((32, 16), jnp.float32)
    for n in range(16):
        pairs = jnp.maximum(pairs, ones_where(own[n : n + 1, :] == key_ids))
    earlier_query = ones_where(iota((16, 16), 0) < iota((16, 16), 1))
    earlier_key = ones_where(iota((32, 32), 1) < iota((32, 32), 0))
    in_key = dot(pairs, earlier_query)
    in_query = dot(earlier_key, pairs)
    key_count = jnp.sum(pairs, axis=1, keepdims=True)
    query_count = jnp.sum(pairs, axis=0, keepdims=True)
    key_first = jnp.sum(in_query, axis=1, keepdims=True)
    query_first = jnp.sum(in_key, axis=0, keepdims=True)
    by_key = jnp.where(pairs > 0, key_first + in_key, -1.0)
    by_query = jnp.where(pairs > 0, query_first + in_query, -1.0)
    total = jnp.sum(jnp.sum(pairs, axis=1, keepdims=True), axis=0, keepdims=True)

    lane = fiota((32, 128), 1)
    keys = fiota((32, 128), 0)
    id_col = (iota((32, 128), 0) // 2) * 16 + 2 * j + iota((32, 128), 0) % 2
    zero = jnp.zeros((32, 128), jnp.float32)
    rows = {n: zero for n in range(7)}
    for q in range(16):
        at_key = by_key[:, q : q + 1] == lane
        at_query = by_query[:, q : q + 1] == lane
        rows[KEY] += jnp.where(at_key, keys, 0.0)
        rows[QUERY] += jnp.where(at_key, float(q), 0.0)
        rows[SAME_KEY] += jnp.where(at_key, ones_where(in_key[:, q : q + 1] > 0), 0.0)
        rows[DIAGONAL] += jnp.where(at_key & (id_col == 16 * i + q), 1.0, 0.0)
        rows[PERM] += jnp.where(at_query, by_key[:, q : q + 1], 0.0)
        rows[PERM_KEY] += jnp.where(at_query, keys, 0.0)
        rows[SAME_QUERY] += jnp.where(at_query, ones_where(in_query[:, q : q + 1] > 0), 0.0)
    most = {KEY: 31, QUERY: 15, SAME_KEY: 1, DIAGONAL: 1, PERM: SLOTS - 1, PERM_KEY: 31, SAME_QUERY: 1}
    for n in range(7):
        rows[n] = jnp.sum(rows[n], axis=0, keepdims=True)
        table[n : n + 1, :] = jnp.clip(rows[n].astype(jnp.int32), 0, most[n])
    key_end = jnp.where(key_count > 0, key_first + key_count, 0.0)
    key_end = jnp.sum(jnp.where(keys == lane, key_end, 0.0), axis=0, keepdims=True)
    table[KEY_END : KEY_END + 1, :] = jnp.clip(key_end.astype(jnp.int32), 0, SLOTS)
    query_end = jnp.where(query_count > 0, query_first + query_count, 0.0)
    table[QUERY_END : QUERY_END + 1, 0:16] = jnp.clip(query_end.astype(jnp.int32), 0, SLOTS)
    if table.shape[0] > LISTED:
        table[LISTED : LISTED + 32, 0:16] = pairs.astype(jnp.int32)
        return

    query_row = jnp.where(fiota((1, 128), 1) < total, rows[QUERY], -1.0)
    slot_query[...] = jnp.sum(
        jnp.where(iota((SLOTS, 128), 0) == iota((SLOTS, 128), 1), query_row, 0.0),
        axis=1,
        keepdims=True,
    )


def most_pairs(lists_ref):
    lists = lists_ref[...]
    groups = (lists // 2) % 8
    counts = jnp.zeros((8, 256), jnp.float32)
    group_of = iota((8, 256), 0)
    for n in range(16):
        fresh = jnp.ones((1, 256), jnp.float32)
        for m in range(n):
            fresh = jnp.where(lists[m : m + 1] == lists[n : n + 1], 0.0, fresh)
        counts += jnp.where(groups[n : n + 1] == group_of, fresh, 0.0)
    member = ones_where(iota((256, 16), 0) // 16 == iota((256, 16), 1))
    return jnp.max(dot(counts, member))


class Refs:
    def __init__(self, names, refs):
        self.__dict__.update(zip(names, refs, strict=True))


def kernel(names, dense, *refs):
    r = Refs(names, refs)
    i, j = lax.axis_index("qblk"), lax.axis_index("kblk")
    core, y, x = i % 2, (i // 2) % 4, i // 8
    h, z = j % 2, j // 2
    scale = 1.0 / math.sqrt(BLOCK)
    kv, qg, table = r.kv, r.qg, r.table

    def sibling():
        return (i + 1 - 2 * core, j)

    def x_partner():
        return ((i + 8) % 16, j)

    def y_peer(d):
        return (x * 8 + ((y + d) % 4) * 2 + core, j)

    def h_partner():
        return (i, j + 1 - 2 * h)

    def z_peer(d):
        return (i, ((z + d) % 4) * 2 + h)

    def zh_peer(d):
        return (i, ((z + d) % 4) * 2 + 1 - h)

    loads = []
    for n, (src, dst) in enumerate(
        ((r.k, kv.at[i, 0]), (r.v, kv.at[i, 1]), (r.q, qg.at[j, 0]), (r.g, qg.at[j, 1]))
    ):
        loads.append(pltpu.make_async_copy(src, dst, r.local_sem.at[n]))
        loads[-1].start()

    peers = [sibling(), x_partner(), h_partner()]
    peers += [y_peer(d) for d in (1, 2, 3)] + [z_peer(d) for d in (1, 2, 3)]
    peers += [zh_peer(d) for d in (1, 2, 3)]
    barrier = pltpu.get_barrier_semaphore()
    for peer in peers:
        pl.semaphore_signal(barrier, inc=1, device_id=peer, device_id_type=MESH)
    pl.semaphore_wait(barrier, len(peers))
    for load in loads:
        load.wait()

    def send(src, dst, sems, n, peer):
        copy = pltpu.make_async_remote_copy(
            src_ref=src, dst_ref=dst, send_sem=sems[0].at[n], recv_sem=sems[1].at[n],
            device_id=peer, device_id_type=MESH,
        )
        copy.start()
        return copy

    kv_sems, qg_sems = (r.kv_send, r.kv_recv), (r.qg_send, r.qg_recv)
    kv_x = send(kv.at[i], kv.at[i], kv_sems, 0, x_partner())
    qg_h = send(qg.at[j], qg.at[j], qg_sems, 0, h_partner())
    kv_y = [send(kv.at[i], kv.at[i], kv_sems, d, y_peer(d)) for d in (1, 3, 2)]
    qg_z = [send(qg.at[j], qg.at[j], qg_sems, d, z_peer(d)) for d in (1, 3, 2)]
    kv_sib = [send(kv.at[i], kv.at[i], kv_sems, 7, sibling())]

    list_pairs(i, j, r.lists, r.table_v, None if dense else r.slot_query)
    to_smem = pltpu.make_async_copy(r.table_v, table, r.local_sem.at[4])
    to_smem.start()
    r.bias[0] = jnp.zeros((BLOCK, BLOCK), jnp.float32)
    r.bias[1] = jnp.where(
        iota((BLOCK, BLOCK), 0) <= iota((BLOCK, BLOCK), 1), 0.0, masked_score
    ).astype(jnp.float32)
    none = 0 if not dense else slice(None)
    r.key_acc[none] = jnp.zeros(r.key_acc[none].shape, jnp.float32)
    r.query_acc[none] = jnp.zeros(r.query_acc[none].shape, jnp.float32)

    kv_x.wait_recv()
    far = (i + 8) % 16
    kv_far = [send(kv.at[far], kv.at[far], kv_sems, 3 + d, y_peer(d)) for d in (1, 3, 2)]
    kv_sib.append(send(kv.at[far], kv.at[far], kv_sems, 8, sibling()))
    qg_h.wait_recv()
    other = j + 1 - 2 * h
    qg_far = [send(qg.at[other], qg.at[other], qg_sems, 3 + d, z_peer(d)) for d in (1, 3, 2)]

    if not dense:
        r.flag[0, 0] = most_pairs(r.lists)

    for n, d in enumerate((1, 3, 2)):
        kv_y[n].wait_recv()
        src = x * 8 + ((y - d + 4) % 4) * 2 + core
        kv_sib.append(send(kv.at[src], kv.at[src], kv_sems, 8 + d, sibling()))
    for n, d in enumerate((1, 3, 2)):
        kv_far[n].wait_recv()
        src = (1 - x) * 8 + ((y - d + 4) % 4) * 2 + core
        kv_sib.append(send(kv.at[src], kv.at[src], kv_sems, 11 + d, sibling()))
    for copy in qg_z + qg_far:
        copy.wait_recv()
    for copy in kv_sib:
        copy.wait_recv()
    to_smem.wait()

    (dense_stats if dense else slot_stats)(r, i, j, scale)

    st_sems = (r.st_send, r.st_recv)
    st_copies = []
    r.stats[j] = r.stats_out[...]
    for n, peer in enumerate(
        [z_peer(1), z_peer(3), h_partner(), z_peer(2), zh_peer(1), zh_peer(3), zh_peer(2)]
    ):
        st_copies.append(send(r.stats_out, r.stats.at[j], st_sems, n, peer))
    for copy in st_copies:
        copy.wait_recv()
    logs = r.stats[:, 0]
    best = jnp.max(logs, axis=0)
    offset = best + jnp.log2(jnp.sum(jnp.exp2(logs - best[None]), axis=0))
    delta = jnp.sum(jnp.exp2(logs - offset[None]) * r.stats[:, 1], axis=0)
    for q in range(16):
        r.offsets[q] = offset[q : q + 1, :]
        r.deltas[q] = delta[q : q + 1, :]

    (dense_key_grads if dense else slot_key_grads)(r, i, j, scale)

    def key_part(block):
        return r.key_acc[block if dense else table[KEY_END, block]]

    def query_part(block):
        return r.query_acc[block if dense else table[QUERY_END, block]]

    red = (r.red_send, r.red_recv)

    def sib_step(n, carry):
        owner = (n % 2) * 8 + (n // 2) * 2 + 1 - core
        for b in range(2):
            r.sib_out[n, :, b] = key_part(owner * 2 + b).astype(jnp.bfloat16)
        return carry

    lax.fori_loop(0, 8, sib_step, 0)
    sib_copy = send(r.sib_out, r.sib_in, red, 0, sibling())

    if not dense:
        slot_query_grads(r)

    def z_step(n, carry):
        for b in range(2):
            r.z_out[n // 2, n % 2, :, b] = query_part(n * 2 + b).astype(jnp.bfloat16)
        return carry

    lax.fori_loop(0, 8, z_step, 0)
    z_copies = []
    for d in (1, 3, 2):
        z_copies.append(send(r.z_out.at[(z + d) % 4], r.z_in.at[d - 1], red, d, z_peer(d)))

    sib_copy.wait_recv()

    def y_step(n, carry):
        owner = (n % 2) * 8 + (n // 2) * 2 + core
        for b in range(2):
            both = key_part(owner * 2 + b) + r.sib_in[n, :, b].astype(jnp.float32)
            r.y_out[n // 2, n % 2, :, b] = both.astype(jnp.bfloat16)
        return carry

    lax.fori_loop(0, 8, y_step, 0)
    y_copies = []
    for d in (1, 3, 2):
        y_copies.append(send(r.y_out.at[(y + d) % 4], r.y_in.at[d - 1], red, 3 + d, y_peer(d)))

    def sum_of(own, arrived, row, col):
        total = own[row, col].astype(jnp.float32)
        for d in range(3):
            total += arrived[d, col].astype(jnp.float32)
        return total

    for copy in z_copies:
        copy.wait_recv()
    r.h_out[...] = sum_of(r.z_out, r.z_in, z, 1 - h).astype(jnp.bfloat16)
    h_copy = send(r.h_out, r.h_in, red, 7, h_partner())
    for copy in y_copies:
        copy.wait_recv()
    r.x_out[...] = sum_of(r.y_out, r.y_in, y, 1 - x).astype(jnp.bfloat16)
    x_copy = send(r.x_out, r.x_in, red, 8, x_partner())
    query_sum = sum_of(r.z_out, r.z_in, z, h)
    key_sum = sum_of(r.y_out, r.y_in, y, x)
    h_copy.wait_recv()
    query_sum += r.h_in[...].astype(jnp.float32)
    for b in range(2):
        rows = pl.ds(b * BLOCK, BLOCK)
        r.query_grads[rows, :] = (query_sum[0, b] * scale).astype(jnp.bfloat16)
        r.attended[rows, :] = query_sum[1, b].astype(jnp.bfloat16)
    x_copy.wait_recv()
    key_sum += r.x_in[...].astype(jnp.float32)
    for b in range(2):
        rows = pl.ds(b * BLOCK, BLOCK)
        r.key_grads[rows, :] = (key_sum[0, b] * scale).astype(jnp.bfloat16)
        r.value_grads[rows, :] = key_sum[1, b].astype(jnp.bfloat16)

    for copy in [kv_x, qg_h, sib_copy, h_copy, x_copy]:
        copy.wait_send()
    for copy in kv_y + kv_far + kv_sib + qg_z + qg_far + st_copies + z_copies + y_copies:
        copy.wait_send()


def slot_stats(r, i, j, scale):
    kv, qg, table = r.kv, r.qg, r.table

    def step(n, carry):
        for u in range(UNROLL):
            s = n * UNROLL + u
            k, q = table[KEY, s], table[QUERY, s]
            scores = against(kv[k // 2, 0, k % 2], qg[q // 2, 0, q % 2]) * (scale * LOG2E)
            scores += r.bias[table[DIAGONAL, s]]
            prob_grad = against(kv[k // 2, 1, k % 2], qg[q // 2, 1, q % 2])
            top = jnp.max(scores, axis=0, keepdims=True)
            prob = jnp.exp2(scores - top)
            r.probs[s] = prob
            r.prob_grads[s] = prob_grad
            r.tops[pl.ds(s, 1), :] = top
            r.totals[pl.ds(s, 1), :] = jnp.sum(prob, axis=0, keepdims=True)
            r.moments[pl.ds(s, 1), :] = jnp.sum(prob * prob_grad, axis=0, keepdims=True)
        return carry

    lax.fori_loop(0, SLOTS // UNROLL, step, 0)

    top, total, moment, owner = r.tops[...], r.totals[...], r.moments[...], r.slot_query[...]
    for q in range(16):
        mine = owner == float(q)
        top_q = jnp.max(jnp.where(mine, top, masked_score), axis=0, keepdims=True)
        part = jnp.where(mine, jnp.exp2(top - top_q), 0.0)
        total_q = jnp.sum(part * total, axis=0, keepdims=True)
        moment_q = jnp.sum(part * moment, axis=0, keepdims=True)
        put_stats(r, q, top_q, total_q, moment_q)


def put_stats(r, q, top, total, moment):
    some = total > 0
    safe = jnp.where(some, total, 1.0)
    r.stats_out[0, pl.ds(q, 1), :] = jnp.where(some, top + jnp.log2(safe), masked_score)
    r.stats_out[1, pl.ds(q, 1), :] = moment / safe


def slot_key_grads(r, i, j, scale):
    def step(n, carry):
        for u in range(UNROLL):
            s = n * UNROLL + u
            q = r.table[QUERY, s]
            keep = r.table[SAME_KEY, s].astype(jnp.float32)
            prob = r.probs[s] * jnp.exp2(r.tops[pl.ds(s, 1), :] - r.offsets[q])
            weights = prob.astype(jnp.bfloat16)
            score_grad = (prob * (r.prob_grads[s] - r.deltas[q])).astype(jnp.bfloat16)
            r.rounded[s, 0] = score_grad
            r.rounded[s, 1] = weights
            r.key_acc[s + 1, 0] = r.key_acc[s, 0] * keep + dot(score_grad, r.qg[q // 2, 0, q % 2])
            r.key_acc[s + 1, 1] = r.key_acc[s, 1] * keep + dot(weights, r.qg[q // 2, 1, q % 2])
        return carry

    lax.fori_loop(0, SLOTS // UNROLL, step, 0)


def slot_query_grads(r):
    def step(n, carry):
        for u in range(UNROLL):
            s = n * UNROLL + u
            k, at = r.table[PERM_KEY, s], r.table[PERM, s]
            keep = r.table[SAME_QUERY, s].astype(jnp.float32)
            for m in range(2):
                new = across(r.rounded[at, m], r.kv[k // 2, m, k % 2])
                r.query_acc[s + 1, m] = r.query_acc[s, m] * keep + new
        return carry

    lax.fori_loop(0, SLOTS // UNROLL, step, 0)


def dense_tile(r, i, j, scale, q, k):
    scores = against(r.kv[k // 2, 0, k % 2], r.qg[q // 2, 0, q % 2]) * (scale * LOG2E)
    own = (k // 2) * 16 + 2 * j + k % 2 == 16 * i + q
    scores += r.bias[own.astype(jnp.int32)]
    prob_grad = against(r.kv[k // 2, 1, k % 2], r.qg[q // 2, 1, q % 2])
    listed = r.table[LISTED + k, q].astype(jnp.float32)
    return scores + (1.0 - listed) * masked_score, prob_grad, listed


def dense_stats(r, i, j, scale):
    def query_step(q, carry):
        def key_step(k, state):
            top, total, moment = state
            scores, prob_grad, listed = dense_tile(r, i, j, scale, q, k)
            higher = jnp.maximum(top, jnp.max(scores, axis=0, keepdims=True))
            prob = jnp.exp2(scores - higher) * listed
            shrink = jnp.exp2(top - higher)
            total = total * shrink + jnp.sum(prob, axis=0, keepdims=True)
            moment = moment * shrink + jnp.sum(prob * prob_grad, axis=0, keepdims=True)
            return higher, total, moment

        zero = jnp.zeros((1, BLOCK), jnp.float32)
        put_stats(r, q, *lax.fori_loop(0, 32, key_step, (zero + masked_score, zero, zero)))
        return carry

    lax.fori_loop(0, 16, query_step, 0)


def dense_key_grads(r, i, j, scale):
    def step(n, carry):
        q, k = n // 32, n % 32
        scores, prob_grad, listed = dense_tile(r, i, j, scale, q, k)
        prob = jnp.exp2(scores - r.offsets[q]) * listed
        weights = prob.astype(jnp.bfloat16)
        score_grad = (prob * (prob_grad - r.deltas[q])).astype(jnp.bfloat16)
        for m, left in enumerate((score_grad, weights)):
            r.key_acc[k, m] = r.key_acc[k, m] + dot(left, r.qg[q // 2, m, q % 2])
            r.query_acc[q, m] = r.query_acc[q, m] + across(left, r.kv[k // 2, m, k % 2])
        return carry

    lax.fori_loop(0, 16 * 32, step, 0)


def attention(dense, queries, keys, values, grad_out, lists):
    rows, head = queries.shape
    out = jax.ShapeDtypeStruct((rows, head), jnp.bfloat16)
    f32, bf16 = jnp.float32, jnp.bfloat16
    tile = (BLOCK, BLOCK)
    table_rows = LISTED + 32 if dense else LISTED
    dma = pltpu.SemaphoreType.DMA
    any_spec = pl.BlockSpec(memory_space=pl.ANY)
    vmem_spec = pl.BlockSpec(memory_space=pltpu.VMEM)
    smem_spec = pl.BlockSpec(memory_space=pltpu.SMEM)
    scratch = {
        "kv": pltpu.VMEM((16, 2, 2) + tile, bf16),
        "qg": pltpu.VMEM((8, 2, 2) + tile, bf16),
        "table_v": pltpu.VMEM((table_rows, 128), jnp.int32),
        "table": pltpu.SMEM((table_rows, 128), jnp.int32),
        "bias": pltpu.VMEM((2,) + tile, f32),
        "stats_out": pltpu.VMEM((2, 16, 128), f32),
        "stats": pltpu.VMEM((8, 2, 16, 128), f32),
        "offsets": pltpu.VMEM((16, 1, 128), f32),
        "deltas": pltpu.VMEM((16, 1, 128), f32),
        "key_acc": pltpu.VMEM((32 if dense else SLOTS + 1, 2) + tile, f32),
        "query_acc": pltpu.VMEM((16 if dense else SLOTS + 1, 2) + tile, f32),
        "sib_out": pltpu.VMEM((8, 2, 2) + tile, bf16),
        "sib_in": pltpu.VMEM((8, 2, 2) + tile, bf16),
        "y_out": pltpu.VMEM((4, 2, 2, 2) + tile, bf16),
        "y_in": pltpu.VMEM((3, 2, 2, 2) + tile, bf16),
        "x_out": pltpu.VMEM((2, 2) + tile, bf16),
        "x_in": pltpu.VMEM((2, 2) + tile, bf16),
        "z_out": pltpu.VMEM((4, 2, 2, 2) + tile, bf16),
        "z_in": pltpu.VMEM((3, 2, 2, 2) + tile, bf16),
        "h_out": pltpu.VMEM((2, 2) + tile, bf16),
        "h_in": pltpu.VMEM((2, 2) + tile, bf16),
        "local_sem": dma((5,)),
        "kv_send": dma((15,)),
        "kv_recv": dma((15,)),
        "qg_send": dma((7,)),
        "qg_recv": dma((7,)),
        "st_send": dma((7,)),
        "st_recv": dma((7,)),
        "red_send": dma((9,)),
        "red_recv": dma((9,)),
    }
    if not dense:
        scratch |= {
            "slot_query": pltpu.VMEM((SLOTS, 1), f32),
            "probs": pltpu.VMEM((SLOTS,) + tile, f32),
            "prob_grads": pltpu.VMEM((SLOTS,) + tile, f32),
            "tops": pltpu.VMEM((SLOTS, 128), f32),
            "totals": pltpu.VMEM((SLOTS, 128), f32),
            "moments": pltpu.VMEM((SLOTS, 128), f32),
            "rounded": pltpu.VMEM((SLOTS, 2) + tile, bf16),
        }
    outs = ["attended", "query_grads", "key_grads", "value_grads"] + ["flag"] * (not dense)
    out_shape, out_specs = [out] * 4, [vmem_spec] * 4
    if not dense:
        out_shape.append(jax.ShapeDtypeStruct((1, 1), f32))
        out_specs.append(smem_spec)
    return pl.pallas_call(
        functools.partial(kernel, ["q", "k", "v", "g", "lists"] + outs + list(scratch), dense),
        out_shape=out_shape,
        in_specs=[any_spec] * 4 + [vmem_spec],
        out_specs=out_specs,
        scratch_shapes=list(scratch.values()),
        compiler_params=pltpu.CompilerParams(
            collective_id=1 if dense else 0, has_side_effects=True, vmem_limit_bytes=56 << 20
        ),
        name="dense_attention" if dense else "block_sparse_attention",
    )(*(a.reshape(2, BLOCK, BLOCK) for a in (queries, keys, values, grad_out)), lists)


def per_device(queries, keys, values, grad_out, key_blocks):
    args = (queries, keys, values, grad_out, key_blocks.T)
    *outs, most = attention(False, *args)
    return lax.cond(
        most[0, 0] > SLOTS,
        lambda: tuple(attention(True, *args)),
        lambda: tuple(outs),
    )


def solution(mesh):
    split = P(("qblk", "kblk"), None)
    return jax.shard_map(
        per_device,
        mesh=mesh,
        in_specs=(split, split, split, split, P()),
        out_specs=(split, split, split, split),
        check_vma=False,
    )
```

```python
import functools
import math

import jax
import jax.numpy as jnp
from jax import lax
from jax.experimental import pallas as pl
from jax.experimental.pallas import tpu as pltpu
from jax.sharding import PartitionSpec as P

BLOCK = 128
SLOTS = 64
UNROLL = 8
MESH = pl.DeviceIdType.MESH

masked_score = -1e30
LOG2E = 1.4426950408889634


def against(left, right):
    return lax.dot_general(
        left, right, (((1,), (1,)), ((), ())), preferred_element_type=jnp.float32
    )


def across(left, right):
    return lax.dot_general(
        left, right, (((0,), (0,)), ((), ())), preferred_element_type=jnp.float32
    )


def dot(left, right):
    return jnp.dot(left, right, preferred_element_type=jnp.float32)


KEY, QUERY, SAME_KEY, DIAGONAL, PERM, PERM_KEY, SAME_QUERY, KEY_END, QUERY_END = range(9)
LISTED = 16

STAT_STEPS = ((False, 1), (False, -1), (True, 0), (False, 2), (True, 1), (True, -1), (True, 2))


def iota(shape, dim):
    return lax.broadcasted_iota(jnp.int32, shape, dim)


def fiota(shape, dim):
    return iota(shape, dim).astype(jnp.float32)


def ones_where(cond):
    return jnp.where(cond, 1.0, 0.0).astype(jnp.float32)


def query_id(i, j, q):
    x = (i // 8 + j % 2 + (q // 2) % 2) % 2
    return (x * 8 + i % 8) * 16 + q


def list_pairs(i, j, lists_ref, table, slot_query):
    lists = lists_ref[...].astype(jnp.float32)
    chosen = ones_where(iota((256, 16), 0) == query_id(i, j, iota((256, 16), 1)))
    own = dot(lists, chosen)
    key_ids = ((iota((32, 16), 0) // 2) * 16 + 2 * j + iota((32, 16), 0) % 2).astype(jnp.float32)
    pairs = jnp.zeros((32, 16), jnp.float32)
    for n in range(16):
        pairs = jnp.maximum(pairs, ones_where(own[n : n + 1, :] == key_ids))
    earlier_query = ones_where(iota((16, 16), 0) < iota((16, 16), 1))
    earlier_key = ones_where(iota((32, 32), 1) < iota((32, 32), 0))
    in_key = dot(pairs, earlier_query)
    in_query = dot(earlier_key, pairs)
    key_count = jnp.sum(pairs, axis=1, keepdims=True)
    query_count = jnp.sum(pairs, axis=0, keepdims=True)
    key_first = jnp.sum(in_query, axis=1, keepdims=True)
    query_first = jnp.sum(in_key, axis=0, keepdims=True)
    by_key = jnp.where(pairs > 0, key_first + in_key, -1.0)
    by_query = jnp.where(pairs > 0, query_first + in_query, -1.0)
    total = jnp.sum(jnp.sum(pairs, axis=1, keepdims=True), axis=0, keepdims=True)

    lane = fiota((32, 128), 1)
    keys = fiota((32, 128), 0)
    id_col = (iota((32, 128), 0) // 2) * 16 + 2 * j + iota((32, 128), 0) % 2
    zero = jnp.zeros((32, 128), jnp.float32)
    rows = {n: zero for n in range(7)}
    for q in range(16):
        at_key = by_key[:, q : q + 1] == lane
        at_query = by_query[:, q : q + 1] == lane
        rows[KEY] += jnp.where(at_key, keys, 0.0)
        rows[QUERY] += jnp.where(at_key, float(q), 0.0)
        rows[SAME_KEY] += jnp.where(at_key, ones_where(in_key[:, q : q + 1] > 0), 0.0)
        rows[DIAGONAL] += jnp.where(at_key & (id_col == query_id(i, j, q)), 1.0, 0.0)
        rows[PERM] += jnp.where(at_query, by_key[:, q : q + 1], 0.0)
        rows[PERM_KEY] += jnp.where(at_query, keys, 0.0)
        rows[SAME_QUERY] += jnp.where(at_query, ones_where(in_query[:, q : q + 1] > 0), 0.0)
    most = {KEY: 31, QUERY: 15, SAME_KEY: 1, DIAGONAL: 1, PERM: SLOTS - 1, PERM_KEY: 31, SAME_QUERY: 1}
    for n in range(7):
        rows[n] = jnp.sum(rows[n], axis=0, keepdims=True)
        table[n : n + 1, :] = jnp.clip(rows[n].astype(jnp.int32), 0, most[n])
    key_end = jnp.where(key_count > 0, key_first + key_count, 0.0)
    key_end = jnp.sum(jnp.where(keys == lane, key_end, 0.0), axis=0, keepdims=True)
    table[KEY_END : KEY_END + 1, :] = jnp.clip(key_end.astype(jnp.int32), 0, SLOTS)
    query_end = jnp.where(query_count > 0, query_first + query_count, 0.0)
    table[QUERY_END : QUERY_END + 1, 0:16] = jnp.clip(query_end.astype(jnp.int32), 0, SLOTS)
    if table.shape[0] > LISTED:
        table[LISTED : LISTED + 32, 0:16] = pairs.astype(jnp.int32)
        return

    query_row = jnp.where(fiota((1, 128), 1) < total, rows[QUERY], -1.0)
    slot_query[...] = jnp.sum(
        jnp.where(iota((SLOTS, 128), 0) == iota((SLOTS, 128), 1), query_row, 0.0),
        axis=1,
        keepdims=True,
    )


def most_pairs(lists_ref):
    lists = lists_ref[...]
    groups = (lists // 2) % 8
    counts = jnp.zeros((8, 256), jnp.float32)
    group_of = iota((8, 256), 0)
    for n in range(16):
        fresh = jnp.ones((1, 256), jnp.float32)
        for m in range(n):
            fresh = jnp.where(lists[m : m + 1] == lists[n : n + 1], 0.0, fresh)
        counts += jnp.where(groups[n : n + 1] == group_of, fresh, 0.0)
    block = iota((256, 16), 0)
    query_group = (block // 16 % 8) * 2 + (block // 128 + block // 2 % 2) % 2
    member = ones_where(query_group == iota((256, 16), 1))
    return jnp.max(dot(counts, member))


class Refs:
    def __init__(self, names, refs):
        self.__dict__.update(zip(names, refs, strict=True))


def flip(bit):
    return 1 - bit


class Ring:
    def __init__(self, a, p, peer, row, blocks, gather_sems, out, own_in, part_in, part_out, sum_out, sum_in, sum_sems):
        self.a, self.p, self.peer, self.row = a, p, peer, row
        self.blocks, self.gather_sems = blocks, gather_sems
        self.out, self.own_in, self.part_in, self.part_out = out, own_in, part_in, part_out
        self.sum_out, self.sum_in, self.sum_sems = sum_out, sum_in, sum_sems
        self.copies = []

    def at(self, step):
        return (self.p + step + 4) % 4

    def send(self, src, dst, sems, n, peer):
        copy = pltpu.make_async_remote_copy(
            src_ref=src, dst_ref=dst, send_sem=sems[0].at[n], recv_sem=sems[1].at[n],
            device_id=peer, device_id_type=MESH,
        )
        copy.start()
        self.copies.append(copy)
        return copy

    def pass_block(self, n, row, peer):
        return self.send(self.blocks.at[row], self.blocks.at[row], self.gather_sems, n, peer)

    def pass_half(self, n, row, half, peer):
        ref = self.blocks.at[row, half]
        return self.send(ref, ref, self.gather_sems, n, peer)

    def start_own(self):
        own = self.row(self.a, self.p)
        self.to_pair = self.pass_block(0, own, self.peer(True, 0))
        self.up = self.pass_block(1, own, self.peer(False, 1))
        self.down = self.pass_block(2, own, self.peer(False, -1))

    def start_far(self):
        self.to_pair.wait_recv()
        far = self.row(flip(self.a), self.p)
        self.far_up = self.pass_block(5, far, self.peer(False, 1))
        self.far_down = self.pass_block(6, far, self.peer(False, -1))
        return far

    def pass_on(self, n, arrived, step, a):
        arrived.wait_recv()
        row = self.row(a, self.at(step))
        half = 0 if step < 0 else 1
        return row, self.pass_half(n, row, half, self.peer(False, -step))

    def start_sum(self, phase):
        a = flip(self.a) if phase == 0 else self.a
        n, out = 6 * phase, self.out
        opposite = self.at(2)
        self.part = [
            self.send(out.at[a, opposite, 0], self.part_in.at[phase, 0], self.sum_sems, n, self.peer(False, 1)),
            self.send(out.at[a, opposite, 1], self.part_in.at[phase, 1], self.sum_sems, n + 1, self.peer(False, -1)),
        ]
        plain = [
            self.send(out.at[a, self.at(1), 1], self.own_in.at[phase, 1], self.sum_sems, n + 2, self.peer(False, 1)),
            self.send(out.at[a, self.at(-1), 0], self.own_in.at[phase, 0], self.sum_sems, n + 3, self.peer(False, -1)),
        ]
        return [a, phase, self.part, plain, []]

    def add_part(self, state):
        a, phase, part, _, summed = state
        n = 6 * phase + 4
        for half, step in ((0, 1), (1, -1)):
            part[half].wait_recv()
            both = self.out[a, self.at(step), half].astype(jnp.float32) + self.part_in[phase, half].astype(jnp.float32)
            self.part_out[phase, half] = both.astype(jnp.bfloat16)
            summed.append(
                self.send(
                    self.part_out.at[phase, half], self.own_in.at[phase, 2 + half], self.sum_sems, n + half,
                    self.peer(False, step),
                )
            )

    def total(self, state):
        a, phase, _, plain, summed = state
        for copy in plain + summed:
            copy.wait_recv()
        total = self.out[a, self.p].astype(jnp.float32)
        total += self.own_in[phase, 0:2].astype(jnp.float32)
        return total + self.own_in[phase, 2:4].astype(jnp.float32)

    def send_total(self, total):
        self.sum_out[...] = total.astype(jnp.bfloat16)
        self.across_pair = self.send(self.sum_out, self.sum_in, self.sum_sems, 12, self.peer(True, 0))

    def other_total(self):
        self.across_pair.wait_recv()
        return self.sum_in[...].astype(jnp.float32)


class Refs:
    def __init__(self, names, refs):
        self.__dict__.update(zip(names, refs, strict=True))


def kernel(names, dense, *refs):
    r = Refs(names, refs)
    i, j = lax.axis_index("qblk"), lax.axis_index("kblk")
    core, y, x = i % 2, (i // 2) % 4, i // 8
    h, z = j % 2, j // 2
    scale = 1.0 / math.sqrt(BLOCK)
    kv, qg, table = r.kv, r.qg, r.table

    def key_row(x, y):
        return x * 8 + y * 2 + core

    def query_row(h, z):
        return z * 2 + h

    def key_peer(pair, step):
        return (key_row(flip(x) if pair else x, (y + step + 4) % 4), j)

    def query_peer(pair, step):
        at = (z + step + 4) % 4
        return ((i + 8) % 16, query_row(flip(h), at)) if pair else (i, query_row(h, at))

    sibling = (i + 1 - 2 * core, j)

    loads = []
    for n, (src, dst) in enumerate(
        ((r.k, kv.at[i, 0]), (r.v, kv.at[i, 1]), (r.q, qg.at[j, 0]), (r.g, qg.at[j, 1]))
    ):
        loads.append(pltpu.make_async_copy(src, dst, r.local_sem.at[n]))
        loads[-1].start()

    stat_peers = [query_peer(pair, step) for pair, step in STAT_STEPS]
    peers = [sibling, key_peer(True, 0), key_peer(False, 1), key_peer(False, -1)] + stat_peers
    barrier = pltpu.get_barrier_semaphore()
    for peer in peers:
        pl.semaphore_signal(barrier, inc=1, device_id=peer, device_id_type=MESH)
    pl.semaphore_wait(barrier, len(peers))
    for load in loads:
        load.wait()

    keys = Ring(
        x, y, key_peer, key_row, kv, (r.kv_send, r.kv_recv), r.key_out, r.key_own_in, r.key_part_in,
        r.key_part_out, r.key_sum_out, r.key_sum_in, (r.key_send, r.key_recv),
    )
    queries = Ring(
        h, z, query_peer, query_row, qg, (r.qg_send, r.qg_recv), r.query_out, r.query_own_in, r.query_part_in,
        r.query_part_out, r.query_sum_out, r.query_sum_in, (r.query_send, r.query_recv),
    )
    sib = []

    def to_sibling(ref):
        sib.append(keys.send(ref, ref, (r.sib_send, r.sib_recv), len(sib), sibling))

    keys.start_own()
    queries.start_own()
    to_sibling(kv.at[i])

    list_pairs(i, j, r.lists, r.table_v, None if dense else r.slot_query)
    to_smem = pltpu.make_async_copy(r.table_v, table, r.local_sem.at[4])
    to_smem.start()

    to_sibling(kv.at[keys.start_far()])
    queries.start_far()
    far = (keys.far_down, keys.far_up), (queries.far_down, queries.far_up)
    on = [], []
    for ring, halves in ((keys, on[0]), (queries, on[1])):
        for n, arrived, step in ((3, ring.up, -1), (4, ring.down, 1)):
            row, copy = ring.pass_on(n, arrived, step, ring.a)
            halves.append((copy, ring.row(ring.a, ring.at(2)), n - 3))
            if ring is keys:
                to_sibling(kv.at[row])

    r.bias[0] = jnp.zeros((BLOCK, BLOCK), jnp.float32)
    r.bias[1] = jnp.where(
        iota((BLOCK, BLOCK), 0) <= iota((BLOCK, BLOCK), 1), 0.0, masked_score
    ).astype(jnp.float32)
    none = 0 if not dense else slice(None)
    r.key_acc[none] = jnp.zeros(r.key_acc[none].shape, jnp.float32)
    r.query_acc[none] = jnp.zeros(r.query_acc[none].shape, jnp.float32)
    if not dense:
        r.flag[0, 0] = most_pairs(r.lists)

    for ring, halves in ((keys, on[0]), (queries, on[1])):
        for n, arrived, step in ((7, ring.far_up, -1), (8, ring.far_down, 1)):
            row, copy = ring.pass_on(n, arrived, step, flip(ring.a))
            halves.append((copy, ring.row(flip(ring.a), ring.at(2)), n - 7))
            if ring is keys:
                to_sibling(kv.at[row])
    for ring, halves in ((keys, on[0]), (queries, on[1])):
        for copy, row, half in halves:
            copy.wait_recv()
            if ring is keys:
                to_sibling(kv.at[row, half])
    for copy in sib:
        copy.wait_recv()
    to_smem.wait()

    (dense_stats if dense else slot_stats)(r, i, j, scale)

    st_sems = (r.st_send, r.st_recv)
    st_copies = []
    r.stats[j] = r.stats_out[...]
    for n, peer in enumerate(stat_peers):
        st_copies.append(queries.send(r.stats_out, r.stats.at[j], st_sems, n, peer))
    for copy in st_copies:
        copy.wait_recv()
    logs = r.stats[:, 0]
    best = jnp.max(logs, axis=0)
    offset = best + jnp.log2(jnp.sum(jnp.exp2(logs - best[None]), axis=0))
    delta = jnp.sum(jnp.exp2(logs - offset[None]) * r.stats[:, 1], axis=0)
    for q in range(16):
        r.offsets[q] = offset[q : q + 1, :]
        r.deltas[q] = delta[q : q + 1, :]

    (dense_key_grads if dense else slot_key_grads)(r, i, j, scale)

    def key_part(block):
        return r.key_acc[block if dense else table[KEY_END, block]]

    def query_part(block):
        return r.query_acc[block if dense else table[QUERY_END, block]]

    swaps = []
    for phase, at in ((0, flip(x)), (1, x)):

        def sib_step(n, carry, phase=phase, at=at):
            owner = at * 8 + n * 2 + 1 - core
            for b in range(2):
                r.sib_out[phase, n, :, b] = key_part(owner * 2 + b).astype(jnp.bfloat16)
            return carry

        lax.fori_loop(0, 4, sib_step, 0)
        swaps.append(
            keys.send(r.sib_out.at[phase], r.sib_in.at[phase], (r.sib_send, r.sib_recv), 10 + phase, sibling)
        )

    if not dense:
        slot_query_grads(r)

    def query_out_step(n, carry):
        for b in range(2):
            r.query_out[n % 2, n // 2, :, b] = query_part(n * 2 + b).astype(jnp.bfloat16)
        return carry

    lax.fori_loop(0, 8, query_out_step, 0)
    query_sums = [queries.start_sum(0), queries.start_sum(1)]

    key_sums = []
    for phase, at in ((0, flip(x)), (1, x)):
        swaps[phase].wait_recv()

        def key_out_step(n, carry, phase=phase, at=at):
            owner = at * 8 + n * 2 + core
            for b in range(2):
                both = key_part(owner * 2 + b) + r.sib_in[phase, n, :, b].astype(jnp.float32)
                r.key_out[at, n, :, b] = both.astype(jnp.bfloat16)
            return carry

        lax.fori_loop(0, 4, key_out_step, 0)
        key_sums.append(keys.start_sum(phase))

    for phase in range(2):
        queries.add_part(query_sums[phase])
        keys.add_part(key_sums[phase])
    queries.send_total(queries.total(query_sums[0]))
    keys.send_total(keys.total(key_sums[0]))
    query_total = queries.total(query_sums[1]) + queries.other_total()
    for b in range(2):
        rows = pl.ds(b * BLOCK, BLOCK)
        r.query_grads[rows, :] = (query_total[0, b] * scale).astype(jnp.bfloat16)
        r.attended[rows, :] = query_total[1, b].astype(jnp.bfloat16)
    key_total = keys.total(key_sums[1]) + keys.other_total()
    for b in range(2):
        rows = pl.ds(b * BLOCK, BLOCK)
        r.key_grads[rows, :] = (key_total[0, b] * scale).astype(jnp.bfloat16)
        r.value_grads[rows, :] = key_total[1, b].astype(jnp.bfloat16)

    for copy in keys.copies + queries.copies:
        copy.wait_send()


def slot_stats(r, i, j, scale):
    kv, qg, table = r.kv, r.qg, r.table

    def step(n, carry):
        for u in range(UNROLL):
            s = n * UNROLL + u
            k, q = table[KEY, s], table[QUERY, s]
            scores = against(kv[k // 2, 0, k % 2], qg[q // 2, 0, q % 2]) * (scale * LOG2E)
            scores += r.bias[table[DIAGONAL, s]]
            prob_grad = against(kv[k // 2, 1, k % 2], qg[q // 2, 1, q % 2])
            top = jnp.max(scores, axis=0, keepdims=True)
            prob = jnp.exp2(scores - top)
            r.probs[s] = prob
            r.prob_grads[s] = prob_grad
            r.tops[pl.ds(s, 1), :] = top
            r.totals[pl.ds(s, 1), :] = jnp.sum(prob, axis=0, keepdims=True)
            r.moments[pl.ds(s, 1), :] = jnp.sum(prob * prob_grad, axis=0, keepdims=True)
        return carry

    lax.fori_loop(0, SLOTS // UNROLL, step, 0)

    top, total, moment, owner = r.tops[...], r.totals[...], r.moments[...], r.slot_query[...]
    for q in range(16):
        mine = owner == float(q)
        top_q = jnp.max(jnp.where(mine, top, masked_score), axis=0, keepdims=True)
        part = jnp.where(mine, jnp.exp2(top - top_q), 0.0)
        total_q = jnp.sum(part * total, axis=0, keepdims=True)
        moment_q = jnp.sum(part * moment, axis=0, keepdims=True)
        put_stats(r, q, top_q, total_q, moment_q)


def put_stats(r, q, top, total, moment):
    some = total > 0
    safe = jnp.where(some, total, 1.0)
    r.stats_out[0, pl.ds(q, 1), :] = jnp.where(some, top + jnp.log2(safe), masked_score)
    r.stats_out[1, pl.ds(q, 1), :] = moment / safe


def slot_key_grads(r, i, j, scale):
    def step(n, carry):
        for u in range(UNROLL):
            s = n * UNROLL + u
            q = r.table[QUERY, s]
            keep = r.table[SAME_KEY, s].astype(jnp.float32)
            prob = r.probs[s] * jnp.exp2(r.tops[pl.ds(s, 1), :] - r.offsets[q])
            weights = prob.astype(jnp.bfloat16)
            score_grad = (prob * (r.prob_grads[s] - r.deltas[q])).astype(jnp.bfloat16)
            r.rounded[s, 0] = score_grad
            r.rounded[s, 1] = weights
            r.key_acc[s + 1, 0] = r.key_acc[s, 0] * keep + dot(score_grad, r.qg[q // 2, 0, q % 2])
            r.key_acc[s + 1, 1] = r.key_acc[s, 1] * keep + dot(weights, r.qg[q // 2, 1, q % 2])
        return carry

    lax.fori_loop(0, SLOTS // UNROLL, step, 0)


def slot_query_grads(r):
    def step(n, carry):
        for u in range(UNROLL):
            s = n * UNROLL + u
            k, at = r.table[PERM_KEY, s], r.table[PERM, s]
            keep = r.table[SAME_QUERY, s].astype(jnp.float32)
            for m in range(2):
                new = across(r.rounded[at, m], r.kv[k // 2, m, k % 2])
                r.query_acc[s + 1, m] = r.query_acc[s, m] * keep + new
        return carry

    lax.fori_loop(0, SLOTS // UNROLL, step, 0)


def dense_tile(r, i, j, scale, q, k):
    scores = against(r.kv[k // 2, 0, k % 2], r.qg[q // 2, 0, q % 2]) * (scale * LOG2E)
    own = (k // 2) * 16 + 2 * j + k % 2 == query_id(i, j, q)
    scores += r.bias[own.astype(jnp.int32)]
    prob_grad = against(r.kv[k // 2, 1, k % 2], r.qg[q // 2, 1, q % 2])
    listed = r.table[LISTED + k, q].astype(jnp.float32)
    return scores + (1.0 - listed) * masked_score, prob_grad, listed


def dense_stats(r, i, j, scale):
    def query_step(q, carry):
        def key_step(k, state):
            top, total, moment = state
            scores, prob_grad, listed = dense_tile(r, i, j, scale, q, k)
            higher = jnp.maximum(top, jnp.max(scores, axis=0, keepdims=True))
            prob = jnp.exp2(scores - higher) * listed
            shrink = jnp.exp2(top - higher)
            total = total * shrink + jnp.sum(prob, axis=0, keepdims=True)
            moment = moment * shrink + jnp.sum(prob * prob_grad, axis=0, keepdims=True)
            return higher, total, moment

        zero = jnp.zeros((1, BLOCK), jnp.float32)
        put_stats(r, q, *lax.fori_loop(0, 32, key_step, (zero + masked_score, zero, zero)))
        return carry

    lax.fori_loop(0, 16, query_step, 0)


def dense_key_grads(r, i, j, scale):
    def step(n, carry):
        q, k = n // 32, n % 32
        scores, prob_grad, listed = dense_tile(r, i, j, scale, q, k)
        prob = jnp.exp2(scores - r.offsets[q]) * listed
        weights = prob.astype(jnp.bfloat16)
        score_grad = (prob * (prob_grad - r.deltas[q])).astype(jnp.bfloat16)
        for m, left in enumerate((score_grad, weights)):
            r.key_acc[k, m] = r.key_acc[k, m] + dot(left, r.qg[q // 2, m, q % 2])
            r.query_acc[q, m] = r.query_acc[q, m] + across(left, r.kv[k // 2, m, k % 2])
        return carry

    lax.fori_loop(0, 16 * 32, step, 0)


def attention(dense, queries, keys, values, grad_out, lists):
    rows, head = queries.shape
    out = jax.ShapeDtypeStruct((rows, head), jnp.bfloat16)
    f32, bf16 = jnp.float32, jnp.bfloat16
    tile = (BLOCK, BLOCK)
    table_rows = LISTED + 32 if dense else LISTED
    dma = pltpu.SemaphoreType.DMA
    any_spec = pl.BlockSpec(memory_space=pl.ANY)
    vmem_spec = pl.BlockSpec(memory_space=pltpu.VMEM)
    smem_spec = pl.BlockSpec(memory_space=pltpu.SMEM)
    scratch = {
        "kv": pltpu.VMEM((16, 2, 2) + tile, bf16),
        "qg": pltpu.VMEM((8, 2, 2) + tile, bf16),
        "table_v": pltpu.VMEM((table_rows, 128), jnp.int32),
        "table": pltpu.SMEM((table_rows, 128), jnp.int32),
        "bias": pltpu.VMEM((2,) + tile, f32),
        "stats_out": pltpu.VMEM((2, 16, 128), f32),
        "stats": pltpu.VMEM((8, 2, 16, 128), f32),
        "offsets": pltpu.VMEM((16, 1, 128), f32),
        "deltas": pltpu.VMEM((16, 1, 128), f32),
        "key_acc": pltpu.VMEM((32 if dense else SLOTS + 1, 2) + tile, f32),
        "query_acc": pltpu.VMEM((16 if dense else SLOTS + 1, 2) + tile, f32),
        "sib_out": pltpu.VMEM((2, 4, 2, 2) + tile, bf16),
        "sib_in": pltpu.VMEM((2, 4, 2, 2) + tile, bf16),
        "local_sem": dma((5,)),
        "kv_send": dma((9,)),
        "kv_recv": dma((9,)),
        "qg_send": dma((9,)),
        "qg_recv": dma((9,)),
        "sib_send": dma((12,)),
        "sib_recv": dma((12,)),
        "st_send": dma((7,)),
        "st_recv": dma((7,)),
    }
    for ring in ("key", "query"):
        scratch |= {
            ring + "_out": pltpu.VMEM((2, 4, 2, 2) + tile, bf16),
            ring + "_own_in": pltpu.VMEM((2, 4, 2) + tile, bf16),
            ring + "_part_in": pltpu.VMEM((2, 2, 2) + tile, bf16),
            ring + "_part_out": pltpu.VMEM((2, 2, 2) + tile, bf16),
            ring + "_sum_out": pltpu.VMEM((2, 2) + tile, bf16),
            ring + "_sum_in": pltpu.VMEM((2, 2) + tile, bf16),
            ring + "_send": dma((13,)),
            ring + "_recv": dma((13,)),
        }
    if not dense:
        scratch |= {
            "slot_query": pltpu.VMEM((SLOTS, 1), f32),
            "probs": pltpu.VMEM((SLOTS,) + tile, f32),
            "prob_grads": pltpu.VMEM((SLOTS,) + tile, f32),
            "tops": pltpu.VMEM((SLOTS, 128), f32),
            "totals": pltpu.VMEM((SLOTS, 128), f32),
            "moments": pltpu.VMEM((SLOTS, 128), f32),
            "rounded": pltpu.VMEM((SLOTS, 2) + tile, bf16),
        }
    outs = ["attended", "query_grads", "key_grads", "value_grads"] + ["flag"] * (not dense)
    out_shape, out_specs = [out] * 4, [vmem_spec] * 4
    if not dense:
        out_shape.append(jax.ShapeDtypeStruct((1, 1), f32))
        out_specs.append(smem_spec)
    return pl.pallas_call(
        functools.partial(kernel, ["q", "k", "v", "g", "lists"] + outs + list(scratch), dense),
        out_shape=out_shape,
        in_specs=[any_spec] * 4 + [vmem_spec],
        out_specs=out_specs,
        scratch_shapes=list(scratch.values()),
        compiler_params=pltpu.CompilerParams(
            collective_id=1 if dense else 0, has_side_effects=True, vmem_limit_bytes=56 << 20
        ),
        name="dense_attention" if dense else "block_sparse_attention",
    )(*(a.reshape(2, BLOCK, BLOCK) for a in (queries, keys, values, grad_out)), lists)


def per_device(queries, keys, values, grad_out, key_blocks):
    args = (queries, keys, values, grad_out, key_blocks.T)
    *outs, most = attention(False, *args)
    return lax.cond(
        most[0, 0] > SLOTS,
        lambda: tuple(attention(True, *args)),
        lambda: tuple(outs),
    )


def solution(mesh):
    split = P(("qblk", "kblk"), None)
    return jax.shard_map(
        per_device,
        mesh=mesh,
        in_specs=(split, split, split, split, P()),
        out_specs=(split, split, split, split),
        check_vma=False,
    )
```

```python
import functools
import math

import jax
import jax.numpy as jnp
from jax import lax
from jax.experimental import pallas as pl
from jax.experimental.pallas import tpu as pltpu
from jax.sharding import PartitionSpec as P

BLOCK = 128
SLOTS = 64
UNROLL = 32
MESH = pl.DeviceIdType.MESH

masked_score = -1e30
LOG2E = 1.4426950408889634


def against(left, right):
    return lax.dot_general(
        left, right, (((1,), (1,)), ((), ())), preferred_element_type=jnp.float32
    )


def across(left, right):
    return lax.dot_general(
        left, right, (((0,), (0,)), ((), ())), preferred_element_type=jnp.float32
    )


def dot(left, right):
    return jnp.dot(left, right, preferred_element_type=jnp.float32)


KEY, QUERY, SAME_KEY, DIAGONAL, PERM, PERM_KEY, SAME_QUERY, KEY_END, QUERY_END = range(9)
LISTED = 16

STAT_STEPS = ((False, 1), (False, -1), (True, 0), (False, 2), (True, 1), (True, -1), (True, 2))


def iota(shape, dim):
    return lax.broadcasted_iota(jnp.int32, shape, dim)


def fiota(shape, dim):
    return iota(shape, dim).astype(jnp.float32)


def ones_where(cond):
    return jnp.where(cond, 1.0, 0.0).astype(jnp.float32)


def query_id(i, j, q):
    x = (i // 8 + j % 2 + (q // 2) % 2) % 2
    return (x * 8 + i % 8) * 16 + q


def list_pairs(i, j, lists_ref, table, slot_query):
    lists = lists_ref[...].astype(jnp.float32)
    chosen = ones_where(iota((256, 16), 0) == query_id(i, j, iota((256, 16), 1)))
    own = dot(lists, chosen)
    key_ids = ((iota((32, 16), 0) // 2) * 16 + 2 * j + iota((32, 16), 0) % 2).astype(jnp.float32)
    pairs = jnp.zeros((32, 16), jnp.float32)
    for n in range(16):
        pairs = jnp.maximum(pairs, ones_where(own[n : n + 1, :] == key_ids))
    earlier_query = ones_where(iota((16, 16), 0) < iota((16, 16), 1))
    earlier_key = ones_where(iota((32, 32), 1) < iota((32, 32), 0))
    in_key = dot(pairs, earlier_query)
    in_query = dot(earlier_key, pairs)
    key_count = jnp.sum(pairs, axis=1, keepdims=True)
    query_count = jnp.sum(pairs, axis=0, keepdims=True)
    key_first = jnp.sum(in_query, axis=1, keepdims=True)
    query_first = jnp.sum(in_key, axis=0, keepdims=True)
    by_key = jnp.where(pairs > 0, key_first + in_key, -1.0)
    by_query = jnp.where(pairs > 0, query_first + in_query, -1.0)
    total = jnp.sum(jnp.sum(pairs, axis=1, keepdims=True), axis=0, keepdims=True)

    lane = fiota((32, 128), 1)
    keys = fiota((32, 128), 0)
    id_col = (iota((32, 128), 0) // 2) * 16 + 2 * j + iota((32, 128), 0) % 2
    zero = jnp.zeros((32, 128), jnp.float32)
    rows = {n: zero for n in range(7)}
    for q in range(16):
        at_key = by_key[:, q : q + 1] == lane
        at_query = by_query[:, q : q + 1] == lane
        rows[KEY] += jnp.where(at_key, keys, 0.0)
        rows[QUERY] += jnp.where(at_key, float(q), 0.0)
        rows[SAME_KEY] += jnp.where(at_key, ones_where(in_key[:, q : q + 1] > 0), 0.0)
        rows[DIAGONAL] += jnp.where(at_key & (id_col == query_id(i, j, q)), 1.0, 0.0)
        rows[PERM] += jnp.where(at_query, by_key[:, q : q + 1], 0.0)
        rows[PERM_KEY] += jnp.where(at_query, keys, 0.0)
        rows[SAME_QUERY] += jnp.where(at_query, ones_where(in_query[:, q : q + 1] > 0), 0.0)
    most = {KEY: 31, QUERY: 15, SAME_KEY: 1, DIAGONAL: 1, PERM: SLOTS - 1, PERM_KEY: 31, SAME_QUERY: 1}
    for n in range(7):
        rows[n] = jnp.sum(rows[n], axis=0, keepdims=True)
        table[n : n + 1, :] = jnp.clip(rows[n].astype(jnp.int32), 0, most[n])
    key_end = jnp.where(key_count > 0, key_first + key_count, 0.0)
    key_end = jnp.sum(jnp.where(keys == lane, key_end, 0.0), axis=0, keepdims=True)
    table[KEY_END : KEY_END + 1, :] = jnp.clip(key_end.astype(jnp.int32), 0, SLOTS)
    query_end = jnp.where(query_count > 0, query_first + query_count, 0.0)
    table[QUERY_END : QUERY_END + 1, 0:16] = jnp.clip(query_end.astype(jnp.int32), 0, SLOTS)
    if table.shape[0] > LISTED:
        table[LISTED : LISTED + 32, 0:16] = pairs.astype(jnp.int32)
        return

    query_row = jnp.where(fiota((1, 128), 1) < total, rows[QUERY], -1.0)
    slot_query[...] = jnp.sum(
        jnp.where(iota((SLOTS, 128), 0) == iota((SLOTS, 128), 1), query_row, 0.0),
        axis=1,
        keepdims=True,
    )


def most_pairs(lists_ref):
    lists = lists_ref[...]
    groups = (lists // 2) % 8
    counts = jnp.zeros((8, 256), jnp.float32)
    group_of = iota((8, 256), 0)
    for n in range(16):
        fresh = jnp.ones((1, 256), jnp.float32)
        for m in range(n):
            fresh = jnp.where(lists[m : m + 1] == lists[n : n + 1], 0.0, fresh)
        counts += jnp.where(groups[n : n + 1] == group_of, fresh, 0.0)
    block = iota((256, 16), 0)
    query_group = (block // 16 % 8) * 2 + (block // 128 + block // 2 % 2) % 2
    member = ones_where(query_group == iota((256, 16), 1))
    return jnp.max(dot(counts, member))


class Refs:
    def __init__(self, names, refs):
        self.__dict__.update(zip(names, refs, strict=True))


def flip(bit):
    return 1 - bit


class Ring:
    def __init__(self, a, p, peer, row, blocks, gather_sems, out, own_in, part_in, part_out, sum_out, sum_in, sum_sems):
        self.a, self.p, self.peer, self.row = a, p, peer, row
        self.blocks, self.gather_sems = blocks, gather_sems
        self.out, self.own_in, self.part_in, self.part_out = out, own_in, part_in, part_out
        self.sum_out, self.sum_in, self.sum_sems = sum_out, sum_in, sum_sems
        self.copies = []

    def at(self, step):
        return (self.p + step + 4) % 4

    def send(self, src, dst, sems, n, peer):
        copy = pltpu.make_async_remote_copy(
            src_ref=src, dst_ref=dst, send_sem=sems[0].at[n], recv_sem=sems[1].at[n],
            device_id=peer, device_id_type=MESH,
        )
        copy.start()
        self.copies.append(copy)
        return copy

    def pass_half(self, n, row, half, peer):
        ref = self.blocks.at[row, half]
        return self.send(ref, ref, self.gather_sems, n, peer)

    def start_own(self):
        own, up, down = self.row(self.a, self.p), self.peer(False, 1), self.peer(False, -1)
        self.gather = {0: self.pass_half(0, own, 0, self.peer(True, 0))}
        self.gather[2] = self.pass_half(2, own, 0, up)
        self.gather[4] = self.pass_half(4, own, 1, down)
        self.gather[1] = self.pass_half(1, own, 1, self.peer(True, 0))
        self.gather[3] = self.pass_half(3, own, 1, up)
        self.gather[5] = self.pass_half(5, own, 0, down)

    def gather_step(self, n):
        self.gather[n].wait_recv()
        up, down = self.peer(False, 1), self.peer(False, -1)
        if n < 2:
            row = self.row(flip(self.a), self.p)
            if n == 0:
                self.gather[8] = self.pass_half(8, row, 0, up)
            else:
                self.gather[10] = self.pass_half(10, row, 1, down)
                self.gather[9] = self.pass_half(9, row, 1, up)
                self.gather[11] = self.pass_half(11, row, 0, down)
            return row, n
        a = self.a if n < 8 else flip(self.a)
        m = (n - 2) % 6
        row = self.row(a, self.at((-1, -1, 1, 1, 2, 2)[m]))
        half = (0, 1, 1, 0, 0, 1)[m]
        if m == 0:
            self.gather[n + 4] = self.pass_half(n + 4, row, half, up)
        if m == 2:
            self.gather[n + 3] = self.pass_half(n + 3, row, half, down)
        return row, half

    def start_part(self, phase):
        a = flip(self.a) if phase == 0 else self.a
        out, sems, n = self.out, self.sum_sems, 6 * phase
        opposite = self.at(2)
        part = [
            self.send(out.at[a, opposite, 0], self.part_in.at[phase, 0], sems, n, self.peer(False, 1)),
            self.send(out.at[a, opposite, 1], self.part_in.at[phase, 1], sems, n + 1, self.peer(False, -1)),
        ]
        return [a, phase, part, [], []]

    def start_plain(self, state):
        a, phase, _, plain, _ = state
        out, sems, n = self.out, self.sum_sems, 6 * phase
        plain += [
            self.send(out.at[a, self.at(1), 1], self.own_in.at[phase, 1], sems, n + 2, self.peer(False, 1)),
            self.send(out.at[a, self.at(-1), 0], self.own_in.at[phase, 0], sems, n + 3, self.peer(False, -1)),
        ]

    def add_part(self, state):
        a, phase, part, _, summed = state
        n = 6 * phase + 4
        for half, step in ((0, 1), (1, -1)):
            part[half].wait_recv()
            both = self.out[a, self.at(step), half].astype(jnp.float32) + self.part_in[phase, half].astype(jnp.float32)
            self.part_out[phase, half] = both.astype(jnp.bfloat16)
            summed.append(
                self.send(
                    self.part_out.at[phase, half], self.own_in.at[phase, 2 + half], self.sum_sems, n + half,
                    self.peer(False, step),
                )
            )

    def total(self, state):
        a, phase, _, plain, summed = state
        for copy in plain + summed:
            copy.wait_recv()
        total = self.out[a, self.p].astype(jnp.float32)
        total += self.own_in[phase, 0:2].astype(jnp.float32)
        return total + self.own_in[phase, 2:4].astype(jnp.float32)

    def send_total(self, total):
        self.sum_out[...] = total.astype(jnp.bfloat16)
        self.across_pair = self.send(self.sum_out, self.sum_in, self.sum_sems, 12, self.peer(True, 0))

    def other_total(self):
        self.across_pair.wait_recv()
        return self.sum_in[...].astype(jnp.float32)


class Refs:
    def __init__(self, names, refs):
        self.__dict__.update(zip(names, refs, strict=True))


def kernel(names, dense, *refs):
    r = Refs(names, refs)
    i, j = lax.axis_index("qblk"), lax.axis_index("kblk")
    core, y, x = i % 2, (i // 2) % 4, i // 8
    h, z = j % 2, j // 2
    scale = 1.0 / math.sqrt(BLOCK)
    kv, qg, table = r.kv, r.qg, r.table

    def key_row(x, y):
        return x * 8 + y * 2 + core

    def query_row(h, z):
        return z * 2 + h

    def key_peer(pair, step):
        return (key_row(flip(x) if pair else x, (y + step + 4) % 4), j)

    def query_peer(pair, step):
        at = (z + step + 4) % 4
        return ((i + 8) % 16, query_row(flip(h), at)) if pair else (i, query_row(h, at))

    sibling = (i + 1 - 2 * core, j)

    loads = []
    for n, (src, dst) in enumerate(
        ((r.k, kv.at[i, 0]), (r.v, kv.at[i, 1]), (r.q, qg.at[j, 0]), (r.g, qg.at[j, 1]))
    ):
        loads.append(pltpu.make_async_copy(src, dst, r.local_sem.at[n]))
        loads[-1].start()

    stat_peers = [query_peer(pair, step) for pair, step in STAT_STEPS]
    peers = [sibling, key_peer(True, 0), key_peer(False, 1), key_peer(False, -1)] + stat_peers
    barrier = pltpu.get_barrier_semaphore()
    for peer in peers:
        pl.semaphore_signal(barrier, inc=1, device_id=peer, device_id_type=MESH)
    pl.semaphore_wait(barrier, len(peers))
    for load in loads:
        load.wait()

    keys = Ring(
        x, y, key_peer, key_row, kv, (r.kv_send, r.kv_recv), r.key_out, r.key_own_in, r.key_part_in,
        r.key_part_out, r.key_sum_out, r.key_sum_in, (r.key_send, r.key_recv),
    )
    queries = Ring(
        h, z, query_peer, query_row, qg, (r.qg_send, r.qg_recv), r.query_out, r.query_own_in, r.query_part_in,
        r.query_part_out, r.query_sum_out, r.query_sum_in, (r.query_send, r.query_recv),
    )
    sib = []

    def to_sibling(row, half):
        ref = kv.at[row, half]
        sib.append(keys.send(ref, ref, (r.sib_send, r.sib_recv), len(sib), sibling))

    def gather_steps(*steps):
        for n in steps:
            to_sibling(*keys.gather_step(n))
            queries.gather_step(n)

    keys.start_own()
    queries.start_own()
    to_sibling(i, 0)
    to_sibling(i, 1)

    list_pairs(i, j, r.lists, r.table_v, None if dense else r.slot_query)
    to_smem = pltpu.make_async_copy(r.table_v, table, r.local_sem.at[4])
    to_smem.start()
    gather_steps(0, 2, 4, 1, 3, 5)

    r.bias[0] = jnp.zeros((BLOCK, BLOCK), jnp.float32)
    r.bias[1] = jnp.where(
        iota((BLOCK, BLOCK), 0) <= iota((BLOCK, BLOCK), 1), 0.0, masked_score
    ).astype(jnp.float32)
    none = 0 if not dense else slice(None)
    r.key_acc[none] = jnp.zeros(r.key_acc[none].shape, jnp.float32)
    r.query_acc[none] = jnp.zeros(r.query_acc[none].shape, jnp.float32)
    if not dense:
        r.flag[0, 0] = most_pairs(r.lists)

    gather_steps(8, 10, 9, 11, 6, 7, 12, 13)
    for copy in sib:
        copy.wait_recv()
    to_smem.wait()

    (dense_stats if dense else slot_stats)(r, i, j, scale)

    st_sems = (r.st_send, r.st_recv)
    st_copies = []
    r.stats[j] = r.stats_out[...]
    for n, peer in enumerate(stat_peers):
        st_copies.append(queries.send(r.stats_out, r.stats.at[j], st_sems, n, peer))
    for copy in st_copies:
        copy.wait_recv()
    logs = r.stats[:, 0]
    best = jnp.max(logs, axis=0)
    offset = best + jnp.log2(jnp.sum(jnp.exp2(logs - best[None]), axis=0))
    delta = jnp.sum(jnp.exp2(logs - offset[None]) * r.stats[:, 1], axis=0)
    for q in range(16):
        r.offsets[q] = offset[q : q + 1, :]
        r.deltas[q] = delta[q : q + 1, :]

    (dense_key_grads if dense else slot_key_grads)(r, i, j, scale)

    def key_part(block):
        return r.key_acc[block if dense else table[KEY_END, block]]

    def query_part(block):
        return r.query_acc[block if dense else table[QUERY_END, block]]

    swaps = []
    for phase, at in ((0, flip(x)), (1, x)):

        def sib_step(n, carry, phase=phase, at=at):
            owner = at * 8 + n * 2 + 1 - core
            for b in range(2):
                r.sib_out[phase, n, :, b] = key_part(owner * 2 + b).astype(jnp.bfloat16)
            return carry

        lax.fori_loop(0, 4, sib_step, 0)
        swaps.append(
            keys.send(r.sib_out.at[phase], r.sib_in.at[phase], (r.sib_send, r.sib_recv), 16 + phase, sibling)
        )

    def key_out(phase, at):
        swaps[phase].wait_recv()

        def step(n, carry):
            owner = at * 8 + n * 2 + core
            for b in range(2):
                both = key_part(owner * 2 + b) + r.sib_in[phase, n, :, b].astype(jnp.float32)
                r.key_out[at, n, :, b] = both.astype(jnp.bfloat16)
            return carry

        lax.fori_loop(0, 4, step, 0)

    def query_out(at):
        def step(n, carry):
            for b in range(2):
                r.query_out[at, n, :, b] = query_part((n * 2 + at) * 2 + b).astype(jnp.bfloat16)
            return carry

        lax.fori_loop(0, 4, step, 0)

    if not dense:
        slot_query_grads(r, 0, SLOTS // 2)
    key_out(0, flip(x))
    key_sums = [keys.start_part(0)]
    keys.start_plain(key_sums[0])
    key_out(1, x)
    key_sums.append(keys.start_part(1))
    if not dense:
        slot_query_grads(r, SLOTS // 2, SLOTS)
    query_out(flip(h))
    query_sums = [queries.start_part(0)]
    queries.start_plain(query_sums[0])
    keys.add_part(key_sums[0])
    keys.start_plain(key_sums[1])
    query_out(h)
    query_sums.append(queries.start_part(1))
    queries.add_part(query_sums[0])
    queries.start_plain(query_sums[1])
    keys.add_part(key_sums[1])
    keys.send_total(keys.total(key_sums[0]))
    queries.add_part(query_sums[1])
    queries.send_total(queries.total(query_sums[0]))
    key_total = keys.total(key_sums[1]) + keys.other_total()
    for b in range(2):
        rows = pl.ds(b * BLOCK, BLOCK)
        r.key_grads[rows, :] = (key_total[0, b] * scale).astype(jnp.bfloat16)
        r.value_grads[rows, :] = key_total[1, b].astype(jnp.bfloat16)
    query_total = queries.total(query_sums[1]) + queries.other_total()
    for b in range(2):
        rows = pl.ds(b * BLOCK, BLOCK)
        r.query_grads[rows, :] = (query_total[0, b] * scale).astype(jnp.bfloat16)
        r.attended[rows, :] = query_total[1, b].astype(jnp.bfloat16)

    for copy in keys.copies + queries.copies:
        copy.wait_send()


def slot_stats(r, i, j, scale):
    kv, qg, table = r.kv, r.qg, r.table

    def step(n, carry):
        for u in range(UNROLL):
            s = n * UNROLL + u
            k, q = table[KEY, s], table[QUERY, s]
            scores = against(kv[k // 2, 0, k % 2], qg[q // 2, 0, q % 2]) * (scale * LOG2E)
            scores += r.bias[table[DIAGONAL, s]]
            prob_grad = against(kv[k // 2, 1, k % 2], qg[q // 2, 1, q % 2])
            top = jnp.max(scores, axis=0, keepdims=True)
            prob = jnp.exp2(scores - top)
            r.probs[s] = prob
            r.prob_grads[s] = prob_grad
            r.tops[pl.ds(s, 1), :] = top
            r.totals[pl.ds(s, 1), :] = jnp.sum(prob, axis=0, keepdims=True)
            r.moments[pl.ds(s, 1), :] = jnp.sum(prob * prob_grad, axis=0, keepdims=True)
        return carry

    lax.fori_loop(0, SLOTS // UNROLL, step, 0)

    top, total, moment, owner = r.tops[...], r.totals[...], r.moments[...], r.slot_query[...]
    for q in range(16):
        mine = owner == float(q)
        top_q = jnp.max(jnp.where(mine, top, masked_score), axis=0, keepdims=True)
        part = jnp.where(mine, jnp.exp2(top - top_q), 0.0)
        total_q = jnp.sum(part * total, axis=0, keepdims=True)
        moment_q = jnp.sum(part * moment, axis=0, keepdims=True)
        put_stats(r, q, top_q, total_q, moment_q)


def put_stats(r, q, top, total, moment):
    some = total > 0
    safe = jnp.where(some, total, 1.0)
    r.stats_out[0, pl.ds(q, 1), :] = jnp.where(some, top + jnp.log2(safe), masked_score)
    r.stats_out[1, pl.ds(q, 1), :] = moment / safe


def slot_key_grads(r, i, j, scale):
    def step(n, carry):
        for u in range(UNROLL):
            s = n * UNROLL + u
            q = r.table[QUERY, s]
            keep = r.table[SAME_KEY, s].astype(jnp.float32)
            prob = r.probs[s] * jnp.exp2(r.tops[pl.ds(s, 1), :] - r.offsets[q])
            weights = prob.astype(jnp.bfloat16)
            score_grad = (prob * (r.prob_grads[s] - r.deltas[q])).astype(jnp.bfloat16)
            r.rounded[s, 0] = score_grad
            r.rounded[s, 1] = weights
            r.key_acc[s + 1, 0] = r.key_acc[s, 0] * keep + dot(score_grad, r.qg[q // 2, 0, q % 2])
            r.key_acc[s + 1, 1] = r.key_acc[s, 1] * keep + dot(weights, r.qg[q // 2, 1, q % 2])
        return carry

    lax.fori_loop(0, SLOTS // UNROLL, step, 0)


def slot_query_grads(r, first, last):
    def step(n, carry):
        for u in range(UNROLL):
            s = first + n * UNROLL + u
            k, at = r.table[PERM_KEY, s], r.table[PERM, s]
            keep = r.table[SAME_QUERY, s].astype(jnp.float32)
            for m in range(2):
                new = across(r.rounded[at, m], r.kv[k // 2, m, k % 2])
                r.query_acc[s + 1, m] = r.query_acc[s, m] * keep + new
        return carry

    lax.fori_loop(0, (last - first) // UNROLL, step, 0)


def dense_tile(r, i, j, scale, q, k):
    scores = against(r.kv[k // 2, 0, k % 2], r.qg[q // 2, 0, q % 2]) * (scale * LOG2E)
    own = (k // 2) * 16 + 2 * j + k % 2 == query_id(i, j, q)
    scores += r.bias[own.astype(jnp.int32)]
    prob_grad = against(r.kv[k // 2, 1, k % 2], r.qg[q // 2, 1, q % 2])
    listed = r.table[LISTED + k, q].astype(jnp.float32)
    return scores + (1.0 - listed) * masked_score, prob_grad, listed


def dense_stats(r, i, j, scale):
    def query_step(q, carry):
        def key_step(k, state):
            top, total, moment = state
            scores, prob_grad, listed = dense_tile(r, i, j, scale, q, k)
            higher = jnp.maximum(top, jnp.max(scores, axis=0, keepdims=True))
            prob = jnp.exp2(scores - higher) * listed
            shrink = jnp.exp2(top - higher)
            total = total * shrink + jnp.sum(prob, axis=0, keepdims=True)
            moment = moment * shrink + jnp.sum(prob * prob_grad, axis=0, keepdims=True)
            return higher, total, moment

        zero = jnp.zeros((1, BLOCK), jnp.float32)
        put_stats(r, q, *lax.fori_loop(0, 32, key_step, (zero + masked_score, zero, zero)))
        return carry

    lax.fori_loop(0, 16, query_step, 0)


def dense_key_grads(r, i, j, scale):
    def step(n, carry):
        q, k = n // 32, n % 32
        scores, prob_grad, listed = dense_tile(r, i, j, scale, q, k)
        prob = jnp.exp2(scores - r.offsets[q]) * listed
        weights = prob.astype(jnp.bfloat16)
        score_grad = (prob * (prob_grad - r.deltas[q])).astype(jnp.bfloat16)
        for m, left in enumerate((score_grad, weights)):
            r.key_acc[k, m] = r.key_acc[k, m] + dot(left, r.qg[q // 2, m, q % 2])
            r.query_acc[q, m] = r.query_acc[q, m] + across(left, r.kv[k // 2, m, k % 2])
        return carry

    lax.fori_loop(0, 16 * 32, step, 0)


def attention(dense, queries, keys, values, grad_out, lists):
    rows, head = queries.shape
    out = jax.ShapeDtypeStruct((rows, head), jnp.bfloat16)
    f32, bf16 = jnp.float32, jnp.bfloat16
    tile = (BLOCK, BLOCK)
    table_rows = LISTED + 32 if dense else LISTED
    dma = pltpu.SemaphoreType.DMA
    any_spec = pl.BlockSpec(memory_space=pl.ANY)
    vmem_spec = pl.BlockSpec(memory_space=pltpu.VMEM)
    smem_spec = pl.BlockSpec(memory_space=pltpu.SMEM)
    scratch = {
        "kv": pltpu.VMEM((16, 2, 2) + tile, bf16),
        "qg": pltpu.VMEM((8, 2, 2) + tile, bf16),
        "table_v": pltpu.VMEM((table_rows, 128), jnp.int32),
        "table": pltpu.SMEM((table_rows, 128), jnp.int32),
        "bias": pltpu.VMEM((2,) + tile, f32),
        "stats_out": pltpu.VMEM((2, 16, 128), f32),
        "stats": pltpu.VMEM((8, 2, 16, 128), f32),
        "offsets": pltpu.VMEM((16, 1, 128), f32),
        "deltas": pltpu.VMEM((16, 1, 128), f32),
        "key_acc": pltpu.VMEM((32 if dense else SLOTS + 1, 2) + tile, f32),
        "query_acc": pltpu.VMEM((16 if dense else SLOTS + 1, 2) + tile, f32),
        "sib_out": pltpu.VMEM((2, 4, 2, 2) + tile, bf16),
        "sib_in": pltpu.VMEM((2, 4, 2, 2) + tile, bf16),
        "local_sem": dma((5,)),
        "kv_send": dma((14,)),
        "kv_recv": dma((14,)),
        "qg_send": dma((14,)),
        "qg_recv": dma((14,)),
        "sib_send": dma((18,)),
        "sib_recv": dma((18,)),
        "st_send": dma((7,)),
        "st_recv": dma((7,)),
    }
    for ring in ("key", "query"):
        scratch |= {
            ring + "_out": pltpu.VMEM((2, 4, 2, 2) + tile, bf16),
            ring + "_own_in": pltpu.VMEM((2, 4, 2) + tile, bf16),
            ring + "_part_in": pltpu.VMEM((2, 2, 2) + tile, bf16),
            ring + "_part_out": pltpu.VMEM((2, 2, 2) + tile, bf16),
            ring + "_sum_out": pltpu.VMEM((2, 2) + tile, bf16),
            ring + "_sum_in": pltpu.VMEM((2, 2) + tile, bf16),
            ring + "_send": dma((13,)),
            ring + "_recv": dma((13,)),
        }
    if not dense:
        scratch |= {
            "slot_query": pltpu.VMEM((SLOTS, 1), f32),
            "probs": pltpu.VMEM((SLOTS,) + tile, f32),
            "prob_grads": pltpu.VMEM((SLOTS,) + tile, f32),
            "tops": pltpu.VMEM((SLOTS, 128), f32),
            "totals": pltpu.VMEM((SLOTS, 128), f32),
            "moments": pltpu.VMEM((SLOTS, 128), f32),
            "rounded": pltpu.VMEM((SLOTS, 2) + tile, bf16),
        }
    outs = ["attended", "query_grads", "key_grads", "value_grads"] + ["flag"] * (not dense)
    out_shape, out_specs = [out] * 4, [vmem_spec] * 4
    if not dense:
        out_shape.append(jax.ShapeDtypeStruct((1, 1), f32))
        out_specs.append(smem_spec)
    return pl.pallas_call(
        functools.partial(kernel, ["q", "k", "v", "g", "lists"] + outs + list(scratch), dense),
        out_shape=out_shape,
        in_specs=[any_spec] * 4 + [vmem_spec],
        out_specs=out_specs,
        scratch_shapes=list(scratch.values()),
        compiler_params=pltpu.CompilerParams(
            collective_id=1 if dense else 0, has_side_effects=True, vmem_limit_bytes=56 << 20
        ),
        name="dense_attention" if dense else "block_sparse_attention",
    )(*(a.reshape(2, BLOCK, BLOCK) for a in (queries, keys, values, grad_out)), lists)


def hand_out_kernel(*refs):
    sems = refs[-1]
    copies = [pltpu.make_async_copy(refs[n], refs[4 + n], sems.at[n]) for n in range(4)]
    for copy in copies:
        copy.start()
    for copy in copies:
        copy.wait()


def hand_out(outs):
    spec = pl.BlockSpec(memory_space=pl.ANY)
    return tuple(
        pl.pallas_call(
            hand_out_kernel,
            out_shape=[jax.ShapeDtypeStruct(out.shape, out.dtype) for out in outs],
            in_specs=[spec] * 4,
            out_specs=[spec] * 4,
            scratch_shapes=[pltpu.SemaphoreType.DMA((4,))],
            name="hand_out",
        )(*outs)
    )


def per_device(queries, keys, values, grad_out, key_blocks):
    args = (queries, keys, values, grad_out, key_blocks.T)
    *outs, most = attention(False, *args)
    return lax.cond(
        most[0, 0] > SLOTS,
        lambda: hand_out(attention(True, *args)),
        lambda: hand_out(outs),
    )


def solution(mesh):
    split = P(("qblk", "kblk"), None)
    return jax.shard_map(
        per_device,
        mesh=mesh,
        in_specs=(split, split, split, split, P()),
        out_specs=(split, split, split, split),
        check_vma=False,
    )
```

```python
import functools
import math

import jax
import jax.numpy as jnp
from jax import lax
from jax.experimental import pallas as pl
from jax.experimental.pallas import tpu as pltpu
from jax.sharding import PartitionSpec as P

BLOCK = 128
SLOTS = 56
UNROLL = 28
MESH = pl.DeviceIdType.MESH

masked_score = -1e30
LOG2E = 1.4426950408889634


def against(left, right):
    return lax.dot_general(
        left, right, (((1,), (1,)), ((), ())), preferred_element_type=jnp.float32
    )


def across(left, right):
    return lax.dot_general(
        left, right, (((0,), (0,)), ((), ())), preferred_element_type=jnp.float32
    )


def dot(left, right):
    return jnp.dot(left, right, preferred_element_type=jnp.float32)


KEY, QUERY, SAME_KEY, DIAGONAL, PERM, PERM_KEY, PERM_QUERY, SAME_QUERY, KEY_END, QUERY_END = range(10)
LISTED = 16

STAT_STEPS = ((False, 1), (False, -1), (True, 0), (False, 2), (True, 1), (True, -1), (True, 2))


def iota(shape, dim):
    return lax.broadcasted_iota(jnp.int32, shape, dim)


def fiota(shape, dim):
    return iota(shape, dim).astype(jnp.float32)


def ones_where(cond):
    return jnp.where(cond, 1.0, 0.0).astype(jnp.float32)


def query_id(i, j, q):
    x = (i // 8 + j % 2 + (q // 2) % 2) % 2
    return (x * 8 + i % 8) * 16 + q


def list_pairs(i, j, lists_ref, table, slot_query):
    lists = lists_ref[...].astype(jnp.float32)
    chosen = ones_where(iota((256, 16), 0) == query_id(i, j, iota((256, 16), 1)))
    own = dot(lists, chosen)
    key_ids = ((iota((32, 16), 0) // 2) * 16 + 2 * j + iota((32, 16), 0) % 2).astype(jnp.float32)
    pairs = jnp.zeros((32, 16), jnp.float32)
    for n in range(16):
        pairs = jnp.maximum(pairs, ones_where(own[n : n + 1, :] == key_ids))
    earlier_query = ones_where(iota((16, 16), 0) < iota((16, 16), 1))
    earlier_key = ones_where(iota((32, 32), 1) < iota((32, 32), 0))
    in_key = dot(pairs, earlier_query)
    in_query = dot(earlier_key, pairs)
    key_count = jnp.sum(pairs, axis=1, keepdims=True)
    query_count = jnp.sum(pairs, axis=0, keepdims=True)
    key_first = jnp.sum(in_query, axis=1, keepdims=True)
    query_first = jnp.sum(in_key, axis=0, keepdims=True)
    by_key = jnp.where(pairs > 0, key_first + in_key, -1.0)
    by_query = jnp.where(pairs > 0, query_first + in_query, -1.0)
    total = jnp.sum(jnp.sum(pairs, axis=1, keepdims=True), axis=0, keepdims=True)

    lane = fiota((32, 128), 1)
    keys = fiota((32, 128), 0)
    id_col = (iota((32, 128), 0) // 2) * 16 + 2 * j + iota((32, 128), 0) % 2
    zero = jnp.zeros((32, 128), jnp.float32)
    rows = {n: zero for n in range(8)}
    for q in range(16):
        at_key = by_key[:, q : q + 1] == lane
        at_query = by_query[:, q : q + 1] == lane
        rows[KEY] += jnp.where(at_key, keys, 0.0)
        rows[QUERY] += jnp.where(at_key, float(q), 0.0)
        rows[SAME_KEY] += jnp.where(at_key, ones_where(in_key[:, q : q + 1] > 0), 0.0)
        rows[DIAGONAL] += jnp.where(at_key & (id_col == query_id(i, j, q)), 1.0, 0.0)
        rows[PERM] += jnp.where(at_query, by_key[:, q : q + 1], 0.0)
        rows[PERM_KEY] += jnp.where(at_query, keys, 0.0)
        rows[PERM_QUERY] += jnp.where(at_query, float(q), 0.0)
        rows[SAME_QUERY] += jnp.where(at_query, ones_where(in_query[:, q : q + 1] > 0), 0.0)
    most = {KEY: 31, QUERY: 15, SAME_KEY: 1, DIAGONAL: 1}
    most |= {PERM: SLOTS - 1, PERM_KEY: 31, PERM_QUERY: 15, SAME_QUERY: 1}
    for n in range(8):
        rows[n] = jnp.sum(rows[n], axis=0, keepdims=True)
        table[n : n + 1, :] = jnp.clip(rows[n].astype(jnp.int32), 0, most[n])
    key_end = jnp.where(key_count > 0, key_first + key_count, 0.0)
    key_end = jnp.sum(jnp.where(keys == lane, key_end, 0.0), axis=0, keepdims=True)
    table[KEY_END : KEY_END + 1, :] = jnp.clip(key_end.astype(jnp.int32), 0, SLOTS)
    query_end = jnp.where(query_count > 0, query_first + query_count, 0.0)
    table[QUERY_END : QUERY_END + 1, 0:16] = jnp.clip(query_end.astype(jnp.int32), 0, SLOTS)
    if table.shape[0] > LISTED:
        table[LISTED : LISTED + 32, 0:16] = pairs.astype(jnp.int32)
        return

    query_row = jnp.where(fiota((1, 128), 1) < total, rows[QUERY], -1.0)
    slot_query[...] = jnp.sum(
        jnp.where(iota((SLOTS, 128), 0) == iota((SLOTS, 128), 1), query_row, 0.0),
        axis=1,
        keepdims=True,
    )


def most_pairs(lists_ref):
    lists = lists_ref[...]
    groups = (lists // 2) % 8
    counts = jnp.zeros((8, 256), jnp.float32)
    group_of = iota((8, 256), 0)
    for n in range(16):
        fresh = jnp.ones((1, 256), jnp.float32)
        for m in range(n):
            fresh = jnp.where(lists[m : m + 1] == lists[n : n + 1], 0.0, fresh)
        counts += jnp.where(groups[n : n + 1] == group_of, fresh, 0.0)
    block = iota((256, 16), 0)
    query_group = (block // 16 % 8) * 2 + (block // 128 + block // 2 % 2) % 2
    member = ones_where(query_group == iota((256, 16), 1))
    return jnp.max(dot(counts, member))


class Refs:
    def __init__(self, names, refs):
        self.__dict__.update(zip(names, refs, strict=True))


def flip(bit):
    return 1 - bit


class Ring:
    def __init__(self, a, p, peer, row, blocks, gather_sems, out, own_in, part_in, part_out, sum_out, sum_in, sum_sems):
        self.a, self.p, self.peer, self.row = a, p, peer, row
        self.blocks, self.gather_sems = blocks, gather_sems
        self.out, self.own_in, self.part_in, self.part_out = out, own_in, part_in, part_out
        self.sum_out, self.sum_in, self.sum_sems = sum_out, sum_in, sum_sems
        self.copies, self.waited = [], 0

    def at(self, step):
        return (self.p + step + 4) % 4

    def send(self, src, dst, sems, n, peer):
        copy = pltpu.make_async_remote_copy(
            src_ref=src, dst_ref=dst, send_sem=sems[0].at[n], recv_sem=sems[1].at[n],
            device_id=peer, device_id_type=MESH,
        )
        copy.start()
        self.copies.append(copy)
        return copy

    def pass_half(self, n, row, half, peer):
        ref = self.blocks.at[row, half]
        return self.send(ref, ref, self.gather_sems, n, peer)

    def start_own(self):
        own, up, down = self.row(self.a, self.p), self.peer(False, 1), self.peer(False, -1)
        self.gather = {0: self.pass_half(0, own, 0, self.peer(True, 0))}
        self.gather[2] = self.pass_half(2, own, 0, up)
        self.gather[4] = self.pass_half(4, own, 1, down)
        self.gather[1] = self.pass_half(1, own, 1, self.peer(True, 0))
        self.gather[3] = self.pass_half(3, own, 1, up)
        self.gather[5] = self.pass_half(5, own, 0, down)

    def gather_step(self, n):
        self.gather[n].wait_recv()
        up, down = self.peer(False, 1), self.peer(False, -1)
        if n < 2:
            row = self.row(flip(self.a), self.p)
            if n == 0:
                self.gather[8] = self.pass_half(8, row, 0, up)
            else:
                self.gather[10] = self.pass_half(10, row, 1, down)
                self.gather[9] = self.pass_half(9, row, 1, up)
                self.gather[11] = self.pass_half(11, row, 0, down)
            return row, n
        a = self.a if n < 8 else flip(self.a)
        m = (n - 2) % 6
        row = self.row(a, self.at((-1, -1, 1, 1, 2, 2)[m]))
        half = (0, 1, 1, 0, 0, 1)[m]
        if m == 0:
            self.gather[n + 4] = self.pass_half(n + 4, row, half, up)
        if m == 2:
            self.gather[n + 3] = self.pass_half(n + 3, row, half, down)
        return row, half

    def start_part(self, phase):
        a = flip(self.a) if phase == 0 else self.a
        out, sems, n = self.out, self.sum_sems, 6 * phase
        opposite = self.at(2)
        part = [
            self.send(out.at[a, opposite, 0], self.part_in.at[phase, 0], sems, n, self.peer(False, 1)),
            self.send(out.at[a, opposite, 1], self.part_in.at[phase, 1], sems, n + 1, self.peer(False, -1)),
        ]
        return [a, phase, part, [], []]

    def start_plain(self, state):
        a, phase, _, plain, _ = state
        out, sems, n = self.out, self.sum_sems, 6 * phase
        plain += [
            self.send(out.at[a, self.at(1), 1], self.own_in.at[phase, 1], sems, n + 2, self.peer(False, 1)),
            self.send(out.at[a, self.at(-1), 0], self.own_in.at[phase, 0], sems, n + 3, self.peer(False, -1)),
        ]

    def add_part(self, state):
        a, phase, part, _, summed = state
        n = 6 * phase + 4
        for half, step in ((0, 1), (1, -1)):
            part[half].wait_recv()
            both = self.out[a, self.at(step), half].astype(jnp.float32) + self.part_in[phase, half].astype(jnp.float32)
            self.part_out[phase, half] = both.astype(jnp.bfloat16)
            summed.append(
                self.send(
                    self.part_out.at[phase, half], self.own_in.at[phase, 2 + half], self.sum_sems, n + half,
                    self.peer(False, step),
                )
            )

    def total(self, state):
        a, phase, _, plain, summed = state
        for copy in plain + summed:
            copy.wait_recv()
        total = self.out[a, self.p].astype(jnp.float32)
        total += self.own_in[phase, 0:2].astype(jnp.float32)
        return total + self.own_in[phase, 2:4].astype(jnp.float32)

    def send_total(self, total):
        self.sum_out[...] = total.astype(jnp.bfloat16)
        self.across_pair = self.send(self.sum_out, self.sum_in, self.sum_sems, 12, self.peer(True, 0))

    def other_total(self):
        self.across_pair.wait_recv()
        return self.sum_in[...].astype(jnp.float32)


class Refs:
    def __init__(self, names, refs):
        self.__dict__.update(zip(names, refs, strict=True))


def kernel(names, dense, *refs):
    r = Refs(names, refs)
    i, j = lax.axis_index("qblk"), lax.axis_index("kblk")
    core, y, x = i % 2, (i // 2) % 4, i // 8
    h, z = j % 2, j // 2
    scale = 1.0 / math.sqrt(BLOCK)
    kv, qg, table = r.kv, r.qg, r.table

    def key_row(x, y):
        return x * 8 + y * 2 + core

    def query_row(h, z):
        return z * 2 + h

    def key_peer(pair, step):
        return (key_row(flip(x) if pair else x, (y + step + 4) % 4), j)

    def query_peer(pair, step):
        at = (z + step + 4) % 4
        return ((i + 8) % 16, query_row(flip(h), at)) if pair else (i, query_row(h, at))

    sibling = (i + 1 - 2 * core, j)

    loads = []
    for n, (src, dst) in enumerate(
        ((r.k, kv.at[i, 0]), (r.q, qg.at[j, 0]), (r.v, kv.at[i, 1]), (r.g, qg.at[j, 1]), (r.lists, r.lists_v))
    ):
        loads.append(pltpu.make_async_copy(src, dst, r.local_sem.at[n]))
        loads[-1].start()

    stat_peers = [query_peer(pair, step) for pair, step in STAT_STEPS]
    peers = [sibling, key_peer(True, 0), key_peer(False, 1), key_peer(False, -1)] + stat_peers[:3]
    barrier = pltpu.get_barrier_semaphore()
    for peer in peers:
        pl.semaphore_signal(barrier, inc=1, device_id=peer, device_id_type=MESH)
    pl.semaphore_wait(barrier, len(peers))
    for load in loads[:4]:
        load.wait()

    keys = Ring(
        x, y, key_peer, key_row, kv, (r.kv_send, r.kv_recv), r.key_out, r.key_own_in, r.key_part_in,
        r.key_part_out, r.key_sum_out, r.key_sum_in, (r.key_send, r.key_recv),
    )
    queries = Ring(
        h, z, query_peer, query_row, qg, (r.qg_send, r.qg_recv), r.query_out, r.query_own_in, r.query_part_in,
        r.query_part_out, r.query_sum_out, r.query_sum_in, (r.query_send, r.query_recv),
    )
    sib = []

    def to_sibling(row, half):
        ref = kv.at[row, half]
        sib.append(keys.send(ref, ref, (r.sib_send, r.sib_recv), len(sib), sibling))

    def gather_steps(*steps):
        for n in steps:
            to_sibling(*keys.gather_step(n))
            queries.gather_step(n)

    keys.start_own()
    queries.start_own()
    to_sibling(i, 0)
    to_sibling(i, 1)

    loads[4].wait()
    list_pairs(i, j, r.lists_v, r.table_v, None if dense else r.slot_query)
    to_smem = pltpu.make_async_copy(r.table_v, table, r.local_sem.at[5])
    to_smem.start()
    gather_steps(0, 2, 4, 1, 3, 5)

    r.bias[0] = jnp.zeros((BLOCK, BLOCK), jnp.float32)
    r.bias[1] = jnp.where(
        iota((BLOCK, BLOCK), 0) <= iota((BLOCK, BLOCK), 1), 0.0, masked_score
    ).astype(jnp.float32)
    none = 0 if not dense else slice(None)
    r.key_acc[none] = jnp.zeros(r.key_acc[none].shape, jnp.float32)
    r.query_acc[none] = jnp.zeros(r.query_acc[none].shape, jnp.float32)
    if not dense:
        r.flag[0, 0] = most_pairs(r.lists_v)

    gather_steps(8, 10, 9, 11, 6, 7, 12, 13)
    for copy in sib:
        copy.wait_recv()
    to_smem.wait()

    (dense_stats if dense else slot_stats)(r, i, j, scale)

    st_sems = (r.st_send, r.st_recv)
    st_copies = []
    r.stats[j] = r.stats_out[...]
    for n, peer in enumerate(stat_peers):
        st_copies.append(queries.send(r.stats_out, r.stats.at[j], st_sems, n, peer))
    for ring in (keys, queries):
        for copy in ring.copies[: -len(st_copies) if ring is queries else None]:
            copy.wait_send()
            ring.waited += 1
    if not dense:
        slot_query_grads(r)
    for copy in st_copies:
        copy.wait_recv()
    logs = r.stats[:, 0]
    best = jnp.max(logs, axis=0)
    offset = best + jnp.log2(jnp.sum(jnp.exp2(logs - best[None]), axis=0))
    delta = jnp.sum(jnp.exp2(logs - offset[None]) * r.stats[:, 1], axis=0)
    for q in range(16):
        r.offsets[q] = offset[q : q + 1, :]
        r.deltas[q] = delta[q : q + 1, :]
    if not dense:
        scales = jnp.exp2(r.stats_out[0] - offset)
        r.columns[...] = jnp.transpose(jnp.concatenate([scales, delta - r.stats_out[1]], axis=0))

    (dense_key_grads if dense else slot_key_grads)(r, i, j, scale)

    def key_part(block):
        return r.key_acc[block if dense else table[KEY_END, block]]

    def query_part(q):
        if dense:
            return r.query_acc[q]
        sums = r.query_acc[table[QUERY_END, q]]
        own = r.columns[:, q : q + 1]
        shift = r.columns[:, 16 + q : 17 + q]
        return jnp.stack([own * (sums[0] - shift * sums[1]), own * sums[2]])

    swaps = []
    for phase, at in ((0, flip(x)), (1, x)):

        def sib_step(n, carry, phase=phase, at=at):
            owner = at * 8 + n * 2 + 1 - core
            for b in range(2):
                r.sib_out[phase, n, :, b] = key_part(owner * 2 + b).astype(jnp.bfloat16)
            return carry

        lax.fori_loop(0, 4, sib_step, 0)
        swaps.append(
            keys.send(r.sib_out.at[phase], r.sib_in.at[phase], (r.sib_send, r.sib_recv), 16 + phase, sibling)
        )

    def key_out(phase, at):
        swaps[phase].wait_recv()

        def step(n, carry):
            owner = at * 8 + n * 2 + core
            for b in range(2):
                both = key_part(owner * 2 + b) + r.sib_in[phase, n, :, b].astype(jnp.float32)
                r.key_out[at, n, :, b] = both.astype(jnp.bfloat16)
            return carry

        lax.fori_loop(0, 4, step, 0)

    def query_out(phase):
        for n in range(4):
            for b in range(2):
                for at in range(2):

                    @pl.when(at == (flip(h) if phase == 0 else h))
                    def _(n=n, b=b, at=at):
                        r.query_out[at, n, :, b] = query_part((n * 2 + at) * 2 + b).astype(jnp.bfloat16)

    query_out(0)
    query_sums = [queries.start_part(0)]
    queries.start_plain(query_sums[0])
    key_out(0, flip(x))
    key_sums = [keys.start_part(0)]
    keys.start_plain(key_sums[0])
    query_out(1)
    query_sums.append(queries.start_part(1))
    key_out(1, x)
    key_sums.append(keys.start_part(1))
    queries.add_part(query_sums[0])
    queries.start_plain(query_sums[1])
    keys.add_part(key_sums[0])
    keys.start_plain(key_sums[1])
    queries.add_part(query_sums[1])
    keys.add_part(key_sums[1])
    queries.send_total(queries.total(query_sums[0]))
    keys.send_total(keys.total(key_sums[0]))
    results = []

    def finish(n, sums, factors, outs):
        for m in range(2):
            for b in range(2):
                rows = pl.ds(b * BLOCK, BLOCK)
                r.finals[n + m, rows, :] = (sums[m, b] * factors[m]).astype(jnp.bfloat16)
            results.append(pltpu.make_async_copy(r.finals.at[n + m], outs[m], r.local_sem.at[6 + n + m]))
            results[-1].start()

    finish(0, queries.total(query_sums[1]) + queries.other_total(), (scale, 1.0), (r.query_grads, r.attended))
    finish(2, keys.total(key_sums[1]) + keys.other_total(), (scale, 1.0), (r.key_grads, r.value_grads))
    for ring in (keys, queries):
        for copy in ring.copies[ring.waited :]:
            copy.wait_send()
    for result in results:
        result.wait()


def slot_stats(r, i, j, scale):
    kv, qg, table = r.kv, r.qg, r.table

    def step(n, carry):
        for u in range(UNROLL):
            s = n * UNROLL + u
            k, q = table[KEY, s], table[QUERY, s]
            scores = against(kv[k // 2, 0, k % 2], qg[q // 2, 0, q % 2]) * (scale * LOG2E)
            scores += r.bias[table[DIAGONAL, s]]
            prob_grad = against(kv[k // 2, 1, k % 2], qg[q // 2, 1, q % 2])
            top = jnp.max(scores, axis=0, keepdims=True)
            prob = jnp.exp2(scores - top)
            r.probs[s] = prob
            r.prob_grads[s] = prob_grad
            r.tops[pl.ds(s, 1), :] = top
            r.totals[pl.ds(s, 1), :] = jnp.sum(prob, axis=0, keepdims=True)
            r.moments[pl.ds(s, 1), :] = jnp.sum(prob * prob_grad, axis=0, keepdims=True)
        return carry

    lax.fori_loop(0, SLOTS // UNROLL, step, 0)

    top, total, moment, owner = r.tops[...], r.totals[...], r.moments[...], r.slot_query[...]
    for q in range(16):
        mine = owner == float(q)
        top_q = jnp.max(jnp.where(mine, top, masked_score), axis=0, keepdims=True)
        part = jnp.where(mine, jnp.exp2(top - top_q), 0.0)
        total_q = jnp.sum(part * total, axis=0, keepdims=True)
        moment_q = jnp.sum(part * moment, axis=0, keepdims=True)
        put_stats(r, q, top_q, total_q, moment_q)


def put_stats(r, q, top, total, moment):
    some = total > 0
    safe = jnp.where(some, total, 1.0)
    log, mean = jnp.where(some, top + jnp.log2(safe), masked_score), moment / safe
    r.stats_out[0, pl.ds(q, 1), :] = log
    r.stats_out[1, pl.ds(q, 1), :] = mean
    r.own_logs[q] = log
    r.own_means[q] = mean


def slot_key_grads(r, i, j, scale):
    def step(n, carry):
        for u in range(UNROLL):
            s = n * UNROLL + u
            q = r.table[QUERY, s]
            keep = r.table[SAME_KEY, s].astype(jnp.float32)
            prob = r.probs[s] * jnp.exp2(r.tops[pl.ds(s, 1), :] - r.offsets[q])
            weights = prob.astype(jnp.bfloat16)
            score_grad = (prob * (r.prob_grads[s] - r.deltas[q])).astype(jnp.bfloat16)
            r.key_acc[s + 1, 0] = r.key_acc[s, 0] * keep + dot(score_grad, r.qg[q // 2, 0, q % 2])
            r.key_acc[s + 1, 1] = r.key_acc[s, 1] * keep + dot(weights, r.qg[q // 2, 1, q % 2])
        return carry

    lax.fori_loop(0, SLOTS // UNROLL, step, 0)


def slot_query_grads(r):
    def step(n, carry):
        for u in range(UNROLL):
            s = n * UNROLL + u
            k, q, at = r.table[PERM_KEY, s], r.table[PERM_QUERY, s], r.table[PERM, s]
            keep = r.table[SAME_QUERY, s].astype(jnp.float32)
            prob = r.probs[at] * jnp.exp2(r.tops[pl.ds(at, 1), :] - r.own_logs[q])
            weights = prob.astype(jnp.bfloat16)
            score_grad = (prob * (r.prob_grads[at] - r.own_means[q])).astype(jnp.bfloat16)
            keys, values = r.kv[k // 2, 0, k % 2], r.kv[k // 2, 1, k % 2]
            r.query_acc[s + 1, 0] = r.query_acc[s, 0] * keep + across(score_grad, keys)
            r.query_acc[s + 1, 1] = r.query_acc[s, 1] * keep + across(weights, keys)
            r.query_acc[s + 1, 2] = r.query_acc[s, 2] * keep + across(weights, values)
        return carry

    lax.fori_loop(0, SLOTS // UNROLL, step, 0)


def dense_tile(r, i, j, scale, q, k):
    scores = against(r.kv[k // 2, 0, k % 2], r.qg[q // 2, 0, q % 2]) * (scale * LOG2E)
    own = (k // 2) * 16 + 2 * j + k % 2 == query_id(i, j, q)
    scores += r.bias[own.astype(jnp.int32)]
    prob_grad = against(r.kv[k // 2, 1, k % 2], r.qg[q // 2, 1, q % 2])
    listed = r.table[LISTED + k, q].astype(jnp.float32)
    return scores + (1.0 - listed) * masked_score, prob_grad, listed


def dense_stats(r, i, j, scale):
    def query_step(q, carry):
        def key_step(k, state):
            top, total, moment = state
            scores, prob_grad, listed = dense_tile(r, i, j, scale, q, k)
            higher = jnp.maximum(top, jnp.max(scores, axis=0, keepdims=True))
            prob = jnp.exp2(scores - higher) * listed
            shrink = jnp.exp2(top - higher)
            total = total * shrink + jnp.sum(prob, axis=0, keepdims=True)
            moment = moment * shrink + jnp.sum(prob * prob_grad, axis=0, keepdims=True)
            return higher, total, moment

        zero = jnp.zeros((1, BLOCK), jnp.float32)
        put_stats(r, q, *lax.fori_loop(0, 32, key_step, (zero + masked_score, zero, zero)))
        return carry

    lax.fori_loop(0, 16, query_step, 0)


def dense_key_grads(r, i, j, scale):
    def step(n, carry):
        q, k = n // 32, n % 32
        scores, prob_grad, listed = dense_tile(r, i, j, scale, q, k)
        prob = jnp.exp2(scores - r.offsets[q]) * listed
        weights = prob.astype(jnp.bfloat16)
        score_grad = (prob * (prob_grad - r.deltas[q])).astype(jnp.bfloat16)
        for m, left in enumerate((score_grad, weights)):
            r.key_acc[k, m] = r.key_acc[k, m] + dot(left, r.qg[q // 2, m, q % 2])
            r.query_acc[q, m] = r.query_acc[q, m] + across(left, r.kv[k // 2, m, k % 2])
        return carry

    lax.fori_loop(0, 16 * 32, step, 0)


def attention(dense, queries, keys, values, grad_out, lists):
    rows, head = queries.shape
    out = jax.ShapeDtypeStruct((rows, head), jnp.bfloat16)
    f32, bf16 = jnp.float32, jnp.bfloat16
    tile = (BLOCK, BLOCK)
    table_rows = LISTED + 32 if dense else LISTED
    dma = pltpu.SemaphoreType.DMA
    any_spec = pl.BlockSpec(memory_space=pl.ANY)
    smem_spec = pl.BlockSpec(memory_space=pltpu.SMEM)
    scratch = {
        "kv": pltpu.VMEM((16, 2, 2) + tile, bf16),
        "qg": pltpu.VMEM((8, 2, 2) + tile, bf16),
        "table_v": pltpu.VMEM((table_rows, 128), jnp.int32),
        "table": pltpu.SMEM((table_rows, 128), jnp.int32),
        "bias": pltpu.VMEM((2,) + tile, f32),
        "stats_out": pltpu.VMEM((2, 16, 128), f32),
        "stats": pltpu.VMEM((8, 2, 16, 128), f32),
        "offsets": pltpu.VMEM((16, 1, 128), f32),
        "deltas": pltpu.VMEM((16, 1, 128), f32),
        "key_acc": pltpu.VMEM((32 if dense else SLOTS + 1, 2) + tile, f32),
        "query_acc": pltpu.VMEM(((16, 2) if dense else (SLOTS + 1, 3)) + tile, f32),
        "own_logs": pltpu.VMEM((16, 1, 128), f32),
        "own_means": pltpu.VMEM((16, 1, 128), f32),
        "sib_out": pltpu.VMEM((2, 4, 2, 2) + tile, bf16),
        "sib_in": pltpu.VMEM((2, 4, 2, 2) + tile, bf16),
        "lists_v": pltpu.VMEM((16, 256), jnp.int32),
        "finals": pltpu.VMEM((4, 2 * BLOCK, BLOCK), bf16),
        "local_sem": dma((10,)),
        "kv_send": dma((14,)),
        "kv_recv": dma((14,)),
        "qg_send": dma((14,)),
        "qg_recv": dma((14,)),
        "sib_send": dma((18,)),
        "sib_recv": dma((18,)),
        "st_send": dma((7,)),
        "st_recv": dma((7,)),
    }
    for ring in ("key", "query"):
        scratch |= {
            ring + "_out": pltpu.VMEM((2, 4, 2, 2) + tile, bf16),
            ring + "_own_in": pltpu.VMEM((2, 4, 2) + tile, bf16),
            ring + "_part_in": pltpu.VMEM((2, 2, 2) + tile, bf16),
            ring + "_part_out": pltpu.VMEM((2, 2, 2) + tile, bf16),
            ring + "_sum_out": pltpu.VMEM((2, 2) + tile, bf16),
            ring + "_sum_in": pltpu.VMEM((2, 2) + tile, bf16),
            ring + "_send": dma((13,)),
            ring + "_recv": dma((13,)),
        }
    if not dense:
        scratch |= {
            "slot_query": pltpu.VMEM((SLOTS, 1), f32),
            "probs": pltpu.VMEM((SLOTS,) + tile, f32),
            "prob_grads": pltpu.VMEM((SLOTS,) + tile, f32),
            "tops": pltpu.VMEM((SLOTS, 128), f32),
            "totals": pltpu.VMEM((SLOTS, 128), f32),
            "moments": pltpu.VMEM((SLOTS, 128), f32),
            "columns": pltpu.VMEM((BLOCK, 32), f32),
        }
    outs = ["attended", "query_grads", "key_grads", "value_grads"] + ["flag"] * (not dense)
    out_shape, out_specs = [out] * 4, [any_spec] * 4
    if not dense:
        out_shape.append(jax.ShapeDtypeStruct((1, 1), f32))
        out_specs.append(smem_spec)
    return pl.pallas_call(
        functools.partial(kernel, ["q", "k", "v", "g", "lists"] + outs + list(scratch), dense),
        out_shape=out_shape,
        in_specs=[any_spec] * 5,
        out_specs=out_specs,
        scratch_shapes=list(scratch.values()),
        compiler_params=pltpu.CompilerParams(
            collective_id=1 if dense else 0, has_side_effects=True, vmem_limit_bytes=56 << 20
        ),
        name="dense_attention" if dense else "block_sparse_attention",
    )(*(a.reshape(2, BLOCK, BLOCK) for a in (queries, keys, values, grad_out)), lists)


def hand_out_kernel(*refs):
    sems = refs[-1]
    copies = [pltpu.make_async_copy(refs[n], refs[4 + n], sems.at[n]) for n in range(4)]
    for copy in copies:
        copy.start()
    for copy in copies:
        copy.wait()


def hand_out(outs):
    spec = pl.BlockSpec(memory_space=pl.ANY)
    return tuple(
        pl.pallas_call(
            hand_out_kernel,
            out_shape=[jax.ShapeDtypeStruct(out.shape, out.dtype) for out in outs],
            in_specs=[spec] * 4,
            out_specs=[spec] * 4,
            scratch_shapes=[pltpu.SemaphoreType.DMA((4,))],
            name="hand_out",
        )(*outs)
    )


def per_device(queries, keys, values, grad_out, key_blocks):
    args = (queries, keys, values, grad_out, key_blocks.T)
    *outs, most = attention(False, *args)
    return lax.cond(
        most[0, 0] > SLOTS,
        lambda: hand_out(attention(True, *args)),
        lambda: hand_out(outs),
    )


def solution(mesh):
    split = P(("qblk", "kblk"), None)
    return jax.shard_map(
        per_device,
        mesh=mesh,
        in_specs=(split, split, split, split, P()),
        out_specs=(split, split, split, split),
        check_vma=False,
    )
```

```python
import functools
import math

import jax
import jax.numpy as jnp
from jax import lax
from jax.experimental import pallas as pl
from jax.experimental.pallas import tpu as pltpu
from jax.sharding import PartitionSpec as P

BLOCK = 128
SLOTS = 56
UNROLL = 28
MESH = pl.DeviceIdType.MESH

masked_score = -1e30
LOG2E = 1.4426950408889634


def against(left, right):
    return lax.dot_general(
        left, right, (((1,), (1,)), ((), ())), preferred_element_type=jnp.float32
    )


def across(left, right):
    return lax.dot_general(
        left, right, (((0,), (0,)), ((), ())), preferred_element_type=jnp.float32
    )


def dot(left, right):
    return jnp.dot(left, right, preferred_element_type=jnp.float32)


KEY, QUERY, SAME_KEY, DIAGONAL, PERM, PERM_KEY, PERM_QUERY, SAME_QUERY, KEY_END, QUERY_END = range(10)
LISTED = 16

STAT_STEPS = ((False, 1), (False, -1), (True, 0), (False, 2), (True, 1), (True, -1), (True, 2))


def iota(shape, dim):
    return lax.broadcasted_iota(jnp.int32, shape, dim)


def fiota(shape, dim):
    return iota(shape, dim).astype(jnp.float32)


def ones_where(cond):
    return jnp.where(cond, 1.0, 0.0).astype(jnp.float32)


def query_id(i, j, q):
    x = (i // 8 + j % 2 + (q // 2) % 2) % 2
    return (x * 8 + i % 8) * 16 + q


def list_pairs(i, j, lists_ref, table, slot_query):
    lists = lists_ref[...].astype(jnp.float32)
    chosen = ones_where(iota((256, 16), 0) == query_id(i, j, iota((256, 16), 1)))
    own = dot(lists, chosen)
    key_ids = ((iota((32, 16), 0) // 2) * 16 + 2 * j + iota((32, 16), 0) % 2).astype(jnp.float32)
    pairs = jnp.zeros((32, 16), jnp.float32)
    for n in range(16):
        pairs = jnp.maximum(pairs, ones_where(own[n : n + 1, :] == key_ids))
    earlier_query = ones_where(iota((16, 16), 0) < iota((16, 16), 1))
    earlier_key = ones_where(iota((32, 32), 1) < iota((32, 32), 0))
    in_key = dot(pairs, earlier_query)
    in_query = dot(earlier_key, pairs)
    key_count = jnp.sum(pairs, axis=1, keepdims=True)
    query_count = jnp.sum(pairs, axis=0, keepdims=True)
    key_first = jnp.sum(in_query, axis=1, keepdims=True)
    query_first = jnp.sum(in_key, axis=0, keepdims=True)
    by_key = jnp.where(pairs > 0, key_first + in_key, -1.0)
    by_query = jnp.where(pairs > 0, query_first + in_query, -1.0)
    total = jnp.sum(jnp.sum(pairs, axis=1, keepdims=True), axis=0, keepdims=True)

    lane = fiota((32, 128), 1)
    keys = fiota((32, 128), 0)
    id_col = (iota((32, 128), 0) // 2) * 16 + 2 * j + iota((32, 128), 0) % 2
    zero = jnp.zeros((32, 128), jnp.float32)
    rows = {n: zero for n in range(8)}
    for q in range(16):
        at_key = by_key[:, q : q + 1] == lane
        at_query = by_query[:, q : q + 1] == lane
        rows[KEY] += jnp.where(at_key, keys, 0.0)
        rows[QUERY] += jnp.where(at_key, float(q), 0.0)
        rows[SAME_KEY] += jnp.where(at_key, ones_where(in_key[:, q : q + 1] > 0), 0.0)
        rows[DIAGONAL] += jnp.where(at_key & (id_col == query_id(i, j, q)), 1.0, 0.0)
        rows[PERM] += jnp.where(at_query, by_key[:, q : q + 1], 0.0)
        rows[PERM_KEY] += jnp.where(at_query, keys, 0.0)
        rows[PERM_QUERY] += jnp.where(at_query, float(q), 0.0)
        rows[SAME_QUERY] += jnp.where(at_query, ones_where(in_query[:, q : q + 1] > 0), 0.0)
    most = {KEY: 31, QUERY: 15, SAME_KEY: 1, DIAGONAL: 1}
    most |= {PERM: SLOTS - 1, PERM_KEY: 31, PERM_QUERY: 15, SAME_QUERY: 1}
    for n in range(8):
        rows[n] = jnp.sum(rows[n], axis=0, keepdims=True)
        table[n : n + 1, :] = jnp.clip(rows[n].astype(jnp.int32), 0, most[n])
    key_end = jnp.where(key_count > 0, key_first + key_count, 0.0)
    key_end = jnp.sum(jnp.where(keys == lane, key_end, 0.0), axis=0, keepdims=True)
    table[KEY_END : KEY_END + 1, :] = jnp.clip(key_end.astype(jnp.int32), 0, SLOTS)
    query_end = jnp.where(query_count > 0, query_first + query_count, 0.0)
    table[QUERY_END : QUERY_END + 1, 0:16] = jnp.clip(query_end.astype(jnp.int32), 0, SLOTS)
    if table.shape[0] > LISTED:
        table[LISTED : LISTED + 32, 0:16] = pairs.astype(jnp.int32)
        return

    query_row = jnp.where(fiota((1, 128), 1) < total, rows[QUERY], -1.0)
    slot_query[...] = jnp.sum(
        jnp.where(iota((SLOTS, 128), 0) == iota((SLOTS, 128), 1), query_row, 0.0),
        axis=1,
        keepdims=True,
    )


def most_pairs(lists_ref):
    lists = lists_ref[...]
    groups = (lists // 2) % 8
    counts = jnp.zeros((8, 256), jnp.float32)
    group_of = iota((8, 256), 0)
    for n in range(16):
        fresh = jnp.ones((1, 256), jnp.float32)
        for m in range(n):
            fresh = jnp.where(lists[m : m + 1] == lists[n : n + 1], 0.0, fresh)
        counts += jnp.where(groups[n : n + 1] == group_of, fresh, 0.0)
    block = iota((256, 16), 0)
    query_group = (block // 16 % 8) * 2 + (block // 128 + block // 2 % 2) % 2
    member = ones_where(query_group == iota((256, 16), 1))
    return jnp.max(dot(counts, member))


def flip(bit):
    return 1 - bit


class Ring:
    def __init__(self, a, p, peer, row, blocks, gather_sems, out, own_in, part_in, part_out, sum_out, sum_in, sum_sems):
        self.a, self.p, self.peer, self.row = a, p, peer, row
        self.blocks, self.gather_sems = blocks, gather_sems
        self.out, self.own_in, self.part_in, self.part_out = out, own_in, part_in, part_out
        self.sum_out, self.sum_in, self.sum_sems = sum_out, sum_in, sum_sems
        self.copies, self.waited = [], 0

    def at(self, step):
        return (self.p + step + 4) % 4

    def send(self, src, dst, sems, n, peer):
        copy = pltpu.make_async_remote_copy(
            src_ref=src, dst_ref=dst, send_sem=sems[0].at[n], recv_sem=sems[1].at[n],
            device_id=peer, device_id_type=MESH,
        )
        copy.start()
        self.copies.append(copy)
        return copy

    def pass_half(self, n, row, half, peer):
        ref = self.blocks.at[row, half]
        return self.send(ref, ref, self.gather_sems, n, peer)

    def start_own(self):
        own, up, down = self.row(self.a, self.p), self.peer(False, 1), self.peer(False, -1)
        self.gather = {2: self.pass_half(2, own, 0, up)}
        self.gather[4] = self.pass_half(4, own, 1, down)
        self.gather[8] = self.pass_half(8, own, 0, self.peer(True, 1))
        self.gather[10] = self.pass_half(10, own, 1, self.peer(True, -1))
        self.gather[0] = self.pass_half(0, own, 0, self.peer(True, 0))
        self.gather[1] = self.pass_half(1, own, 1, self.peer(True, 0))
        self.gather[3] = self.pass_half(3, own, 1, up)
        self.gather[5] = self.pass_half(5, own, 0, down)

    def gather_step(self, n):
        self.gather[n].wait_recv()
        up, down = self.peer(False, 1), self.peer(False, -1)
        if n < 2:
            row = self.row(flip(self.a), self.p)
            if n == 0:
                self.gather[11] = self.pass_half(11, row, 0, down)
            else:
                self.gather[9] = self.pass_half(9, row, 1, up)
            return row, n
        a = self.a if n < 8 else flip(self.a)
        m = (n - 2) % 6
        row = self.row(a, self.at((-1, -1, 1, 1, 2, 2)[m]))
        half = (0, 1, 1, 0, 0, 1)[m]
        if m == 0:
            self.gather[n + 4] = self.pass_half(n + 4, row, half, up)
        if m == 2:
            self.gather[n + 3] = self.pass_half(n + 3, row, half, down)
        return row, half

    def pieces(self, phase):
        return [(half, b) for b in ((0, 1) if phase == 0 else (None,)) for half in (0, 1)]

    def start_part(self, phase, cross=None):
        a = flip(self.a) if phase == 0 else self.a
        parts = {}
        for half, b in self.pieces(phase):
            n = 12 + half if b is None else 2 * half + b
            step = 1 if half == 0 else -1
            src, dst = self.out.at[a, self.at(2), half], self.part_in.at[phase, half]
            if b is not None:
                src, dst = src.at[b], dst.at[b]
            parts[half, b] = [self.send(src, dst, self.sum_sems, n, self.peer(False, step))]
            if cross is not None:
                cross_out, cross_in, cross_peer = cross
                parts[half, b].append(
                    self.send(
                        cross_out.at[half, b], cross_in.at[half, b], self.sum_sems, 18 + n, cross_peer(step)
                    )
                )
        return [a, phase, parts, [], {}, cross]

    def start_plain(self, state):
        a, phase, _, plain, _, _ = state
        out, sems, n = self.out, self.sum_sems, 4 + 10 * phase
        plain += [
            self.send(out.at[a, self.at(1), 1], self.own_in.at[phase, 1], sems, n, self.peer(False, 1)),
            self.send(out.at[a, self.at(-1), 0], self.own_in.at[phase, 0], sems, n + 1, self.peer(False, -1)),
        ]

    def add_part(self, state):
        a, phase, parts, _, sums, cross = state
        for half, b in self.pieces(phase):
            n = 16 + half if b is None else 6 + 2 * half + b
            step = 1 if half == 0 else -1
            for copy in parts[half, b]:
                copy.wait_recv()
            at = slice(None) if b is None else b
            both = self.out[a, self.at(step), half, at].astype(jnp.float32)
            both += self.part_in[phase, half, at].astype(jnp.float32)
            if cross is not None:
                both += cross[1][half, at].astype(jnp.float32)
            self.part_out[phase, half, at] = both.astype(jnp.bfloat16)
            src, dst = self.part_out.at[phase, half], self.own_in.at[phase, 2 + half]
            if b is not None:
                src, dst = src.at[b], dst.at[b]
            sums[half, b] = self.send(src, dst, self.sum_sems, n, self.peer(False, step))

    def total(self, state, b):
        a, phase, _, plain, sums, _ = state
        while plain:
            plain.pop().wait_recv()
        for piece in [piece for piece in sums if piece[1] in (b, None)]:
            sums.pop(piece).wait_recv()
        total = self.out[a, self.p, :, b].astype(jnp.float32)
        total += self.own_in[phase, 0:2, b].astype(jnp.float32)
        return total + self.own_in[phase, 2:4, b].astype(jnp.float32)

    def send_total(self, state, b):
        self.sum_out[b] = self.total(state, b).astype(jnp.bfloat16)
        copy = self.send(self.sum_out.at[b], self.sum_in.at[b], self.sum_sems, 10 + b, self.peer(True, 0))
        self.to_total = getattr(self, "to_total", {}) | {b: copy}

    def whole_total(self, state, b):
        total = self.total(state, b)
        self.to_total[b].wait_recv()
        return total + self.sum_in[b].astype(jnp.float32)


class Refs:
    def __init__(self, names, refs):
        self.__dict__.update(zip(names, refs, strict=True))


def kernel(names, dense, *refs):
    r = Refs(names, refs)
    i, j = lax.axis_index("qblk"), lax.axis_index("kblk")
    core, y, x = i % 2, (i // 2) % 4, i // 8
    h, z = j % 2, j // 2
    scale = 1.0 / math.sqrt(BLOCK)
    kv, qg, table = r.kv, r.qg, r.table

    def key_row(x, y):
        return x * 8 + y * 2 + core

    def query_row(h, z):
        return z * 2 + h

    def key_peer(pair, step):
        return (key_row(flip(x) if pair else x, (y + step + 4) % 4), j)

    def query_peer(pair, step):
        at = (z + step + 4) % 4
        return ((i + 8) % 16, query_row(flip(h), at)) if pair else (i, query_row(h, at))

    sibling = (i + 1 - 2 * core, j)

    loads = []
    for n, (src, dst) in enumerate(
        ((r.k, kv.at[i, 0]), (r.q, qg.at[j, 0]), (r.v, kv.at[i, 1]), (r.g, qg.at[j, 1]), (r.lists, r.lists_v))
    ):
        loads.append(pltpu.make_async_copy(src, dst, r.local_sem.at[n]))
        loads[-1].start()

    stat_peers = [query_peer(pair, step) for pair, step in STAT_STEPS]
    peers = [sibling, key_peer(True, 0), key_peer(False, 1), key_peer(False, -1), key_peer(True, 1), key_peer(True, -1)] + stat_peers[:3] + stat_peers[4:6]
    barrier = pltpu.get_barrier_semaphore()
    for peer in peers:
        pl.semaphore_signal(barrier, inc=1, device_id=peer, device_id_type=MESH)
    pl.semaphore_wait(barrier, len(peers))
    for load in loads[:4]:
        load.wait()

    keys = Ring(
        x, y, key_peer, key_row, kv, (r.kv_send, r.kv_recv), r.key_out, r.key_own_in, r.key_part_in,
        r.key_part_out, r.key_sum_out, r.key_sum_in, (r.key_send, r.key_recv),
    )
    queries = Ring(
        h, z, query_peer, query_row, qg, (r.qg_send, r.qg_recv), r.query_out, r.query_own_in, r.query_part_in,
        r.query_part_out, r.query_sum_out, r.query_sum_in, (r.query_send, r.query_recv),
    )
    sib = []

    def to_sibling(row, half):
        ref = kv.at[row, half]
        sib.append(keys.send(ref, ref, (r.sib_send, r.sib_recv), len(sib), sibling))

    def gather_steps(*steps):
        for n in steps:
            to_sibling(*keys.gather_step(n))
            queries.gather_step(n)

    keys.start_own()
    queries.start_own()
    to_sibling(i, 0)
    to_sibling(i, 1)

    loads[4].wait()
    list_pairs(i, j, r.lists_v, r.table_v, None if dense else r.slot_query)
    to_smem = pltpu.make_async_copy(r.table_v, table, r.local_sem.at[5])
    to_smem.start()
    gather_steps(2, 4, 0, 1, 8, 10)

    r.bias[0] = jnp.zeros((BLOCK, BLOCK), jnp.float32)
    r.bias[1] = jnp.where(
        iota((BLOCK, BLOCK), 0) <= iota((BLOCK, BLOCK), 1), 0.0, masked_score
    ).astype(jnp.float32)
    none = 0 if not dense else slice(None)
    r.key_acc[none] = jnp.zeros(r.key_acc[none].shape, jnp.float32)
    r.query_acc[none] = jnp.zeros(r.query_acc[none].shape, jnp.float32)
    if not dense:
        r.flag[0, 0] = most_pairs(r.lists_v)

    gather_steps(3, 5, 6, 7, 9, 11, 12, 13)
    for copy in sib:
        copy.wait_recv()
    to_smem.wait()

    (dense_stats if dense else slot_stats)(r, i, j, scale)

    st_sems = (r.st_send, r.st_recv)
    st_copies = []
    r.stats[j] = r.stats_out[...]
    for n, peer in enumerate(stat_peers):
        st_copies.append(queries.send(r.stats_out, r.stats.at[j], st_sems, n, peer))
    for ring in (keys, queries):
        for copy in ring.copies[: -len(st_copies) if ring is queries else None]:
            copy.wait_send()
            ring.waited += 1
    if not dense:
        slot_query_grads(r)
    for copy in st_copies:
        copy.wait_recv()
    logs = r.stats[:, 0]
    best = jnp.max(logs, axis=0)
    offset = best + jnp.log2(jnp.sum(jnp.exp2(logs - best[None]), axis=0))
    delta = jnp.sum(jnp.exp2(logs - offset[None]) * r.stats[:, 1], axis=0)
    for q in range(16):
        r.offsets[q] = offset[q : q + 1, :]
        r.deltas[q] = delta[q : q + 1, :]
    if not dense:
        scales = jnp.exp2(r.stats_out[0] - offset)
        r.columns[...] = jnp.transpose(jnp.concatenate([scales, delta - r.stats_out[1]], axis=0))

    if dense:
        dense_key_grads(r, i, j, scale)
    def query_part(q):
        if dense:
            return r.query_acc[q]
        sums = r.query_acc[table[QUERY_END, q]]
        own = r.columns[:, q : q + 1]
        shift = r.columns[:, 16 + q : 17 + q]
        return jnp.stack([own * (sums[0] - shift * sums[1]), own * sums[2]])

    def query_out(phase):
        for n in range(4):
            for b in range(2):
                for at in range(2):

                    @pl.when(at == (flip(h) if phase == 0 else h))
                    def _(n=n, b=b, at=at):
                        r.query_out[at, n, :, b] = query_part((n * 2 + at) * 2 + b).astype(jnp.bfloat16)

    query_out(0)
    query_sums = [queries.start_part(0)]
    queries.start_plain(query_sums[0])
    if not dense:
        slot_key_grads(r, i, j, scale)

    def key_part(block):
        return r.key_acc[block if dense else table[KEY_END, block]]

    def key_owner(at, step, parity):
        return at * 8 + keys.at(step) * 2 + parity

    for b in range(2):
        same = key_part(key_owner(flip(x), 2, core) * 2 + b).astype(jnp.bfloat16)
        other = key_part(key_owner(flip(x), 2, 1 - core) * 2 + b).astype(jnp.bfloat16)
        for half in range(2):
            r.key_out[flip(x), keys.at(2), half, b] = same[half]
            r.cross_out[half, b] = other[half]

    def cross_peer(step):
        return (x * 8 + keys.at(step) * 2 + 1 - core, j)

    key_sums = [keys.start_part(0, (r.cross_out, r.cross_in, cross_peer))]

    swaps = []
    ring_steps = ((0, 1, -1), (0, 1, -1, 2))
    for phase, at in ((0, flip(x)), (1, x)):
        for n, step in enumerate(ring_steps[phase]):
            for b in range(2):
                block = key_owner(at, step, 1 - core) * 2 + b
                r.sib_out[phase, n, :, b] = key_part(block).astype(jnp.bfloat16)
        some = pl.ds(0, len(ring_steps[phase]))
        swaps.append(
            keys.send(
                r.sib_out.at[phase, some], r.sib_in.at[phase, some], (r.sib_send, r.sib_recv), 16 + phase, sibling
            )
        )

    def key_out(phase, at):
        swaps[phase].wait_recv()
        for n, step in enumerate(ring_steps[phase]):
            for b in range(2):
                both = key_part(key_owner(at, step, core) * 2 + b) + r.sib_in[phase, n, :, b].astype(jnp.float32)
                r.key_out[at, keys.at(step), :, b] = both.astype(jnp.bfloat16)

    query_out(1)
    query_sums.append(queries.start_part(1))
    queries.add_part(query_sums[0])
    queries.start_plain(query_sums[1])
    key_out(0, flip(x))
    keys.start_plain(key_sums[0])
    keys.add_part(key_sums[0])
    key_out(1, x)
    key_sums.append(keys.start_part(1))
    keys.start_plain(key_sums[1])
    for b in range(2):
        queries.send_total(query_sums[0], b)
    queries.add_part(query_sums[1])
    for b in range(2):
        keys.send_total(key_sums[0], b)
    keys.add_part(key_sums[1])
    results = []

    def finish(n, ring, state, factors, outs):
        for b in range(2):
            rows = pl.ds(b * BLOCK, BLOCK)
            sums = ring.whole_total(state, b)
            for m in range(2):
                r.finals[n + m, rows, :] = (sums[m] * factors[m]).astype(jnp.bfloat16)
        for m in range(2):
            results.append(pltpu.make_async_copy(r.finals.at[n + m], outs[m], r.local_sem.at[6 + n + m]))
            results[-1].start()

    finish(0, queries, query_sums[1], (scale, 1.0), (r.query_grads, r.attended))
    finish(2, keys, key_sums[1], (scale, 1.0), (r.key_grads, r.value_grads))
    for ring in (keys, queries):
        for copy in ring.copies[ring.waited :]:
            copy.wait_send()
    for result in results:
        result.wait()


def slot_stats(r, i, j, scale):
    kv, qg, table = r.kv, r.qg, r.table

    def step(n, carry):
        for u in range(UNROLL):
            s = n * UNROLL + u
            k, q = table[KEY, s], table[QUERY, s]
            scores = against(kv[k // 2, 0, k % 2], qg[q // 2, 0, q % 2]) * (scale * LOG2E)
            scores += r.bias[table[DIAGONAL, s]]
            prob_grad = against(kv[k // 2, 1, k % 2], qg[q // 2, 1, q % 2])
            top = jnp.max(scores, axis=0, keepdims=True)
            prob = jnp.exp2(scores - top)
            r.probs[s] = prob
            r.prob_grads[s] = prob_grad
            r.tops[pl.ds(s, 1), :] = top
            r.totals[pl.ds(s, 1), :] = jnp.sum(prob, axis=0, keepdims=True)
            r.moments[pl.ds(s, 1), :] = jnp.sum(prob * prob_grad, axis=0, keepdims=True)
        return carry

    lax.fori_loop(0, SLOTS // UNROLL, step, 0)

    top, total, moment, owner = r.tops[...], r.totals[...], r.moments[...], r.slot_query[...]
    for q in range(16):
        mine = owner == float(q)
        top_q = jnp.max(jnp.where(mine, top, masked_score), axis=0, keepdims=True)
        part = jnp.where(mine, jnp.exp2(top - top_q), 0.0)
        total_q = jnp.sum(part * total, axis=0, keepdims=True)
        moment_q = jnp.sum(part * moment, axis=0, keepdims=True)
        put_stats(r, q, top_q, total_q, moment_q)


def put_stats(r, q, top, total, moment):
    some = total > 0
    safe = jnp.where(some, total, 1.0)
    log, mean = jnp.where(some, top + jnp.log2(safe), masked_score), moment / safe
    r.stats_out[0, pl.ds(q, 1), :] = log
    r.stats_out[1, pl.ds(q, 1), :] = mean
    r.own_logs[q] = log
    r.own_means[q] = mean


def slot_key_grads(r, i, j, scale):
    def step(n, carry):
        for u in range(UNROLL):
            s = n * UNROLL + u
            q = r.table[QUERY, s]
            keep = r.table[SAME_KEY, s].astype(jnp.float32)
            prob = r.probs[s] * jnp.exp2(r.tops[pl.ds(s, 1), :] - r.offsets[q])
            weights = prob.astype(jnp.bfloat16)
            score_grad = (prob * (r.prob_grads[s] - r.deltas[q])).astype(jnp.bfloat16)
            r.key_acc[s + 1, 0] = r.key_acc[s, 0] * keep + dot(score_grad, r.qg[q // 2, 0, q % 2])
            r.key_acc[s + 1, 1] = r.key_acc[s, 1] * keep + dot(weights, r.qg[q // 2, 1, q % 2])
        return carry

    lax.fori_loop(0, SLOTS // UNROLL, step, 0)


def slot_query_grads(r):
    def step(n, carry):
        for u in range(UNROLL):
            s = n * UNROLL + u
            k, q, at = r.table[PERM_KEY, s], r.table[PERM_QUERY, s], r.table[PERM, s]
            keep = r.table[SAME_QUERY, s].astype(jnp.float32)
            prob = r.probs[at] * jnp.exp2(r.tops[pl.ds(at, 1), :] - r.own_logs[q])
            weights = prob.astype(jnp.bfloat16)
            score_grad = (prob * (r.prob_grads[at] - r.own_means[q])).astype(jnp.bfloat16)
            keys, values = r.kv[k // 2, 0, k % 2], r.kv[k // 2, 1, k % 2]
            r.query_acc[s + 1, 0] = r.query_acc[s, 0] * keep + across(score_grad, keys)
            r.query_acc[s + 1, 1] = r.query_acc[s, 1] * keep + across(weights, keys)
            r.query_acc[s + 1, 2] = r.query_acc[s, 2] * keep + across(weights, values)
        return carry

    lax.fori_loop(0, SLOTS // UNROLL, step, 0)


def dense_tile(r, i, j, scale, q, k):
    scores = against(r.kv[k // 2, 0, k % 2], r.qg[q // 2, 0, q % 2]) * (scale * LOG2E)
    own = (k // 2) * 16 + 2 * j + k % 2 == query_id(i, j, q)
    scores += r.bias[own.astype(jnp.int32)]
    prob_grad = against(r.kv[k // 2, 1, k % 2], r.qg[q // 2, 1, q % 2])
    listed = r.table[LISTED + k, q].astype(jnp.float32)
    return scores + (1.0 - listed) * masked_score, prob_grad, listed


def dense_stats(r, i, j, scale):
    def query_step(q, carry):
        def key_step(k, state):
            top, total, moment = state
            scores, prob_grad, listed = dense_tile(r, i, j, scale, q, k)
            higher = jnp.maximum(top, jnp.max(scores, axis=0, keepdims=True))
            prob = jnp.exp2(scores - higher) * listed
            shrink = jnp.exp2(top - higher)
            total = total * shrink + jnp.sum(prob, axis=0, keepdims=True)
            moment = moment * shrink + jnp.sum(prob * prob_grad, axis=0, keepdims=True)
            return higher, total, moment

        zero = jnp.zeros((1, BLOCK), jnp.float32)
        put_stats(r, q, *lax.fori_loop(0, 32, key_step, (zero + masked_score, zero, zero)))
        return carry

    lax.fori_loop(0, 16, query_step, 0)


def dense_key_grads(r, i, j, scale):
    def step(n, carry):
        q, k = n // 32, n % 32
        scores, prob_grad, listed = dense_tile(r, i, j, scale, q, k)
        prob = jnp.exp2(scores - r.offsets[q]) * listed
        weights = prob.astype(jnp.bfloat16)
        score_grad = (prob * (prob_grad - r.deltas[q])).astype(jnp.bfloat16)
        for m, left in enumerate((score_grad, weights)):
            r.key_acc[k, m] = r.key_acc[k, m] + dot(left, r.qg[q // 2, m, q % 2])
            r.query_acc[q, m] = r.query_acc[q, m] + across(left, r.kv[k // 2, m, k % 2])
        return carry

    lax.fori_loop(0, 16 * 32, step, 0)


def attention(dense, queries, keys, values, grad_out, lists):
    rows, head = queries.shape
    out = jax.ShapeDtypeStruct((rows, head), jnp.bfloat16)
    f32, bf16 = jnp.float32, jnp.bfloat16
    tile = (BLOCK, BLOCK)
    table_rows = LISTED + 32 if dense else LISTED
    dma = pltpu.SemaphoreType.DMA
    any_spec = pl.BlockSpec(memory_space=pl.ANY)
    smem_spec = pl.BlockSpec(memory_space=pltpu.SMEM)
    scratch = {
        "kv": pltpu.VMEM((16, 2, 2) + tile, bf16),
        "qg": pltpu.VMEM((8, 2, 2) + tile, bf16),
        "table_v": pltpu.VMEM((table_rows, 128), jnp.int32),
        "table": pltpu.SMEM((table_rows, 128), jnp.int32),
        "bias": pltpu.VMEM((2,) + tile, f32),
        "stats_out": pltpu.VMEM((2, 16, 128), f32),
        "stats": pltpu.VMEM((8, 2, 16, 128), f32),
        "offsets": pltpu.VMEM((16, 1, 128), f32),
        "deltas": pltpu.VMEM((16, 1, 128), f32),
        "key_acc": pltpu.VMEM((32 if dense else SLOTS + 1, 2) + tile, f32),
        "query_acc": pltpu.VMEM(((16, 2) if dense else (SLOTS + 1, 3)) + tile, f32),
        "own_logs": pltpu.VMEM((16, 1, 128), f32),
        "own_means": pltpu.VMEM((16, 1, 128), f32),
        "cross_out": pltpu.VMEM((2, 2) + tile, bf16),
        "cross_in": pltpu.VMEM((2, 2) + tile, bf16),
        "sib_out": pltpu.VMEM((2, 4, 2, 2) + tile, bf16),
        "sib_in": pltpu.VMEM((2, 4, 2, 2) + tile, bf16),
        "lists_v": pltpu.VMEM((16, 256), jnp.int32),
        "finals": pltpu.VMEM((4, 2 * BLOCK, BLOCK), bf16),
        "local_sem": dma((10,)),
        "kv_send": dma((14,)),
        "kv_recv": dma((14,)),
        "qg_send": dma((14,)),
        "qg_recv": dma((14,)),
        "sib_send": dma((18,)),
        "sib_recv": dma((18,)),
        "st_send": dma((7,)),
        "st_recv": dma((7,)),
    }
    for ring in ("key", "query"):
        scratch |= {
            ring + "_out": pltpu.VMEM((2, 4, 2, 2) + tile, bf16),
            ring + "_own_in": pltpu.VMEM((2, 4, 2) + tile, bf16),
            ring + "_part_in": pltpu.VMEM((2, 2, 2) + tile, bf16),
            ring + "_part_out": pltpu.VMEM((2, 2, 2) + tile, bf16),
            ring + "_sum_out": pltpu.VMEM((2, 2) + tile, bf16),
            ring + "_sum_in": pltpu.VMEM((2, 2) + tile, bf16),
            ring + "_send": dma((22,)),
            ring + "_recv": dma((22,)),
        }
    if not dense:
        scratch |= {
            "slot_query": pltpu.VMEM((SLOTS, 1), f32),
            "probs": pltpu.VMEM((SLOTS,) + tile, f32),
            "prob_grads": pltpu.VMEM((SLOTS,) + tile, f32),
            "tops": pltpu.VMEM((SLOTS, 128), f32),
            "totals": pltpu.VMEM((SLOTS, 128), f32),
            "moments": pltpu.VMEM((SLOTS, 128), f32),
            "columns": pltpu.VMEM((BLOCK, 32), f32),
        }
    outs = ["attended", "query_grads", "key_grads", "value_grads"] + ["flag"] * (not dense)
    out_shape, out_specs = [out] * 4, [any_spec] * 4
    if not dense:
        out_shape.append(jax.ShapeDtypeStruct((1, 1), f32))
        out_specs.append(smem_spec)
    return pl.pallas_call(
        functools.partial(kernel, ["q", "k", "v", "g", "lists"] + outs + list(scratch), dense),
        out_shape=out_shape,
        in_specs=[any_spec] * 5,
        out_specs=out_specs,
        scratch_shapes=list(scratch.values()),
        compiler_params=pltpu.CompilerParams(
            collective_id=1 if dense else 0, has_side_effects=True, vmem_limit_bytes=56 << 20
        ),
        name="dense_attention" if dense else "block_sparse_attention",
    )(*(a.reshape(2, BLOCK, BLOCK) for a in (queries, keys, values, grad_out)), lists)


def hand_out_kernel(*refs):
    sems = refs[-1]
    copies = [pltpu.make_async_copy(refs[n], refs[4 + n], sems.at[n]) for n in range(4)]
    for copy in copies:
        copy.start()
    for copy in copies:
        copy.wait()


def hand_out(outs):
    spec = pl.BlockSpec(memory_space=pl.ANY)
    return tuple(
        pl.pallas_call(
            hand_out_kernel,
            out_shape=[jax.ShapeDtypeStruct(out.shape, out.dtype) for out in outs],
            in_specs=[spec] * 4,
            out_specs=[spec] * 4,
            scratch_shapes=[pltpu.SemaphoreType.DMA((4,))],
            name="hand_out",
        )(*outs)
    )


def per_device(queries, keys, values, grad_out, key_blocks):
    args = (queries, keys, values, grad_out, key_blocks.T)
    *outs, most = attention(False, *args)
    return lax.cond(
        most[0, 0] > SLOTS,
        lambda: hand_out(attention(True, *args)),
        lambda: hand_out(outs),
    )


def solution(mesh):
    split = P(("qblk", "kblk"), None)
    return jax.shard_map(
        per_device,
        mesh=mesh,
        in_specs=(split, split, split, split, P()),
        out_specs=(split, split, split, split),
        check_vma=False,
    )
```

```python
import functools
import math

import jax
import jax.numpy as jnp
from jax import lax
from jax.experimental import pallas as pl
from jax.experimental.pallas import tpu as pltpu
from jax.sharding import PartitionSpec as P

BLOCK = 128
SLOTS = 56
UNROLL = 56
MESH = pl.DeviceIdType.MESH

masked_score = -1e30
LOG2E = 1.4426950408889634


def against(left, right):
    return lax.dot_general(
        left, right, (((1,), (1,)), ((), ())), preferred_element_type=jnp.float32
    )


def across(left, right):
    return lax.dot_general(
        left, right, (((0,), (0,)), ((), ())), preferred_element_type=jnp.float32
    )


def dot(left, right):
    return jnp.dot(left, right, preferred_element_type=jnp.float32)


KEY, QUERY, SAME_KEY, DIAGONAL, PERM, PERM_KEY, PERM_QUERY, SAME_QUERY, KEY_END, QUERY_END = range(10)
LISTED = 16

STAT_STEPS = ((False, 1), (False, -1), (True, 0), (False, 2), (True, 1), (True, -1), (True, 2))


def iota(shape, dim):
    return lax.broadcasted_iota(jnp.int32, shape, dim)


def fiota(shape, dim):
    return iota(shape, dim).astype(jnp.float32)


def ones_where(cond):
    return jnp.where(cond, 1.0, 0.0).astype(jnp.float32)


def query_id(i, j, q):
    x = (i // 8 + j % 2 + (q // 2) % 2) % 2
    return (x * 8 + i % 8) * 16 + q


def list_pairs(i, j, lists_ref, table, slot_query):
    lists = lists_ref[...].astype(jnp.float32)
    chosen = ones_where(iota((256, 16), 0) == query_id(i, j, iota((256, 16), 1)))
    own = dot(lists, chosen)
    key_ids = ((iota((32, 16), 0) // 2) * 16 + 2 * j + iota((32, 16), 0) % 2).astype(jnp.float32)
    pairs = jnp.zeros((32, 16), jnp.float32)
    for n in range(16):
        pairs = jnp.maximum(pairs, ones_where(own[n : n + 1, :] == key_ids))
    earlier_query = ones_where(iota((16, 16), 0) < iota((16, 16), 1))
    earlier_key = ones_where(iota((32, 32), 1) < iota((32, 32), 0))
    in_key = dot(pairs, earlier_query)
    in_query = dot(earlier_key, pairs)
    key_count = jnp.sum(pairs, axis=1, keepdims=True)
    query_count = jnp.sum(pairs, axis=0, keepdims=True)
    key_first = jnp.sum(in_query, axis=1, keepdims=True)
    query_first = jnp.sum(in_key, axis=0, keepdims=True)
    by_key = jnp.where(pairs > 0, key_first + in_key, -1.0)
    by_query = jnp.where(pairs > 0, query_first + in_query, -1.0)
    total = jnp.sum(jnp.sum(pairs, axis=1, keepdims=True), axis=0, keepdims=True)

    lane = fiota((32, 128), 1)
    keys = fiota((32, 128), 0)
    id_col = (iota((32, 128), 0) // 2) * 16 + 2 * j + iota((32, 128), 0) % 2
    zero = jnp.zeros((32, 128), jnp.float32)
    rows = {n: zero for n in range(8)}
    for q in range(16):
        at_key = by_key[:, q : q + 1] == lane
        at_query = by_query[:, q : q + 1] == lane
        rows[KEY] += jnp.where(at_key, keys, 0.0)
        rows[QUERY] += jnp.where(at_key, float(q), 0.0)
        rows[SAME_KEY] += jnp.where(at_key, ones_where(in_key[:, q : q + 1] > 0), 0.0)
        rows[DIAGONAL] += jnp.where(at_key & (id_col == query_id(i, j, q)), 1.0, 0.0)
        rows[PERM] += jnp.where(at_query, by_key[:, q : q + 1], 0.0)
        rows[PERM_KEY] += jnp.where(at_query, keys, 0.0)
        rows[PERM_QUERY] += jnp.where(at_query, float(q), 0.0)
        rows[SAME_QUERY] += jnp.where(at_query, ones_where(in_query[:, q : q + 1] > 0), 0.0)
    most = {KEY: 31, QUERY: 15, SAME_KEY: 1, DIAGONAL: 1}
    most |= {PERM: SLOTS - 1, PERM_KEY: 31, PERM_QUERY: 15, SAME_QUERY: 1}
    for n in range(8):
        rows[n] = jnp.sum(rows[n], axis=0, keepdims=True)
        table[n : n + 1, :] = jnp.clip(rows[n].astype(jnp.int32), 0, most[n])
    key_end = jnp.where(key_count > 0, key_first + key_count, 0.0)
    key_end = jnp.sum(jnp.where(keys == lane, key_end, 0.0), axis=0, keepdims=True)
    table[KEY_END : KEY_END + 1, :] = jnp.clip(key_end.astype(jnp.int32), 0, SLOTS)
    query_end = jnp.where(query_count > 0, query_first + query_count, 0.0)
    table[QUERY_END : QUERY_END + 1, 0:16] = jnp.clip(query_end.astype(jnp.int32), 0, SLOTS)
    if table.shape[0] > LISTED:
        table[LISTED : LISTED + 32, 0:16] = pairs.astype(jnp.int32)
        return

    query_row = jnp.where(fiota((1, 128), 1) < total, rows[QUERY], -1.0)
    slot_query[...] = jnp.sum(
        jnp.where(iota((SLOTS, 128), 0) == iota((SLOTS, 128), 1), query_row, 0.0),
        axis=1,
        keepdims=True,
    )


def most_pairs(lists_ref):
    lists = lists_ref[...]
    groups = (lists // 2) % 8
    counts = jnp.zeros((8, 256), jnp.float32)
    group_of = iota((8, 256), 0)
    for n in range(16):
        fresh = jnp.ones((1, 256), jnp.float32)
        for m in range(n):
            fresh = jnp.where(lists[m : m + 1] == lists[n : n + 1], 0.0, fresh)
        counts += jnp.where(groups[n : n + 1] == group_of, fresh, 0.0)
    block = iota((256, 16), 0)
    query_group = (block // 16 % 8) * 2 + (block // 128 + block // 2 % 2) % 2
    member = ones_where(query_group == iota((256, 16), 1))
    return jnp.max(dot(counts, member))


def flip(bit):
    return 1 - bit


class Ring:
    def __init__(self, a, p, peer, row, blocks, gather_sems, out, own_in, part_in, part_out, sum_out, sum_in, sum_sems):
        self.a, self.p, self.peer, self.row = a, p, peer, row
        self.blocks, self.gather_sems = blocks, gather_sems
        self.out, self.own_in, self.part_in, self.part_out = out, own_in, part_in, part_out
        self.sum_out, self.sum_in, self.sum_sems = sum_out, sum_in, sum_sems
        self.copies, self.waited = [], 0

    def at(self, step):
        return (self.p + step + 4) % 4

    def send(self, src, dst, sems, n, peer):
        copy = pltpu.make_async_remote_copy(
            src_ref=src, dst_ref=dst, send_sem=sems[0].at[n], recv_sem=sems[1].at[n],
            device_id=peer, device_id_type=MESH,
        )
        copy.start()
        self.copies.append(copy)
        return copy

    def pass_half(self, n, row, half, peer):
        ref = self.blocks.at[row, half]
        return self.send(ref, ref, self.gather_sems, n, peer)

    def start_own(self):
        own, up, down = self.row(self.a, self.p), self.peer(False, 1), self.peer(False, -1)
        self.gather = {2: self.pass_half(2, own, 0, up)}
        self.gather[4] = self.pass_half(4, own, 1, down)
        self.gather[8] = self.pass_half(8, own, 0, self.peer(True, 1))
        self.gather[10] = self.pass_half(10, own, 1, self.peer(True, -1))
        self.gather[0] = self.pass_half(0, own, 0, self.peer(True, 0))
        self.gather[1] = self.pass_half(1, own, 1, self.peer(True, 0))
        self.gather[3] = self.pass_half(3, own, 1, up)
        self.gather[5] = self.pass_half(5, own, 0, down)

    def gather_step(self, n):
        self.gather[n].wait_recv()
        up, down = self.peer(False, 1), self.peer(False, -1)
        if n < 2:
            row = self.row(flip(self.a), self.p)
            if n == 0:
                self.gather[11] = self.pass_half(11, row, 0, down)
            else:
                self.gather[9] = self.pass_half(9, row, 1, up)
            return row, n
        a = self.a if n < 8 else flip(self.a)
        m = (n - 2) % 6
        row = self.row(a, self.at((-1, -1, 1, 1, 2, 2)[m]))
        half = (0, 1, 1, 0, 0, 1)[m]
        if m == 0:
            self.gather[n + 4] = self.pass_half(n + 4, row, half, up)
        if m == 2:
            self.gather[n + 3] = self.pass_half(n + 3, row, half, down)
        return row, half

    def pieces(self, phase):
        return [(half, b) for b in ((0, 1) if phase == 0 else (None,)) for half in (0, 1)]

    def start_part(self, phase, cross=None):
        a = flip(self.a) if phase == 0 else self.a
        parts = {}
        for half, b in self.pieces(phase):
            n = 12 + half if b is None else 2 * half + b
            step = 1 if half == 0 else -1
            src, dst = self.out.at[a, self.at(2), half], self.part_in.at[phase, half]
            if b is not None:
                src, dst = src.at[b], dst.at[b]
            parts[half, b] = [self.send(src, dst, self.sum_sems, n, self.peer(False, step))]
            if cross is not None:
                cross_out, cross_in, cross_peer = cross
                parts[half, b].append(
                    self.send(
                        cross_out.at[half, b], cross_in.at[half, b], self.sum_sems, 18 + n, cross_peer(step)
                    )
                )
        return [a, phase, parts, [], {}, cross]

    def start_plain(self, state):
        a, phase, _, plain, _, _ = state
        out, sems, n = self.out, self.sum_sems, 4 + 10 * phase
        plain += [
            self.send(out.at[a, self.at(1), 1], self.own_in.at[phase, 1], sems, n, self.peer(False, 1)),
            self.send(out.at[a, self.at(-1), 0], self.own_in.at[phase, 0], sems, n + 1, self.peer(False, -1)),
        ]

    def add_part(self, state):
        a, phase, parts, _, sums, cross = state
        for half, b in self.pieces(phase):
            n = 16 + half if b is None else 6 + 2 * half + b
            step = 1 if half == 0 else -1
            for copy in parts[half, b]:
                copy.wait_recv()
            at = slice(None) if b is None else b
            both = self.out[a, self.at(step), half, at].astype(jnp.float32)
            both += self.part_in[phase, half, at].astype(jnp.float32)
            if cross is not None:
                both += cross[1][half, at].astype(jnp.float32)
            self.part_out[phase, half, at] = both.astype(jnp.bfloat16)
            src, dst = self.part_out.at[phase, half], self.own_in.at[phase, 2 + half]
            if b is not None:
                src, dst = src.at[b], dst.at[b]
            sums[half, b] = self.send(src, dst, self.sum_sems, n, self.peer(False, step))

    def total(self, state, b):
        a, phase, _, plain, sums, _ = state
        while plain:
            plain.pop().wait_recv()
        for piece in [piece for piece in sums if piece[1] in (b, None)]:
            sums.pop(piece).wait_recv()
        total = self.out[a, self.p, :, b].astype(jnp.float32)
        total += self.own_in[phase, 0:2, b].astype(jnp.float32)
        return total + self.own_in[phase, 2:4, b].astype(jnp.float32)

    def send_total(self, state, b):
        self.sum_out[b] = self.total(state, b).astype(jnp.bfloat16)
        copy = self.send(self.sum_out.at[b], self.sum_in.at[b], self.sum_sems, 10 + b, self.peer(True, 0))
        self.to_total = getattr(self, "to_total", {}) | {b: copy}

    def whole_total(self, state, b):
        total = self.total(state, b)
        self.to_total[b].wait_recv()
        return total + self.sum_in[b].astype(jnp.float32)


class Refs:
    def __init__(self, names, refs):
        self.__dict__.update(zip(names, refs, strict=True))


def kernel(names, dense, *refs):
    r = Refs(names, refs)
    i, j = lax.axis_index("qblk"), lax.axis_index("kblk")
    core, y, x = i % 2, (i // 2) % 4, i // 8
    h, z = j % 2, j // 2
    scale = 1.0 / math.sqrt(BLOCK)
    kv, qg, table = r.kv, r.qg, r.table

    def key_row(x, y):
        return x * 8 + y * 2 + core

    def query_row(h, z):
        return z * 2 + h

    def key_peer(pair, step):
        return (key_row(flip(x) if pair else x, (y + step + 4) % 4), j)

    def query_peer(pair, step):
        at = (z + step + 4) % 4
        return ((i + 8) % 16, query_row(flip(h), at)) if pair else (i, query_row(h, at))

    sibling = (i + 1 - 2 * core, j)

    loads = []
    for n, (src, dst) in enumerate(
        ((r.k, kv.at[i, 0]), (r.q, qg.at[j, 0]), (r.v, kv.at[i, 1]), (r.g, qg.at[j, 1]), (r.lists, r.lists_v))
    ):
        loads.append(pltpu.make_async_copy(src, dst, r.local_sem.at[n]))
        loads[-1].start()

    stat_peers = [query_peer(pair, step) for pair, step in STAT_STEPS]
    peers = [sibling, key_peer(True, 0), key_peer(False, 1), key_peer(False, -1), key_peer(True, 1), key_peer(True, -1)] + stat_peers[:3] + stat_peers[4:6]
    barrier = pltpu.get_barrier_semaphore()
    for peer in peers:
        pl.semaphore_signal(barrier, inc=1, device_id=peer, device_id_type=MESH)
    pl.semaphore_wait(barrier, len(peers))
    for load in loads[:4]:
        load.wait()

    keys = Ring(
        x, y, key_peer, key_row, kv, (r.kv_send, r.kv_recv), r.key_out, r.key_own_in, r.key_part_in,
        r.key_part_out, r.key_sum_out, r.key_sum_in, (r.key_send, r.key_recv),
    )
    queries = Ring(
        h, z, query_peer, query_row, qg, (r.qg_send, r.qg_recv), r.query_out, r.query_own_in, r.query_part_in,
        r.query_part_out, r.query_sum_out, r.query_sum_in, (r.query_send, r.query_recv),
    )
    sib = []

    def to_sibling(row, half):
        ref = kv.at[row, half]
        sib.append(keys.send(ref, ref, (r.sib_send, r.sib_recv), len(sib), sibling))

    def gather_steps(*steps):
        for n in steps:
            to_sibling(*keys.gather_step(n))
            queries.gather_step(n)

    keys.start_own()
    queries.start_own()
    to_sibling(i, 0)
    to_sibling(i, 1)

    loads[4].wait()
    list_pairs(i, j, r.lists_v, r.table_v, None if dense else r.slot_query)
    to_smem = pltpu.make_async_copy(r.table_v, table, r.local_sem.at[5])
    to_smem.start()
    gather_steps(2, 4, 0, 1, 8, 10)

    r.bias[0] = jnp.zeros((BLOCK, BLOCK), jnp.float32)
    r.bias[1] = jnp.where(
        iota((BLOCK, BLOCK), 0) <= iota((BLOCK, BLOCK), 1), 0.0, masked_score
    ).astype(jnp.float32)
    none = 0 if not dense else slice(None)
    r.key_acc[none] = jnp.zeros(r.key_acc[none].shape, jnp.float32)
    r.query_acc[none] = jnp.zeros(r.query_acc[none].shape, jnp.float32)
    if not dense:
        r.flag[0, 0] = most_pairs(r.lists_v)

    gather_steps(3, 5, 6, 7, 9, 11, 12, 13)
    for copy in sib:
        copy.wait_recv()
    to_smem.wait()

    (dense_stats if dense else slot_stats)(r, i, j, scale)

    st_sems = (r.st_send, r.st_recv)
    st_copies = []
    r.stats[j] = r.stats_out[...]
    for n, peer in enumerate(stat_peers):
        st_copies.append(queries.send(r.stats_out, r.stats.at[j], st_sems, n, peer))
    for ring in (keys, queries):
        for copy in ring.copies[: -len(st_copies) if ring is queries else None]:
            copy.wait_send()
            ring.waited += 1
    if not dense:
        slot_query_grads(r)
    for copy in st_copies:
        copy.wait_recv()
    logs = r.stats[:, 0]
    best = jnp.max(logs, axis=0)
    offset = best + jnp.log2(jnp.sum(jnp.exp2(logs - best[None]), axis=0))
    delta = jnp.sum(jnp.exp2(logs - offset[None]) * r.stats[:, 1], axis=0)
    for q in range(16):
        r.offsets[q] = offset[q : q + 1, :]
        r.deltas[q] = delta[q : q + 1, :]
    if not dense:
        scales = jnp.exp2(r.stats_out[0] - offset)
        r.columns[...] = jnp.transpose(jnp.concatenate([scales, delta - r.stats_out[1]], axis=0))

    if dense:
        dense_key_grads(r, i, j, scale)
    def query_part(q):
        if dense:
            return r.query_acc[q]
        sums = r.query_acc[table[QUERY_END, q]]
        own = r.columns[:, q : q + 1]
        shift = r.columns[:, 16 + q : 17 + q]
        return jnp.stack([own * (sums[0] - shift * sums[1]), own * sums[2]])

    def query_out(phase):
        for n in range(4):
            for b in range(2):
                for at in range(2):

                    @pl.when(at == (flip(h) if phase == 0 else h))
                    def _(n=n, b=b, at=at):
                        r.query_out[at, n, :, b] = query_part((n * 2 + at) * 2 + b).astype(jnp.bfloat16)

    query_out(0)
    query_sums = [queries.start_part(0)]
    queries.start_plain(query_sums[0])
    if not dense:
        slot_key_grads(r, i, j, scale)

    def key_part(block):
        return r.key_acc[block if dense else table[KEY_END, block]]

    def key_owner(at, step, parity):
        return at * 8 + keys.at(step) * 2 + parity

    for b in range(2):
        same = key_part(key_owner(flip(x), 2, core) * 2 + b).astype(jnp.bfloat16)
        other = key_part(key_owner(flip(x), 2, 1 - core) * 2 + b).astype(jnp.bfloat16)
        for half in range(2):
            r.key_out[flip(x), keys.at(2), half, b] = same[half]
            r.cross_out[half, b] = other[half]

    def cross_peer(step):
        return (x * 8 + keys.at(step) * 2 + 1 - core, j)

    key_sums = [keys.start_part(0, (r.cross_out, r.cross_in, cross_peer))]

    swaps = []
    ring_steps = ((0, 1, -1), (0, 1, -1, 2))
    for phase, at in ((0, flip(x)), (1, x)):
        for n, step in enumerate(ring_steps[phase]):
            for b in range(2):
                block = key_owner(at, step, 1 - core) * 2 + b
                r.sib_out[phase, n, :, b] = key_part(block).astype(jnp.bfloat16)
        some = pl.ds(0, len(ring_steps[phase]))
        swaps.append(
            keys.send(
                r.sib_out.at[phase, some], r.sib_in.at[phase, some], (r.sib_send, r.sib_recv), 16 + phase, sibling
            )
        )

    def key_out(phase, at):
        swaps[phase].wait_recv()
        for n, step in enumerate(ring_steps[phase]):
            for b in range(2):
                both = key_part(key_owner(at, step, core) * 2 + b) + r.sib_in[phase, n, :, b].astype(jnp.float32)
                r.key_out[at, keys.at(step), :, b] = both.astype(jnp.bfloat16)

    query_out(1)
    query_sums.append(queries.start_part(1))
    queries.add_part(query_sums[0])
    queries.start_plain(query_sums[1])
    key_out(0, flip(x))
    keys.start_plain(key_sums[0])
    keys.add_part(key_sums[0])
    key_out(1, x)
    key_sums.append(keys.start_part(1))
    keys.start_plain(key_sums[1])
    for b in range(2):
        queries.send_total(query_sums[0], b)
    queries.add_part(query_sums[1])
    for b in range(2):
        keys.send_total(key_sums[0], b)
    keys.add_part(key_sums[1])
    results = []

    def finish(n, ring, state, factors, outs):
        for b in range(2):
            rows = pl.ds(b * BLOCK, BLOCK)
            sums = ring.whole_total(state, b)
            for m in range(2):
                r.finals[n + m, rows, :] = (sums[m] * factors[m]).astype(jnp.bfloat16)
        for m in range(2):
            results.append(pltpu.make_async_copy(r.finals.at[n + m], outs[m], r.local_sem.at[6 + n + m]))
            results[-1].start()

    finish(0, queries, query_sums[1], (scale, 1.0), (r.query_grads, r.attended))
    finish(2, keys, key_sums[1], (scale, 1.0), (r.key_grads, r.value_grads))
    for ring in (keys, queries):
        for copy in ring.copies[ring.waited :]:
            copy.wait_send()
    for result in results:
        result.wait()


def slot_stats(r, i, j, scale):
    kv, qg, table = r.kv, r.qg, r.table

    def step(n, carry):
        for u in range(UNROLL):
            s = n * UNROLL + u
            k, q = table[KEY, s], table[QUERY, s]
            scores = against(kv[k // 2, 0, k % 2], qg[q // 2, 0, q % 2]) * (scale * LOG2E)
            scores += r.bias[table[DIAGONAL, s]]
            prob_grad = against(kv[k // 2, 1, k % 2], qg[q // 2, 1, q % 2])
            top = jnp.max(scores, axis=0, keepdims=True)
            prob = jnp.exp2(scores - top)
            r.probs[s] = prob
            r.prob_grads[s] = prob_grad
            r.tops[pl.ds(s, 1), :] = top
            r.totals[pl.ds(s, 1), :] = jnp.sum(prob, axis=0, keepdims=True)
            r.moments[pl.ds(s, 1), :] = jnp.sum(prob * prob_grad, axis=0, keepdims=True)
        return carry

    lax.fori_loop(0, SLOTS // UNROLL, step, 0)

    top, total, moment, owner = r.tops[...], r.totals[...], r.moments[...], r.slot_query[...]
    for q in range(16):
        mine = owner == float(q)
        top_q = jnp.max(jnp.where(mine, top, masked_score), axis=0, keepdims=True)
        part = jnp.where(mine, jnp.exp2(top - top_q), 0.0)
        total_q = jnp.sum(part * total, axis=0, keepdims=True)
        moment_q = jnp.sum(part * moment, axis=0, keepdims=True)
        put_stats(r, q, top_q, total_q, moment_q)


def put_stats(r, q, top, total, moment):
    some = total > 0
    safe = jnp.where(some, total, 1.0)
    log, mean = jnp.where(some, top + jnp.log2(safe), masked_score), moment / safe
    r.stats_out[0, pl.ds(q, 1), :] = log
    r.stats_out[1, pl.ds(q, 1), :] = mean
    r.own_logs[q] = log
    r.own_means[q] = mean


def slot_key_grads(r, i, j, scale):
    def step(n, carry):
        for u in range(UNROLL):
            s = n * UNROLL + u
            q = r.table[QUERY, s]
            keep = r.table[SAME_KEY, s].astype(jnp.float32)
            prob = r.probs[s] * jnp.exp2(r.tops[pl.ds(s, 1), :] - r.offsets[q])
            weights = prob.astype(jnp.bfloat16)
            score_grad = (prob * (r.prob_grads[s] - r.deltas[q])).astype(jnp.bfloat16)
            r.key_acc[s + 1, 0] = r.key_acc[s, 0] * keep + dot(score_grad, r.qg[q // 2, 0, q % 2])
            r.key_acc[s + 1, 1] = r.key_acc[s, 1] * keep + dot(weights, r.qg[q // 2, 1, q % 2])
        return carry

    lax.fori_loop(0, SLOTS // UNROLL, step, 0)


def slot_query_grads(r):
    def step(n, carry):
        for u in range(UNROLL):
            s = n * UNROLL + u
            k, q, at = r.table[PERM_KEY, s], r.table[PERM_QUERY, s], r.table[PERM, s]
            keep = r.table[SAME_QUERY, s].astype(jnp.float32)
            prob = r.probs[at] * jnp.exp2(r.tops[pl.ds(at, 1), :] - r.own_logs[q])
            weights = prob.astype(jnp.bfloat16)
            score_grad = (prob * (r.prob_grads[at] - r.own_means[q])).astype(jnp.bfloat16)
            keys, values = r.kv[k // 2, 0, k % 2], r.kv[k // 2, 1, k % 2]
            r.query_acc[s + 1, 0] = r.query_acc[s, 0] * keep + across(score_grad, keys)
            r.query_acc[s + 1, 1] = r.query_acc[s, 1] * keep + across(weights, keys)
            r.query_acc[s + 1, 2] = r.query_acc[s, 2] * keep + across(weights, values)
        return carry

    lax.fori_loop(0, SLOTS // UNROLL, step, 0)


def dense_tile(r, i, j, scale, q, k):
    scores = against(r.kv[k // 2, 0, k % 2], r.qg[q // 2, 0, q % 2]) * (scale * LOG2E)
    own = (k // 2) * 16 + 2 * j + k % 2 == query_id(i, j, q)
    scores += r.bias[own.astype(jnp.int32)]
    prob_grad = against(r.kv[k // 2, 1, k % 2], r.qg[q // 2, 1, q % 2])
    listed = r.table[LISTED + k, q].astype(jnp.float32)
    return scores + (1.0 - listed) * masked_score, prob_grad, listed


def dense_stats(r, i, j, scale):
    def query_step(q, carry):
        def key_step(k, state):
            top, total, moment = state
            scores, prob_grad, listed = dense_tile(r, i, j, scale, q, k)
            higher = jnp.maximum(top, jnp.max(scores, axis=0, keepdims=True))
            prob = jnp.exp2(scores - higher) * listed
            shrink = jnp.exp2(top - higher)
            total = total * shrink + jnp.sum(prob, axis=0, keepdims=True)
            moment = moment * shrink + jnp.sum(prob * prob_grad, axis=0, keepdims=True)
            return higher, total, moment

        zero = jnp.zeros((1, BLOCK), jnp.float32)
        put_stats(r, q, *lax.fori_loop(0, 32, key_step, (zero + masked_score, zero, zero)))
        return carry

    lax.fori_loop(0, 16, query_step, 0)


def dense_key_grads(r, i, j, scale):
    def step(n, carry):
        q, k = n // 32, n % 32
        scores, prob_grad, listed = dense_tile(r, i, j, scale, q, k)
        prob = jnp.exp2(scores - r.offsets[q]) * listed
        weights = prob.astype(jnp.bfloat16)
        score_grad = (prob * (prob_grad - r.deltas[q])).astype(jnp.bfloat16)
        for m, left in enumerate((score_grad, weights)):
            r.key_acc[k, m] = r.key_acc[k, m] + dot(left, r.qg[q // 2, m, q % 2])
            r.query_acc[q, m] = r.query_acc[q, m] + across(left, r.kv[k // 2, m, k % 2])
        return carry

    lax.fori_loop(0, 16 * 32, step, 0)


def attention(dense, queries, keys, values, grad_out, lists):
    rows, head = queries.shape
    out = jax.ShapeDtypeStruct((rows, head), jnp.bfloat16)
    f32, bf16 = jnp.float32, jnp.bfloat16
    tile = (BLOCK, BLOCK)
    table_rows = LISTED + 32 if dense else LISTED
    dma = pltpu.SemaphoreType.DMA
    any_spec = pl.BlockSpec(memory_space=pl.ANY)
    smem_spec = pl.BlockSpec(memory_space=pltpu.SMEM)
    scratch = {
        "kv": pltpu.VMEM((16, 2, 2) + tile, bf16),
        "qg": pltpu.VMEM((8, 2, 2) + tile, bf16),
        "table_v": pltpu.VMEM((table_rows, 128), jnp.int32),
        "table": pltpu.SMEM((table_rows, 128), jnp.int32),
        "bias": pltpu.VMEM((2,) + tile, f32),
        "stats_out": pltpu.VMEM((2, 16, 128), f32),
        "stats": pltpu.VMEM((8, 2, 16, 128), f32),
        "offsets": pltpu.VMEM((16, 1, 128), f32),
        "deltas": pltpu.VMEM((16, 1, 128), f32),
        "key_acc": pltpu.VMEM((32 if dense else SLOTS + 1, 2) + tile, f32),
        "query_acc": pltpu.VMEM(((16, 2) if dense else (SLOTS + 1, 3)) + tile, f32),
        "own_logs": pltpu.VMEM((16, 1, 128), f32),
        "own_means": pltpu.VMEM((16, 1, 128), f32),
        "cross_out": pltpu.VMEM((2, 2) + tile, bf16),
        "cross_in": pltpu.VMEM((2, 2) + tile, bf16),
        "sib_out": pltpu.VMEM((2, 4, 2, 2) + tile, bf16),
        "sib_in": pltpu.VMEM((2, 4, 2, 2) + tile, bf16),
        "lists_v": pltpu.VMEM((16, 256), jnp.int32),
        "finals": pltpu.VMEM((4, 2 * BLOCK, BLOCK), bf16),
        "local_sem": dma((10,)),
        "kv_send": dma((14,)),
        "kv_recv": dma((14,)),
        "qg_send": dma((14,)),
        "qg_recv": dma((14,)),
        "sib_send": dma((18,)),
        "sib_recv": dma((18,)),
        "st_send": dma((7,)),
        "st_recv": dma((7,)),
    }
    for ring in ("key", "query"):
        scratch |= {
            ring + "_out": pltpu.VMEM((2, 4, 2, 2) + tile, bf16),
            ring + "_own_in": pltpu.VMEM((2, 4, 2) + tile, bf16),
            ring + "_part_in": pltpu.VMEM((2, 2, 2) + tile, bf16),
            ring + "_part_out": pltpu.VMEM((2, 2, 2) + tile, bf16),
            ring + "_sum_out": pltpu.VMEM((2, 2) + tile, bf16),
            ring + "_sum_in": pltpu.VMEM((2, 2) + tile, bf16),
            ring + "_send": dma((22,)),
            ring + "_recv": dma((22,)),
        }
    if not dense:
        scratch |= {
            "slot_query": pltpu.VMEM((SLOTS, 1), f32),
            "probs": pltpu.VMEM((SLOTS,) + tile, f32),
            "prob_grads": pltpu.VMEM((SLOTS,) + tile, f32),
            "tops": pltpu.VMEM((SLOTS, 128), f32),
            "totals": pltpu.VMEM((SLOTS, 128), f32),
            "moments": pltpu.VMEM((SLOTS, 128), f32),
            "columns": pltpu.VMEM((BLOCK, 32), f32),
        }
    outs = ["attended", "query_grads", "key_grads", "value_grads"] + ["flag"] * (not dense)
    out_shape, out_specs = [out] * 4, [any_spec] * 4
    if not dense:
        out_shape.append(jax.ShapeDtypeStruct((1, 1), f32))
        out_specs.append(smem_spec)
    return pl.pallas_call(
        functools.partial(kernel, ["q", "k", "v", "g", "lists"] + outs + list(scratch), dense),
        out_shape=out_shape,
        in_specs=[any_spec] * 5,
        out_specs=out_specs,
        scratch_shapes=list(scratch.values()),
        compiler_params=pltpu.CompilerParams(
            collective_id=1 if dense else 0, has_side_effects=True, vmem_limit_bytes=56 << 20
        ),
        name="dense_attention" if dense else "block_sparse_attention",
    )(*(a.reshape(2, BLOCK, BLOCK) for a in (queries, keys, values, grad_out)), lists)


def hand_out_kernel(*refs):
    sems = refs[-1]
    copies = [pltpu.make_async_copy(refs[n], refs[4 + n], sems.at[n]) for n in range(4)]
    for copy in copies:
        copy.start()
    for copy in copies:
        copy.wait()


def hand_out(outs):
    spec = pl.BlockSpec(memory_space=pl.ANY)
    return tuple(
        pl.pallas_call(
            hand_out_kernel,
            out_shape=[jax.ShapeDtypeStruct(out.shape, out.dtype) for out in outs],
            in_specs=[spec] * 4,
            out_specs=[spec] * 4,
            scratch_shapes=[pltpu.SemaphoreType.DMA((4,))],
            name="hand_out",
        )(*outs)
    )


def per_device(queries, keys, values, grad_out, key_blocks):
    args = (queries, keys, values, grad_out, key_blocks.T)
    *outs, most = attention(False, *args)
    return lax.cond(
        most[0, 0] > SLOTS,
        lambda: hand_out(attention(True, *args)),
        lambda: hand_out(outs),
    )


def solution(mesh):
    split = P(("qblk", "kblk"), None)
    return jax.shard_map(
        per_device,
        mesh=mesh,
        in_specs=(split, split, split, split, P()),
        out_specs=(split, split, split, split),
        check_vma=False,
    )
```

```python
import functools
import math

import jax
import jax.numpy as jnp
from jax import lax
from jax.experimental import pallas as pl
from jax.experimental.pallas import tpu as pltpu
from jax.sharding import PartitionSpec as P

BLOCK = 128
SLOTS = 56
UNROLL = 56
MESH = pl.DeviceIdType.MESH

masked_score = -1e30
LOG2E = 1.4426950408889634


def against(left, right):
    return lax.dot_general(
        left, right, (((1,), (1,)), ((), ())), preferred_element_type=jnp.float32
    )


def across(left, right):
    return lax.dot_general(
        left, right, (((0,), (0,)), ((), ())), preferred_element_type=jnp.float32
    )


def dot(left, right):
    return jnp.dot(left, right, preferred_element_type=jnp.float32)


KEY, QUERY, SAME_KEY, DIAGONAL, PERM, PERM_KEY, PERM_QUERY, SAME_QUERY, KEY_END, QUERY_END = range(10)
LISTED = 16

STAT_STEPS = ((False, 1), (False, -1), (True, 0), (False, 2), (True, 1), (True, -1), (True, 2))


def iota(shape, dim):
    return lax.broadcasted_iota(jnp.int32, shape, dim)


def fiota(shape, dim):
    return iota(shape, dim).astype(jnp.float32)


def ones_where(cond):
    return jnp.where(cond, 1.0, 0.0).astype(jnp.float32)


def query_id(i, j, q):
    x = (i // 8 + j % 2 + (q // 2) % 2) % 2
    return (x * 8 + i % 8) * 16 + q


def list_pairs(i, j, lists_ref, table, slot_query):
    lists = lists_ref[...].astype(jnp.float32)
    chosen = ones_where(iota((256, 16), 0) == query_id(i, j, iota((256, 16), 1)))
    own = dot(lists, chosen)
    key_ids = ((iota((32, 16), 0) // 2) * 16 + 2 * j + iota((32, 16), 0) % 2).astype(jnp.float32)
    pairs = jnp.zeros((32, 16), jnp.float32)
    for n in range(16):
        pairs = jnp.maximum(pairs, ones_where(own[n : n + 1, :] == key_ids))
    earlier_query = ones_where(iota((16, 16), 0) < iota((16, 16), 1))
    earlier_key = ones_where(iota((32, 32), 1) < iota((32, 32), 0))
    in_key = dot(pairs, earlier_query)
    in_query = dot(earlier_key, pairs)
    key_count = jnp.sum(pairs, axis=1, keepdims=True)
    query_count = jnp.sum(pairs, axis=0, keepdims=True)
    key_first = jnp.sum(in_query, axis=1, keepdims=True)
    query_first = jnp.sum(in_key, axis=0, keepdims=True)
    by_key = jnp.where(pairs > 0, key_first + in_key, -1.0)
    by_query = jnp.where(pairs > 0, query_first + in_query, -1.0)
    total = jnp.sum(jnp.sum(pairs, axis=1, keepdims=True), axis=0, keepdims=True)

    lane = fiota((32, 128), 1)
    keys = fiota((32, 128), 0)
    id_col = (iota((32, 128), 0) // 2) * 16 + 2 * j + iota((32, 128), 0) % 2
    zero = jnp.zeros((32, 128), jnp.float32)
    rows = {n: zero for n in range(8)}
    for q in range(16):
        at_key = by_key[:, q : q + 1] == lane
        at_query = by_query[:, q : q + 1] == lane
        rows[KEY] += jnp.where(at_key, keys, 0.0)
        rows[QUERY] += jnp.where(at_key, float(q), 0.0)
        rows[SAME_KEY] += jnp.where(at_key, ones_where(in_key[:, q : q + 1] > 0), 0.0)
        rows[DIAGONAL] += jnp.where(at_key & (id_col == query_id(i, j, q)), 1.0, 0.0)
        rows[PERM] += jnp.where(at_query, by_key[:, q : q + 1], 0.0)
        rows[PERM_KEY] += jnp.where(at_query, keys, 0.0)
        rows[PERM_QUERY] += jnp.where(at_query, float(q), 0.0)
        rows[SAME_QUERY] += jnp.where(at_query, ones_where(in_query[:, q : q + 1] > 0), 0.0)
    most = {KEY: 31, QUERY: 15, SAME_KEY: 1, DIAGONAL: 1}
    most |= {PERM: SLOTS - 1, PERM_KEY: 31, PERM_QUERY: 15, SAME_QUERY: 1}
    for n in range(8):
        rows[n] = jnp.sum(rows[n], axis=0, keepdims=True)
        table[n : n + 1, :] = jnp.clip(rows[n].astype(jnp.int32), 0, most[n])
    key_end = jnp.where(key_count > 0, key_first + key_count, 0.0)
    key_end = jnp.sum(jnp.where(keys == lane, key_end, 0.0), axis=0, keepdims=True)
    table[KEY_END : KEY_END + 1, :] = jnp.clip(key_end.astype(jnp.int32), 0, SLOTS)
    query_end = jnp.where(query_count > 0, query_first + query_count, 0.0)
    table[QUERY_END : QUERY_END + 1, 0:16] = jnp.clip(query_end.astype(jnp.int32), 0, SLOTS)
    if table.shape[0] > LISTED:
        table[LISTED : LISTED + 32, 0:16] = pairs.astype(jnp.int32)
        return

    query_row = jnp.where(fiota((1, 128), 1) < total, rows[QUERY], -1.0)
    slot_query[...] = jnp.sum(
        jnp.where(iota((SLOTS, 128), 0) == iota((SLOTS, 128), 1), query_row, 0.0),
        axis=1,
        keepdims=True,
    )


def most_pairs(lists_ref):
    lists = lists_ref[...]
    groups = (lists // 2) % 8
    counts = jnp.zeros((8, 256), jnp.float32)
    group_of = iota((8, 256), 0)
    for n in range(16):
        fresh = jnp.ones((1, 256), jnp.float32)
        for m in range(n):
            fresh = jnp.where(lists[m : m + 1] == lists[n : n + 1], 0.0, fresh)
        counts += jnp.where(groups[n : n + 1] == group_of, fresh, 0.0)
    block = iota((256, 16), 0)
    query_group = (block // 16 % 8) * 2 + (block // 128 + block // 2 % 2) % 2
    member = ones_where(query_group == iota((256, 16), 1))
    return jnp.max(dot(counts, member))


def flip(bit):
    return 1 - bit


class Ring:
    def __init__(self, a, p, peer, row, blocks, gather_sems, out, own_in, part_in, part_out, sum_out, sum_in, sum_sems):
        self.a, self.p, self.peer, self.row = a, p, peer, row
        self.blocks, self.gather_sems = blocks, gather_sems
        self.out, self.own_in, self.part_in, self.part_out = out, own_in, part_in, part_out
        self.sum_out, self.sum_in, self.sum_sems = sum_out, sum_in, sum_sems
        self.copies, self.waited = [], 0

    def at(self, step):
        return (self.p + step + 4) % 4

    def send(self, src, dst, sems, n, peer):
        copy = pltpu.make_async_remote_copy(
            src_ref=src, dst_ref=dst, send_sem=sems[0].at[n], recv_sem=sems[1].at[n],
            device_id=peer, device_id_type=MESH,
        )
        copy.start()
        self.copies.append(copy)
        return copy

    def pass_half(self, n, row, half, peer):
        ref = self.blocks.at[row, half]
        return self.send(ref, ref, self.gather_sems, n, peer)

    def start_own(self):
        own, up, down = self.row(self.a, self.p), self.peer(False, 1), self.peer(False, -1)
        self.gather = {2: self.pass_half(2, own, 0, up)}
        self.gather[4] = self.pass_half(4, own, 1, down)
        self.gather[8] = self.pass_half(8, own, 0, self.peer(True, 1))
        self.gather[10] = self.pass_half(10, own, 1, self.peer(True, -1))
        self.gather[0] = self.pass_half(0, own, 0, self.peer(True, 0))
        self.gather[1] = self.pass_half(1, own, 1, self.peer(True, 0))
        self.gather[3] = self.pass_half(3, own, 1, up)
        self.gather[5] = self.pass_half(5, own, 0, down)

    def gather_step(self, n):
        self.gather[n].wait_recv()
        up, down = self.peer(False, 1), self.peer(False, -1)
        if n < 2:
            row = self.row(flip(self.a), self.p)
            if n == 0:
                self.gather[11] = self.pass_half(11, row, 0, down)
            else:
                self.gather[9] = self.pass_half(9, row, 1, up)
            return row, n
        a = self.a if n < 8 else flip(self.a)
        m = (n - 2) % 6
        row = self.row(a, self.at((-1, -1, 1, 1, 2, 2)[m]))
        half = (0, 1, 1, 0, 0, 1)[m]
        if m == 0:
            self.gather[n + 4] = self.pass_half(n + 4, row, half, up)
        if m == 2:
            self.gather[n + 3] = self.pass_half(n + 3, row, half, down)
        return row, half

    def pieces(self, phase):
        return [(half, b) for b in ((0, 1) if phase == 0 else (None,)) for half in (0, 1)]

    def start_part(self, phase, cross=None):
        a = flip(self.a) if phase == 0 else self.a
        parts = {}
        for half, b in self.pieces(phase):
            n = 12 + half if b is None else 2 * half + b
            step = 1 if half == 0 else -1
            src, dst = self.out.at[a, self.at(2), half], self.part_in.at[phase, half]
            if b is not None:
                src, dst = src.at[b], dst.at[b]
            parts[half, b] = [self.send(src, dst, self.sum_sems, n, self.peer(False, step))]
            if cross is not None:
                cross_out, cross_in, cross_peer = cross
                parts[half, b].append(
                    self.send(
                        cross_out.at[half, b], cross_in.at[half, b], self.sum_sems, 18 + n, cross_peer(step)
                    )
                )
        return [a, phase, parts, [], {}, cross]

    def start_plain(self, state):
        a, phase, _, plain, _, _ = state
        out, sems, n = self.out, self.sum_sems, 4 + 10 * phase
        plain += [
            self.send(out.at[a, self.at(1), 1], self.own_in.at[phase, 1], sems, n, self.peer(False, 1)),
            self.send(out.at[a, self.at(-1), 0], self.own_in.at[phase, 0], sems, n + 1, self.peer(False, -1)),
        ]

    def add_part(self, state):
        a, phase, parts, _, sums, cross = state
        for half, b in self.pieces(phase):
            n = 16 + half if b is None else 6 + 2 * half + b
            step = 1 if half == 0 else -1
            for copy in parts[half, b]:
                copy.wait_recv()
            at = slice(None) if b is None else b
            both = self.out[a, self.at(step), half, at].astype(jnp.float32)
            both += self.part_in[phase, half, at].astype(jnp.float32)
            if cross is not None:
                both += cross[1][half, at].astype(jnp.float32)
            self.part_out[phase, half, at] = both.astype(jnp.bfloat16)
            src, dst = self.part_out.at[phase, half], self.own_in.at[phase, 2 + half]
            if b is not None:
                src, dst = src.at[b], dst.at[b]
            sums[half, b] = self.send(src, dst, self.sum_sems, n, self.peer(False, step))

    def total(self, state, b):
        a, phase, _, plain, sums, _ = state
        while plain:
            plain.pop().wait_recv()
        for piece in [piece for piece in sums if piece[1] in (b, None)]:
            sums.pop(piece).wait_recv()
        total = self.out[a, self.p, :, b].astype(jnp.float32)
        total += self.own_in[phase, 0:2, b].astype(jnp.float32)
        return total + self.own_in[phase, 2:4, b].astype(jnp.float32)

    def send_total(self, state, b):
        self.sum_out[b] = self.total(state, b).astype(jnp.bfloat16)
        copy = self.send(self.sum_out.at[b], self.sum_in.at[b], self.sum_sems, 10 + b, self.peer(True, 0))
        self.to_total = getattr(self, "to_total", {}) | {b: copy}

    def whole_total(self, state, b):
        total = self.total(state, b)
        self.to_total[b].wait_recv()
        return total + self.sum_in[b].astype(jnp.float32)


class Refs:
    def __init__(self, names, refs):
        self.__dict__.update(zip(names, refs, strict=True))


def kernel(names, dense, *refs):
    r = Refs(names, refs)
    i, j = lax.axis_index("qblk"), lax.axis_index("kblk")
    core, y, x = i % 2, (i // 2) % 4, i // 8
    h, z = j % 2, j // 2
    scale = 1.0 / math.sqrt(BLOCK)
    kv, qg, table = r.kv, r.qg, r.table

    def key_row(x, y):
        return x * 8 + y * 2 + core

    def query_row(h, z):
        return z * 2 + h

    def key_peer(pair, step):
        return (key_row(flip(x) if pair else x, (y + step + 4) % 4), j)

    def query_peer(pair, step):
        at = (z + step + 4) % 4
        return ((i + 8) % 16, query_row(flip(h), at)) if pair else (i, query_row(h, at))

    sibling = (i + 1 - 2 * core, j)

    loads = []
    for n, (src, dst) in enumerate(
        ((r.k, kv.at[i, 0]), (r.q, qg.at[j, 0]), (r.v, kv.at[i, 1]), (r.g, qg.at[j, 1]), (r.lists, r.lists_v))
    ):
        loads.append(pltpu.make_async_copy(src, dst, r.local_sem.at[n]))
        loads[-1].start()

    stat_peers = [query_peer(pair, step) for pair, step in STAT_STEPS]
    peers = [sibling, key_peer(True, 0), key_peer(False, 1), key_peer(False, -1), key_peer(True, 1), key_peer(True, -1)] + stat_peers[:3] + stat_peers[4:6]
    barrier = pltpu.get_barrier_semaphore()
    for peer in peers:
        pl.semaphore_signal(barrier, inc=1, device_id=peer, device_id_type=MESH)
    pl.semaphore_wait(barrier, len(peers))
    for load in loads[:4]:
        load.wait()

    keys = Ring(
        x, y, key_peer, key_row, kv, (r.kv_send, r.kv_recv), r.key_out, r.key_own_in, r.key_part_in,
        r.key_part_out, r.key_sum_out, r.key_sum_in, (r.key_send, r.key_recv),
    )
    queries = Ring(
        h, z, query_peer, query_row, qg, (r.qg_send, r.qg_recv), r.query_out, r.query_own_in, r.query_part_in,
        r.query_part_out, r.query_sum_out, r.query_sum_in, (r.query_send, r.query_recv),
    )
    sib = []

    def to_sibling(row, half):
        ref = kv.at[row, half]
        sib.append(keys.send(ref, ref, (r.sib_send, r.sib_recv), len(sib), sibling))

    def gather_steps(*steps):
        for n in steps:
            to_sibling(*keys.gather_step(n))
            queries.gather_step(n)

    keys.start_own()
    queries.start_own()
    to_sibling(i, 0)
    to_sibling(i, 1)

    loads[4].wait()
    list_pairs(i, j, r.lists_v, r.table_v, None if dense else r.slot_query)
    to_smem = pltpu.make_async_copy(r.table_v, table, r.local_sem.at[5])
    to_smem.start()
    gather_steps(2, 4, 0, 1, 8, 10)

    r.bias[0] = jnp.zeros((BLOCK, BLOCK), jnp.float32)
    r.bias[1] = jnp.where(
        iota((BLOCK, BLOCK), 0) <= iota((BLOCK, BLOCK), 1), 0.0, masked_score
    ).astype(jnp.float32)
    none = 0 if not dense else slice(None)
    r.key_acc[none] = jnp.zeros(r.key_acc[none].shape, jnp.float32)
    r.query_acc[none] = jnp.zeros(r.query_acc[none].shape, jnp.float32)

    gather_steps(3, 5, 6, 7, 9, 11, 12, 13)
    for copy in sib:
        copy.wait_recv()
    to_smem.wait()

    (dense_stats if dense else slot_stats)(r, i, j, scale)

    st_sems = (r.st_send, r.st_recv)
    st_copies = []
    r.stats[j] = r.stats_out[...]
    for n, peer in enumerate(stat_peers):
        st_copies.append(queries.send(r.stats_out, r.stats.at[j], st_sems, n, peer))
    for ring in (keys, queries):
        for copy in ring.copies[: -len(st_copies) if ring is queries else None]:
            copy.wait_send()
            ring.waited += 1
    if not dense:
        r.flag[0, 0] = most_pairs(r.lists_v)
        slot_query_grads(r)
    for copy in st_copies:
        copy.wait_recv()
    logs = r.stats[:, 0]
    best = jnp.max(logs, axis=0)
    offset = best + jnp.log2(jnp.sum(jnp.exp2(logs - best[None]), axis=0))
    delta = jnp.sum(jnp.exp2(logs - offset[None]) * r.stats[:, 1], axis=0)
    for q in range(16):
        r.offsets[q] = offset[q : q + 1, :]
        r.deltas[q] = delta[q : q + 1, :]
    if not dense:
        scales = jnp.exp2(r.stats_out[0] - offset)
        r.columns[...] = jnp.transpose(jnp.concatenate([scales, delta - r.stats_out[1]], axis=0))

    if dense:
        dense_key_grads(r, i, j, scale)
    def query_part(q):
        if dense:
            return r.query_acc[q]
        sums = r.query_acc[table[QUERY_END, q]]
        own = r.columns[:, q : q + 1]
        shift = r.columns[:, 16 + q : 17 + q]
        return jnp.stack([own * (sums[0] - shift * sums[1]), own * sums[2]])

    def query_out(phase):
        for n in range(4):
            for b in range(2):
                for at in range(2):

                    @pl.when(at == (flip(h) if phase == 0 else h))
                    def _(n=n, b=b, at=at):
                        r.query_out[at, n, :, b] = query_part((n * 2 + at) * 2 + b).astype(jnp.bfloat16)

    query_out(0)
    query_sums = [queries.start_part(0)]
    queries.start_plain(query_sums[0])
    if not dense:
        slot_key_grads(r, i, j, scale)

    def key_part(block):
        return r.key_acc[block if dense else table[KEY_END, block]]

    def key_owner(at, step, parity):
        return at * 8 + keys.at(step) * 2 + parity

    for b in range(2):
        same = key_part(key_owner(flip(x), 2, core) * 2 + b).astype(jnp.bfloat16)
        other = key_part(key_owner(flip(x), 2, 1 - core) * 2 + b).astype(jnp.bfloat16)
        for half in range(2):
            r.key_out[flip(x), keys.at(2), half, b] = same[half]
            r.cross_out[half, b] = other[half]

    def cross_peer(step):
        return (x * 8 + keys.at(step) * 2 + 1 - core, j)

    key_sums = [keys.start_part(0, (r.cross_out, r.cross_in, cross_peer))]

    swaps = []
    ring_steps = ((0, 1, -1), (0, 1, -1, 2))
    for phase, at in ((0, flip(x)), (1, x)):
        for n, step in enumerate(ring_steps[phase]):
            for b in range(2):
                block = key_owner(at, step, 1 - core) * 2 + b
                r.sib_out[phase, n, :, b] = key_part(block).astype(jnp.bfloat16)
        some = pl.ds(0, len(ring_steps[phase]))
        swaps.append(
            keys.send(
                r.sib_out.at[phase, some], r.sib_in.at[phase, some], (r.sib_send, r.sib_recv), 16 + phase, sibling
            )
        )

    def key_out(phase, at):
        swaps[phase].wait_recv()
        for n, step in enumerate(ring_steps[phase]):
            for b in range(2):
                both = key_part(key_owner(at, step, core) * 2 + b) + r.sib_in[phase, n, :, b].astype(jnp.float32)
                r.key_out[at, keys.at(step), :, b] = both.astype(jnp.bfloat16)

    query_out(1)
    query_sums.append(queries.start_part(1))
    queries.add_part(query_sums[0])
    queries.start_plain(query_sums[1])
    key_out(0, flip(x))
    keys.start_plain(key_sums[0])
    keys.add_part(key_sums[0])
    key_out(1, x)
    key_sums.append(keys.start_part(1))
    keys.start_plain(key_sums[1])
    for b in range(2):
        queries.send_total(query_sums[0], b)
    queries.add_part(query_sums[1])
    for b in range(2):
        keys.send_total(key_sums[0], b)
    keys.add_part(key_sums[1])
    results = []

    def finish(n, ring, state, factors, outs):
        for b in range(2):
            rows = pl.ds(b * BLOCK, BLOCK)
            sums = ring.whole_total(state, b)
            for m in range(2):
                r.finals[n + m, rows, :] = (sums[m] * factors[m]).astype(jnp.bfloat16)
        for m in range(2):
            results.append(pltpu.make_async_copy(r.finals.at[n + m], outs[m], r.local_sem.at[6 + n + m]))
            results[-1].start()

    finish(0, queries, query_sums[1], (scale, 1.0), (r.query_grads, r.attended))
    finish(2, keys, key_sums[1], (scale, 1.0), (r.key_grads, r.value_grads))
    for ring in (keys, queries):
        for copy in ring.copies[ring.waited :]:
            copy.wait_send()
    for result in results:
        result.wait()


def slot_stats(r, i, j, scale):
    kv, qg, table = r.kv, r.qg, r.table

    def step(n, carry):
        for u in range(UNROLL):
            s = n * UNROLL + u
            k, q = table[KEY, s], table[QUERY, s]
            scores = against(kv[k // 2, 0, k % 2], qg[q // 2, 0, q % 2]) * (scale * LOG2E)
            scores += r.bias[table[DIAGONAL, s]]
            prob_grad = against(kv[k // 2, 1, k % 2], qg[q // 2, 1, q % 2])
            top = jnp.max(scores, axis=0, keepdims=True)
            prob = jnp.exp2(scores - top)
            r.probs[s] = prob
            r.prob_grads[s] = prob_grad
            r.tops[pl.ds(s, 1), :] = top
            r.totals[pl.ds(s, 1), :] = jnp.sum(prob, axis=0, keepdims=True)
            r.moments[pl.ds(s, 1), :] = jnp.sum(prob * prob_grad, axis=0, keepdims=True)
        return carry

    lax.fori_loop(0, SLOTS // UNROLL, step, 0)

    top, total, moment, owner = r.tops[...], r.totals[...], r.moments[...], r.slot_query[...]
    for q in range(16):
        mine = owner == float(q)
        top_q = jnp.max(jnp.where(mine, top, masked_score), axis=0, keepdims=True)
        part = jnp.where(mine, jnp.exp2(top - top_q), 0.0)
        total_q = jnp.sum(part * total, axis=0, keepdims=True)
        moment_q = jnp.sum(part * moment, axis=0, keepdims=True)
        put_stats(r, q, top_q, total_q, moment_q)


def put_stats(r, q, top, total, moment):
    some = total > 0
    safe = jnp.where(some, total, 1.0)
    log, mean = jnp.where(some, top + jnp.log2(safe), masked_score), moment / safe
    r.stats_out[0, pl.ds(q, 1), :] = log
    r.stats_out[1, pl.ds(q, 1), :] = mean
    r.own_logs[q] = log
    r.own_means[q] = mean


def slot_key_grads(r, i, j, scale):
    def step(n, carry):
        for u in range(UNROLL):
            s = n * UNROLL + u
            q = r.table[QUERY, s]
            keep = r.table[SAME_KEY, s].astype(jnp.float32)
            prob = r.probs[s] * jnp.exp2(r.tops[pl.ds(s, 1), :] - r.offsets[q])
            weights = prob.astype(jnp.bfloat16)
            score_grad = (prob * (r.prob_grads[s] - r.deltas[q])).astype(jnp.bfloat16)
            r.key_acc[s + 1, 0] = r.key_acc[s, 0] * keep + dot(score_grad, r.qg[q // 2, 0, q % 2])
            r.key_acc[s + 1, 1] = r.key_acc[s, 1] * keep + dot(weights, r.qg[q // 2, 1, q % 2])
        return carry

    lax.fori_loop(0, SLOTS // UNROLL, step, 0)


def slot_query_grads(r):
    def step(n, carry):
        for u in range(UNROLL):
            s = n * UNROLL + u
            k, q, at = r.table[PERM_KEY, s], r.table[PERM_QUERY, s], r.table[PERM, s]
            keep = r.table[SAME_QUERY, s].astype(jnp.float32)
            prob = r.probs[at] * jnp.exp2(r.tops[pl.ds(at, 1), :] - r.own_logs[q])
            weights = prob.astype(jnp.bfloat16)
            score_grad = (prob * (r.prob_grads[at] - r.own_means[q])).astype(jnp.bfloat16)
            keys, values = r.kv[k // 2, 0, k % 2], r.kv[k // 2, 1, k % 2]
            r.query_acc[s + 1, 0] = r.query_acc[s, 0] * keep + across(score_grad, keys)
            r.query_acc[s + 1, 1] = r.query_acc[s, 1] * keep + across(weights, keys)
            r.query_acc[s + 1, 2] = r.query_acc[s, 2] * keep + across(weights, values)
        return carry

    lax.fori_loop(0, SLOTS // UNROLL, step, 0)


def dense_tile(r, i, j, scale, q, k):
    scores = against(r.kv[k // 2, 0, k % 2], r.qg[q // 2, 0, q % 2]) * (scale * LOG2E)
    own = (k // 2) * 16 + 2 * j + k % 2 == query_id(i, j, q)
    scores += r.bias[own.astype(jnp.int32)]
    prob_grad = against(r.kv[k // 2, 1, k % 2], r.qg[q // 2, 1, q % 2])
    listed = r.table[LISTED + k, q].astype(jnp.float32)
    return scores + (1.0 - listed) * masked_score, prob_grad, listed


def dense_stats(r, i, j, scale):
    def query_step(q, carry):
        def key_step(k, state):
            top, total, moment = state
            scores, prob_grad, listed = dense_tile(r, i, j, scale, q, k)
            higher = jnp.maximum(top, jnp.max(scores, axis=0, keepdims=True))
            prob = jnp.exp2(scores - higher) * listed
            shrink = jnp.exp2(top - higher)
            total = total * shrink + jnp.sum(prob, axis=0, keepdims=True)
            moment = moment * shrink + jnp.sum(prob * prob_grad, axis=0, keepdims=True)
            return higher, total, moment

        zero = jnp.zeros((1, BLOCK), jnp.float32)
        put_stats(r, q, *lax.fori_loop(0, 32, key_step, (zero + masked_score, zero, zero)))
        return carry

    lax.fori_loop(0, 16, query_step, 0)


def dense_key_grads(r, i, j, scale):
    def step(n, carry):
        q, k = n // 32, n % 32
        scores, prob_grad, listed = dense_tile(r, i, j, scale, q, k)
        prob = jnp.exp2(scores - r.offsets[q]) * listed
        weights = prob.astype(jnp.bfloat16)
        score_grad = (prob * (prob_grad - r.deltas[q])).astype(jnp.bfloat16)
        for m, left in enumerate((score_grad, weights)):
            r.key_acc[k, m] = r.key_acc[k, m] + dot(left, r.qg[q // 2, m, q % 2])
            r.query_acc[q, m] = r.query_acc[q, m] + across(left, r.kv[k // 2, m, k % 2])
        return carry

    lax.fori_loop(0, 16 * 32, step, 0)


def attention(dense, queries, keys, values, grad_out, lists):
    rows, head = queries.shape
    out = jax.ShapeDtypeStruct((rows, head), jnp.bfloat16)
    f32, bf16 = jnp.float32, jnp.bfloat16
    tile = (BLOCK, BLOCK)
    table_rows = LISTED + 32 if dense else LISTED
    dma = pltpu.SemaphoreType.DMA
    any_spec = pl.BlockSpec(memory_space=pl.ANY)
    smem_spec = pl.BlockSpec(memory_space=pltpu.SMEM)
    scratch = {
        "kv": pltpu.VMEM((16, 2, 2) + tile, bf16),
        "qg": pltpu.VMEM((8, 2, 2) + tile, bf16),
        "table_v": pltpu.VMEM((table_rows, 128), jnp.int32),
        "table": pltpu.SMEM((table_rows, 128), jnp.int32),
        "bias": pltpu.VMEM((2,) + tile, f32),
        "stats_out": pltpu.VMEM((2, 16, 128), f32),
        "stats": pltpu.VMEM((8, 2, 16, 128), f32),
        "offsets": pltpu.VMEM((16, 1, 128), f32),
        "deltas": pltpu.VMEM((16, 1, 128), f32),
        "key_acc": pltpu.VMEM((32 if dense else SLOTS + 1, 2) + tile, f32),
        "query_acc": pltpu.VMEM(((16, 2) if dense else (SLOTS + 1, 3)) + tile, f32),
        "own_logs": pltpu.VMEM((16, 1, 128), f32),
        "own_means": pltpu.VMEM((16, 1, 128), f32),
        "cross_out": pltpu.VMEM((2, 2) + tile, bf16),
        "cross_in": pltpu.VMEM((2, 2) + tile, bf16),
        "sib_out": pltpu.VMEM((2, 4, 2, 2) + tile, bf16),
        "sib_in": pltpu.VMEM((2, 4, 2, 2) + tile, bf16),
        "lists_v": pltpu.VMEM((16, 256), jnp.int32),
        "finals": pltpu.VMEM((4, 2 * BLOCK, BLOCK), bf16),
        "local_sem": dma((10,)),
        "kv_send": dma((14,)),
        "kv_recv": dma((14,)),
        "qg_send": dma((14,)),
        "qg_recv": dma((14,)),
        "sib_send": dma((18,)),
        "sib_recv": dma((18,)),
        "st_send": dma((7,)),
        "st_recv": dma((7,)),
    }
    for ring in ("key", "query"):
        scratch |= {
            ring + "_out": pltpu.VMEM((2, 4, 2, 2) + tile, bf16),
            ring + "_own_in": pltpu.VMEM((2, 4, 2) + tile, bf16),
            ring + "_part_in": pltpu.VMEM((2, 2, 2) + tile, bf16),
            ring + "_part_out": pltpu.VMEM((2, 2, 2) + tile, bf16),
            ring + "_sum_out": pltpu.VMEM((2, 2) + tile, bf16),
            ring + "_sum_in": pltpu.VMEM((2, 2) + tile, bf16),
            ring + "_send": dma((22,)),
            ring + "_recv": dma((22,)),
        }
    if not dense:
        scratch |= {
            "slot_query": pltpu.VMEM((SLOTS, 1), f32),
            "probs": pltpu.VMEM((SLOTS,) + tile, f32),
            "prob_grads": pltpu.VMEM((SLOTS,) + tile, f32),
            "tops": pltpu.VMEM((SLOTS, 128), f32),
            "totals": pltpu.VMEM((SLOTS, 128), f32),
            "moments": pltpu.VMEM((SLOTS, 128), f32),
            "columns": pltpu.VMEM((BLOCK, 32), f32),
        }
    outs = ["attended", "query_grads", "key_grads", "value_grads"] + ["flag"] * (not dense)
    out_shape, out_specs = [out] * 4, [any_spec] * 4
    if not dense:
        out_shape.append(jax.ShapeDtypeStruct((1, 1), f32))
        out_specs.append(smem_spec)
    return pl.pallas_call(
        functools.partial(kernel, ["q", "k", "v", "g", "lists"] + outs + list(scratch), dense),
        out_shape=out_shape,
        in_specs=[any_spec] * 5,
        out_specs=out_specs,
        scratch_shapes=list(scratch.values()),
        compiler_params=pltpu.CompilerParams(
            collective_id=1 if dense else 0, has_side_effects=True, vmem_limit_bytes=56 << 20
        ),
        name="dense_attention" if dense else "block_sparse_attention",
    )(*(a.reshape(2, BLOCK, BLOCK) for a in (queries, keys, values, grad_out)), lists)


def hand_out_kernel(*refs):
    sems = refs[-1]
    copies = [pltpu.make_async_copy(refs[n], refs[4 + n], sems.at[n]) for n in range(4)]
    for copy in copies:
        copy.start()
    for copy in copies:
        copy.wait()


def hand_out(outs):
    spec = pl.BlockSpec(memory_space=pl.ANY)
    return tuple(
        pl.pallas_call(
            hand_out_kernel,
            out_shape=[jax.ShapeDtypeStruct(out.shape, out.dtype) for out in outs],
            in_specs=[spec] * 4,
            out_specs=[spec] * 4,
            scratch_shapes=[pltpu.SemaphoreType.DMA((4,))],
            name="hand_out",
        )(*outs)
    )


def per_device(queries, keys, values, grad_out, key_blocks):
    args = (queries, keys, values, grad_out, key_blocks.T)
    *outs, most = attention(False, *args)
    return lax.cond(
        most[0, 0] > SLOTS,
        lambda: hand_out(attention(True, *args)),
        lambda: hand_out(outs),
    )


def solution(mesh):
    split = P(("qblk", "kblk"), None)
    return jax.shard_map(
        per_device,
        mesh=mesh,
        in_specs=(split, split, split, split, P()),
        out_specs=(split, split, split, split),
        check_vma=False,
    )
```
